32 devices in a mesh: rep: 4 (over z), fsdp: 8 (over y, x, core).
Axes of the slice: x: 2, y: 2, z: 4, core: 2. Of those that a mesh axis runs over, the one named last changes fastest.
Arguments:
- tokens: bfloat16 [256, 256, 512], P(('rep', 'fsdp')), may hold values from -11 to 11
- cotangent: bfloat16 [256, 256, 512], P(('rep', 'fsdp')), may hold values from -6 to 6
- slot_items: int32 [256], P(('rep', 'fsdp')), may hold values from 0 to 4
- filter_gain: bfloat16 [512], P('fsdp'), may hold values from 0.5 to 1.5
- filter_shift: bfloat16 [512], P('fsdp'), may hold values from -4 to 4
- inner_weight: bfloat16 [512, 128], P('fsdp'), may hold values from -0.5 to 0.5
- inner_bias: bfloat16 [1024], P('fsdp'), may hold values from -4 to 4
- outer_weight: bfloat16 [512, 128], P('fsdp'), may hold values from -0.75 to 0.75
- outer_bias: bfloat16 [1024], P('fsdp'), may hold values from -4 to 4
- feed_gain: bfloat16 [512], P('fsdp'), may hold values from 0.5 to 1.5
- feed_shift: bfloat16 [512], P('fsdp'), may hold values from -4 to 4
- expand_weight: bfloat16 [512, 2048], P('fsdp'), may hold values from -0.25 to 0.25
- expand_bias: bfloat16 [2048], P('fsdp'), may hold values from -4 to 4
- contract_weight: bfloat16 [2048, 512], P('fsdp'), may hold values from -0.25 to 0.25
- contract_bias: bfloat16 [512], P('fsdp'), may hold values from -4 to 4
Outputs:
- block_output: bfloat16 [256, 256, 512], P(('rep', 'fsdp'))
- input_grad: float32 [256, 256, 512], P(('rep', 'fsdp'))
- filter_gain_grad: float32 [512], P('fsdp')
- filter_shift_grad: float32 [512], P('fsdp')
- inner_weight_grad: float32 [512, 128], P('fsdp')
- inner_bias_grad: float32 [1024], P('fsdp')
- outer_weight_grad: float32 [512, 128], P('fsdp')
- outer_bias_grad: float32 [1024], P('fsdp')
- feed_gain_grad: float32 [512], P('fsdp')
- feed_shift_grad: float32 [512], P('fsdp')
- expand_weight_grad: float32 [512, 2048], P('fsdp')
- expand_bias_grad: float32 [2048], P('fsdp')
- contract_weight_grad: float32 [2048, 512], P('fsdp')
- contract_bias_grad: float32 [512], P('fsdp')
- statistics: float32 [5], replicated
The draws below stay inside these ranges and needn't reach their ends.
Inputs may be any that keep to these rules, and one draw needn't show every extreme that they name: `slot_items`: 0: the slot holds one item of 16 x 16 patches; 1 to 4: it holds that many items of (8) x (8) patches in its first quadrants, and the rest is padding.
All inputs are finite; a program needn't handle non-finite values.
Results may differ from the reference program's by a relative error of at most 0.014.
The reference program's roundings to bfloat16 on the way count: a program that leaves them out, or rounds other values in their place, can miss the bound.
Values may be sent and summed in bfloat16 or wider, within the bound.
A program may use at most 192 MiB of HBM per device.

```python
import jax
import jax.numpy as jnp
from jax import lax

BS = 64
NB = 8
FF = 2048
D = 512
SIDE = 16
ALL_SLOTS = 256


def draw_tokens(key, part):
    key = jax.random.fold_in(key, 7)
    key_values = jax.random.fold_in(key, 0)
    shape_all = (ALL_SLOTS, SIDE * SIDE, D)
    position = jnp.arange(ALL_SLOTS, dtype=jnp.float32) / max(ALL_SLOTS - 1, 1)
    slot_scale = 0.5 * jnp.exp(jnp.log(3.0) * position)
    values = jnp.clip(jax.random.normal(key_values, shape_all, jnp.float32), -6.0, 6.0)
    return (values * slot_scale[:, None, None]).astype(jnp.bfloat16)


def with_ends(array, rng, smallest, top_value):
    shape = array.shape
    place = [jax.random.randint(jax.random.fold_in(rng, axis), (), 0, shape[axis]) for axis in range(len(shape))]
    array = array.at[tuple(place)].set(smallest)
    longest = shape.index(max(shape))
    place[longest] = (place[longest] + 1) % shape[longest]
    return array.at[tuple(place)].set(top_value)


def block_levels(stream_key, dims, shards, least, top_value):
    level = 1.0
    for axis_at, parts in shards:
        draws = jax.random.uniform(jax.random.fold_in(jax.random.fold_in(stream_key, 6), axis_at), (parts,), jnp.float32, least / len(shards), top_value / len(shards))
        level = level * jnp.repeat(jnp.exp(draws), dims[axis_at] // parts).reshape((-1,) + (1,) * (len(dims) - 1 - axis_at))
    return level


def scatter_about(key, extent, scale, limit, cuts=(), kind=jnp.bfloat16):
    loudness = block_levels(key, extent, cuts, -0.22, 0.18) if cuts else 1.0
    values = jax.random.normal(key, extent, jnp.float32) * scale * loudness
    return jnp.minimum(jnp.maximum(values, -limit), limit).astype(kind)


def setup_inputs(seed: int = 0) -> dict:
    key_of = jax.random.split(jax.random.key(seed), 16)
    tokens = draw_tokens(jax.random.fold_in(key_of[15], 71), 0)
    cotangent = scatter_about(key_of[1], (ALL_SLOTS, SIDE * SIDE, D), 1.0, 6.0, ((0, 32),))
    slot_items = with_ends(jax.random.randint(key_of[2], (ALL_SLOTS,), 0, 5), jax.random.fold_in(key_of[2], 1), 0, 4).astype(jnp.int32)
    filter_gain = jnp.clip(1.0 + 0.1 * jax.random.normal(key_of[3], (D,), jnp.float32), 0.5, 1.5).astype(jnp.bfloat16)
    filter_shift = scatter_about(key_of[4], (D,), 0.3, 4.0, ((0, 8),))
    inner_weight = scatter_about(key_of[5], (D, 2 * BS), (2 * BS) ** -0.5, 0.5, ((0, 8),))
    inner_bias = scatter_about(key_of[6], (2 * D,), 0.3, 4.0, ((0, 8),))
    outer_weight = scatter_about(key_of[7], (D, 2 * BS), BS ** -0.5, 0.75, ((0, 8),))
    outer_bias = scatter_about(key_of[8], (2 * D,), 0.3, 4.0, ((0, 8),))
    feed_gain = jnp.clip(1.0 + 0.1 * jax.random.normal(key_of[9], (D,), jnp.float32), 0.5, 1.5).astype(jnp.bfloat16)
    feed_shift = scatter_about(key_of[10], (D,), 0.3, 4.0, ((0, 8),))
    expand_weight = scatter_about(key_of[11], (D, FF), D ** -0.5, 0.25, ((0, 8),))
    expand_bias = scatter_about(key_of[12], (FF,), 0.3, 4.0, ((0, 8),))
    contract_weight = scatter_about(key_of[13], (FF, D), (FF // 4) ** -0.5, 0.25, ((0, 8),))
    contract_bias = scatter_about(key_of[14], (D,), 0.3, 4.0, ((0, 8),))
    return dict(tokens=tokens, cotangent=cotangent, slot_items=slot_items, filter_gain=filter_gain, filter_shift=filter_shift, inner_weight=inner_weight, inner_bias=inner_bias, outer_weight=outer_weight, outer_bias=outer_bias, feed_gain=feed_gain, feed_shift=feed_shift, expand_weight=expand_weight, expand_bias=expand_bias, contract_weight=contract_weight, contract_bias=contract_bias)


EPSILON = 1e-05
SHRINK = 0.25
HIGHEST = lax.Precision.HIGHEST

@jax.custom_vjp
def low(v):
    return lax.optimization_barrier(v.astype(jnp.bfloat16)).astype(jnp.float32)

@jax.custom_vjp
def low_back(v):
    return v

def low_keep(v):
    return (low(v), None)

def low_pass(kept, grad):
    return (grad,)

def back_keep(v):
    return (v, None)

def back_low(kept, grad):
    return (low(grad),)
low.defvjp(low_keep, low_pass)
low_back.defvjp(back_keep, back_low)

def norm_rows(values, scale_gain, offset_shift):
    centre = values - lax.optimization_barrier(jnp.mean(values, axis=-1, keepdims=True))
    spread = lax.optimization_barrier(jnp.mean(centre * centre, axis=-1, keepdims=True))
    return centre * lax.rsqrt(spread + EPSILON) * scale_gain + offset_shift

def valid_rows(slot_kinds):
    position = jnp.arange(SIDE * SIDE)
    half_side = SIDE // 2
    quadrant = position // SIDE // half_side * 2 + position % SIDE // half_side
    chosen = (slot_kinds[:, None] == 0) | (quadrant[None, :] < slot_kinds[:, None])
    return jnp.where(chosen, 1.0, 0.0).astype(jnp.float32)

def spectrum_ref(grid_field, slot_kinds):
    slot_total = grid_field.shape[0]
    half_side = SIDE // 2
    whole_grid = jnp.fft.fft2(grid_field, axes=(1, 2), norm='ortho')
    pieces = grid_field.reshape(slot_total, 2, half_side, 2, half_side, D)
    quarter_grid = jnp.fft.fft2(pieces, axes=(2, 4), norm='ortho').reshape(slot_total, SIDE, SIDE, D)
    chosen = jnp.where((slot_kinds == 0)[:, None, None, None], whole_grid, quarter_grid)
    return (jnp.real(chosen), jnp.imag(chosen))

def inverse_ref(real_part, imag_part, slot_kinds):
    slot_total = real_part.shape[0]
    half_side = SIDE // 2
    joined = lax.complex(real_part, imag_part)
    whole_grid = jnp.fft.ifft2(joined, axes=(1, 2), norm='ortho')
    pieces = joined.reshape(slot_total, 2, half_side, 2, half_side, D)
    quarter_grid = jnp.fft.ifft2(pieces, axes=(2, 4), norm='ortho').reshape(slot_total, SIDE, SIDE, D)
    chosen = jnp.where((slot_kinds == 0)[:, None, None, None], whole_grid, quarter_grid)
    return jnp.real(chosen)

def mix_ref(real_in, imag_in, weight, offset):
    blocks = weight.reshape(NB, BS, 2, BS)
    weight_real = blocks[:, :, 0, :]
    weight_imag = blocks[:, :, 1, :]
    pieces = offset.reshape(NB, 2, BS)

    def product_of(left, right):
        return jnp.einsum('nkc,kco->nko', left, right, precision=HIGHEST)
    out_real = product_of(real_in, weight_real) - product_of(imag_in, weight_imag) + pieces[:, 0, :]
    out_imag = product_of(real_in, weight_imag) + product_of(imag_in, weight_real) + pieces[:, 1, :]
    return (out_real, out_imag)

def forward(tokens_in, params, slot_kinds):
    filter_gain, filter_shift, inner_weight, inner_bias, outer_weight, outer_bias, feed_gain, feed_shift, expand_weight, expand_bias, contract_weight, contract_bias = params
    slot_total = tokens_in.shape[0]
    normed = norm_rows(tokens_in, filter_gain, filter_shift)
    spec_real, spec_imag = spectrum_ref(normed.reshape(slot_total, SIDE, SIDE, D), slot_kinds)
    spec_real = low(spec_real).reshape(-1, NB, BS)
    spec_imag = low(spec_imag).reshape(-1, NB, BS)
    inner_real, inner_imag = mix_ref(spec_real, spec_imag, inner_weight, inner_bias)
    inner_real = low_back(inner_real)
    inner_imag = low_back(inner_imag)
    act_real = low(jax.nn.gelu(inner_real, approximate=False))
    act_imag = low(jax.nn.gelu(inner_imag, approximate=False))
    outer_real, outer_imag = mix_ref(act_real, act_imag, outer_weight, outer_bias)
    outer_real = low_back(outer_real)
    outer_imag = low_back(outer_imag)
    shrunk_real = outer_real - SHRINK * jnp.tanh(outer_real / SHRINK)
    shrunk_imag = outer_imag - SHRINK * jnp.tanh(outer_imag / SHRINK)
    mixer_out = inverse_ref(shrunk_real.reshape(slot_total, SIDE, SIDE, D), shrunk_imag.reshape(slot_total, SIDE, SIDE, D), slot_kinds)
    mixer_out = mixer_out.reshape(slot_total, SIDE * SIDE, D)
    middle = tokens_in + mixer_out
    feed_in = low(norm_rows(middle, feed_gain, feed_shift)).reshape(-1, D)
    hidden_pre = low_back(jnp.dot(feed_in, expand_weight, precision=HIGHEST) + expand_bias)
    hidden_act = low(jax.nn.gelu(hidden_pre, approximate=False))
    branch = low_back(jnp.dot(hidden_act, contract_weight, precision=HIGHEST) + contract_bias)
    branch = branch.reshape(middle.shape)
    result = middle + branch
    return (result, (mixer_out, middle, branch))

def reference(tokens, cotangent, slot_items, filter_gain, filter_shift, inner_weight, inner_bias, outer_weight, outer_bias, feed_gain, feed_shift, expand_weight, expand_bias, contract_weight, contract_bias):
    params = tuple((item.astype(jnp.float32) for item in (filter_gain, filter_shift, inner_weight, inner_bias, outer_weight, outer_bias, feed_gain, feed_shift, expand_weight, expand_bias, contract_weight, contract_bias)))
    tokens_in = tokens.astype(jnp.float32)

    def wrapped(tokens_arg, *param_args):
        return forward(tokens_arg, param_args, slot_items)
    result, backward_fn, extras = jax.vjp(wrapped, tokens_in, *params, has_aux=True)
    mask = valid_rows(slot_items)
    masked_grad = cotangent.astype(jnp.float32) * mask[:, :, None]
    gradients = backward_fn(masked_grad)
    mixer_out, middle, branch = extras
    patch_total = jnp.sum(mask) * D

    def root_square(values):
        return jnp.sqrt(jnp.sum(values * values * mask[:, :, None]) / patch_total)
    statistics = jnp.stack([root_square(tokens_in), root_square(mixer_out), root_square(middle), root_square(branch), root_square(result)])
    return (result.astype(jnp.bfloat16), gradients[0], gradients[1], gradients[2], gradients[3], gradients[4], gradients[5], gradients[6], gradients[7], gradients[8], gradients[9], gradients[10], gradients[11], gradients[12], statistics)
```

```python
import functools
import math

import jax
import jax.numpy as jnp
import numpy as np
from jax import lax
from jax.experimental import pallas as pl
from jax.experimental.pallas import tpu as pltpu
from jax.sharding import PartitionSpec as P

BS = 64
NB = 8
SIDE = 16
PATCHES = SIDE * SIDE
WIDTH = NB * BS
HALF = PATCHES // 2
PAIRS = NB // 2
EPSILON = 1e-05
SHRINK = 0.25
F32 = jnp.float32
BF16 = jnp.bfloat16
NT = (((1,), (1,)), ((), ()))
TN = (((0,), (0,)), ((), ()))
TABLE_SCALE = 1.132805


def frequency_order(side):
    pairs, selfs = [], []
    for a in range(side):
        for b in range(side):
            other = ((-a) % side, (-b) % side)
            if other == (a, b):
                selfs.append((a, b))
            elif (a, b) < other:
                pairs.append((a, b))
    return pairs, selfs


def spectrum_table(side):
    tiles = SIDE // side
    pairs, selfs = frequency_order(side)
    row = np.arange(PATCHES) // SIDE
    col = np.arange(PATCHES) % SIDE
    top, bottom = [], []
    for kind in ("pair", "self"):
        for qr in range(tiles):
            for qc in range(tiles):
                inside = (row // side == qr) & (col // side == qc)
                listed = pairs if kind == "pair" else selfs
                for at, (a, b) in enumerate(listed):
                    angle = 2.0 * math.pi / side * ((a * row + b * col) % side)
                    if kind == "pair":
                        top.append(np.where(inside, np.cos(angle), 0.0) / side)
                        bottom.append(np.where(inside, -np.sin(angle), 0.0) / side)
    extra = []
    for at in range(len(selfs)):
        for qr in range(tiles):
            for qc in range(tiles):
                inside = (row // side == qr) & (col // side == qc)
                a, b = selfs[at]
                angle = 2.0 * math.pi / side * ((a * row + b * col) % side)
                extra.append(np.where(inside, np.cos(angle), 0.0) / side)
    half = len(extra) // 2
    return np.array(top + extra[:half] + bottom + extra[half:]), len(top), tiles * tiles


WHOLE_TABLE, WHOLE_PAIRS, WHOLE_ZEROS = spectrum_table(SIDE)
PART_TABLE, PART_PAIRS, PART_ZEROS = spectrum_table(SIDE // 2)
TABLES = np.concatenate([WHOLE_TABLE * TABLE_SCALE, PART_TABLE], axis=0)


def dot(a, b, dims=(((1,), (0,)), ((), ()))):
    return lax.dot_general(a, b, dims, preferred_element_type=F32)


def sum8(values):
    return jnp.sum(values.reshape(-1, 8, values.shape[-1]), axis=0)


def gelu_and_slope(v):
    phi = 0.5 * lax.erf(v * 0.7071067811865476) + 0.5
    bell = jnp.exp2(v * v * (-0.5 / math.log(2.0))) * (1.0 / math.sqrt(2.0 * math.pi))
    return v * phi, phi + v * bell


def row_stats(values):
    centre = values - jnp.mean(values, axis=-1, keepdims=True)
    scale = lax.rsqrt(jnp.mean(centre * centre, axis=-1, keepdims=True) + EPSILON)
    return centre * scale, scale


def slot_facts(kind):
    whole = kind == 0
    pairs = jnp.where(whole, WHOLE_PAIRS, PART_PAIRS)
    zeros = jnp.where(whole, WHOLE_ZEROS, PART_ZEROS)
    scale = jnp.where(whole, 1.0 / TABLE_SCALE, 1.0).astype(F32)
    return whole, pairs, zeros, scale


def table_of(R, kind):
    at = pl.multiple_of(jnp.minimum(kind, 1) * PATCHES, PATCHES)
    return R.table[pl.ds(at, PATCHES), :]


def spread(halves, pairs):
    top, bottom = halves[:HALF], halves[HALF:]
    is_pair = lax.broadcasted_iota(jnp.int32, top.shape, 0) < pairs
    imag = jnp.where(is_pair, bottom, 0.0)
    return top, imag, jnp.where(is_pair, top, bottom), -imag


def fold(block, pairs):
    ra, ia = block[:HALF, :128], block[:HALF, 128:]
    rb, ib = block[HALF:, :128], block[HALF:, 128:]
    is_pair = lax.broadcasted_iota(jnp.int32, ra.shape, 0) < pairs
    return ra + jnp.where(is_pair, rb, 0.0), jnp.where(is_pair, ia - ib, rb)


def complex_pairs(weight_ref, out_ref):
    low = lax.broadcasted_iota(jnp.int32, (BS, 128), 1) < BS
    for j in range(PAIRS):
        first = weight_ref[pl.ds(128 * j, BS), :].astype(F32)
        second = weight_ref[pl.ds(128 * j + BS, BS), :].astype(F32)
        real = jnp.concatenate([jnp.where(low, first, 0.0), jnp.where(low, 0.0, pltpu.roll(second, BS, 1))], axis=0)
        imag = jnp.concatenate([jnp.where(low, pltpu.roll(first, BS, 1), 0.0), jnp.where(low, 0.0, second)], axis=0)
        out_ref[pl.ds(256 * j, 256), :] = jnp.concatenate(
            [jnp.concatenate([real, imag], axis=1), jnp.concatenate([-imag, real], axis=1)], axis=0
        ).astype(BF16)


def pair_gradient(product):
    real = product[:128, :128] + product[128:, 128:]
    imag = product[:128, 128:] - product[128:, :128]
    low = lax.broadcasted_iota(jnp.int32, (BS, 128), 1) < BS
    first = jnp.where(low, real[:BS], pltpu.roll(imag[:BS], BS, 1))
    second = jnp.where(low, pltpu.roll(real[BS:], BS, 1), imag[BS:])
    return jnp.concatenate([first, second], axis=0)


def masked_squares(values, kind):
    squares = values * values
    parts = jnp.sum(squares.reshape(2, 8, 2, 8, squares.shape[-1]), axis=1)
    total = parts[0, 0]
    for q in range(1, 4):
        valid = jnp.where((kind == 0) | (q < kind), 1.0, 0.0).astype(F32)
        total = total + valid * parts[q // 2, q % 2]
    return total


def masked(values, kind):
    position = lax.broadcasted_iota(jnp.int32, values.shape, 0)
    quadrant = (position >> 7) * 2 + ((position >> 3) & 1)
    return jnp.where((kind == 0) | (quadrant < kind), values, 0.0)


def mixer_forward(R, slot):
    kind = R.items[slot]
    whole, pairs, zeros, scale = slot_facts(kind)
    rows = pl.ds(pl.multiple_of(slot * PATCHES, PATCHES), PATCHES)
    table = table_of(R, kind)
    x = R.tok[rows, :].astype(F32)
    xhat, _ = row_stats(x)
    R.stats[pl.ds(0, 8), :] += masked_squares(x, kind)
    spec = dot(table, xhat.astype(BF16)) * (R.vec[0:1, :] * scale)
    top = lax.broadcasted_iota(jnp.int32, (HALF, WIDTH), 0)
    at_zero = (top >= pairs) & (top < pairs + zeros)
    shift = R.vec[1:2, :] * jnp.where(whole, float(SIDE), float(SIDE // 2)).astype(F32)
    spec = jnp.concatenate([spec[:HALF] + jnp.where(at_zero, shift, 0.0), spec[HALF:]], axis=0)
    ra, ia, rb, ib = [part.astype(BF16) for part in spread(spec, pairs)]
    tops, bottoms = [], []
    for j in range(PAIRS):
        lanes = slice(256 * j, 256 * j + 256)
        cols = slice(128 * j, 128 * j + 128)
        low = jnp.concatenate(
            [
                jnp.concatenate([ra[:, cols], ia[:, cols]], axis=1),
                jnp.concatenate([rb[:, cols], ib[:, cols]], axis=1),
            ],
            axis=0,
        )
        R.spec[rows, lanes] = low
        pre = dot(low, R.win[pl.ds(256 * j, 256), :]) + jnp.concatenate([R.vec[2:3, cols], R.vec[3:4, cols]], axis=1)
        act, slope = gelu_and_slope(pre)
        act = act.astype(BF16)
        R.act[rows, lanes] = act
        R.slope[rows, lanes] = slope.astype(BF16)
        post = dot(act, R.wout[pl.ds(256 * j, 256), :]) + jnp.concatenate(
            [R.vec[4:5, cols], R.vec[5:6, cols]], axis=1
        )
        bent = jnp.tanh(post * (1.0 / SHRINK))
        R.bent[rows, lanes] = (bent * bent).astype(BF16)
        u, v = fold(post - SHRINK * bent, pairs)
        tops.append(u.astype(BF16))
        bottoms.append(v.astype(BF16))
    folded = jnp.concatenate([jnp.concatenate(tops, axis=1), jnp.concatenate(bottoms, axis=1)], axis=0)
    mixer_out = dot(table, folded, TN) * scale
    R.stats[pl.ds(8, 8), :] += masked_squares(mixer_out, kind)
    middle = x + mixer_out
    R.stats[pl.ds(16, 8), :] += masked_squares(middle, kind)
    R.mid[rows, :] = middle
    yhat, _ = row_stats(middle)
    R.feed[rows, :] = (yhat * R.vec[6:7, :] + R.vec[7:8, :]).astype(BF16)
    grad = masked(R.cot[rows, :].astype(F32), kind)
    R.sums[pl.ds(16, 8), :] += sum8(grad)
    R.msk[rows, :] = grad.astype(BF16)


def mlp_chunk(R, rows, cols, first):
    feed, grad = R.feed[rows, :], R.msk[rows, :]
    hidden, slope = gelu_and_slope(dot(feed, R.we[:, cols]) + R.be[0:1, cols])
    hidden = hidden.astype(BF16)
    R.hidden[rows, cols] = hidden
    back = (dot(grad, R.wc[cols, :], NT) * slope).astype(BF16)
    R.hgrad[rows, :] = back
    R.dbe[:, cols] += sum8(back.astype(F32))
    branch = dot(hidden, R.wc[cols, :])
    fgrad = dot(back, R.we[:, cols], NT)
    if first:
        R.br[rows, :] = branch
        R.fg[rows, :] = fgrad
    else:
        R.br[rows, :] += branch
        R.fg[rows, :] += fgrad


def mixer_backward_first(R, slot):
    kind = R.items[slot]
    whole, pairs, zeros, scale = slot_facts(kind)
    rows = pl.ds(pl.multiple_of(slot * PATCHES, PATCHES), PATCHES)
    table = table_of(R, kind)
    branch = R.br[rows, :] + R.vec[8:9, :]
    middle = R.mid[rows, :]
    result = middle + branch
    R.stats[pl.ds(24, 8), :] += masked_squares(branch, kind)
    R.stats[pl.ds(32, 8), :] += masked_squares(result, kind)
    R.out[rows, :] = result.astype(BF16)
    feed_grad = R.fg[rows, :]
    yhat, yscale = row_stats(middle)
    R.sums[pl.ds(0, 8), :] += sum8(feed_grad * yhat)
    R.sums[pl.ds(8, 8), :] += sum8(feed_grad)
    scaled = feed_grad * R.vec[6:7, :]
    inner = scaled - jnp.mean(scaled, axis=-1, keepdims=True) - yhat * jnp.mean(scaled * yhat, axis=-1, keepdims=True)
    mgrad = R.msk[rows, :].astype(F32) + inner * yscale
    R.mgrad[rows, :] = mgrad
    parts = spread(dot(table, mgrad.astype(BF16)) * scale, pairs)
    for j in range(PAIRS):
        lanes = slice(256 * j, 256 * j + 256)
        cols = slice(128 * j, 128 * j + 128)
        ra, ia, rb, ib = [part[:, cols] for part in parts]
        grad = jnp.concatenate([jnp.concatenate([ra, ia], axis=1), jnp.concatenate([rb, ib], axis=1)], axis=0)
        grad = (grad * R.bent[rows, lanes].astype(F32)).astype(BF16)
        R.ograd[rows, lanes] = grad
        R.dbias[pl.ds(0, 8), lanes] += sum8(grad.astype(F32))
        grad = dot(grad, R.wout[pl.ds(256 * j, 256), :], NT) * R.slope[rows, lanes].astype(F32)
        grad = grad.astype(BF16)
        R.igrad[rows, lanes] = grad
        R.dbias[pl.ds(8, 8), lanes] += sum8(grad.astype(F32))


def mixer_weight_gradients(R, put_inner, put_outer):
    for j in range(PAIRS):
        lanes = slice(256 * j, 256 * j + 256)
        put_outer(j, pair_gradient(dot(R.act[:, lanes], R.ograd[:, lanes], TN)))
        put_inner(j, pair_gradient(dot(R.spec[:, lanes], R.igrad[:, lanes], TN)))


def mixer_backward_second(R, slot, put):
    kind = R.items[slot]
    whole, pairs, zeros, scale = slot_facts(kind)
    rows = pl.ds(pl.multiple_of(slot * PATCHES, PATCHES), PATCHES)
    table = table_of(R, kind)
    tops, bottoms = [], []
    for j in range(PAIRS):
        lanes = slice(256 * j, 256 * j + 256)
        u, v = fold(dot(R.igrad[rows, lanes], R.win[pl.ds(256 * j, 256), :], NT), pairs)
        tops.append(u.astype(BF16))
        bottoms.append(v.astype(BF16))
    folded = jnp.concatenate([jnp.concatenate(tops, axis=1), jnp.concatenate(bottoms, axis=1)], axis=0)
    ngrad = dot(table, folded, TN) * scale
    xhat, xscale = row_stats(R.tok[rows, :].astype(F32))
    R.sums[pl.ds(24, 8), :] += sum8(ngrad * xhat)
    R.sums[pl.ds(32, 8), :] += sum8(ngrad)
    scaled = ngrad * R.vec[0:1, :]
    inner = scaled - jnp.mean(scaled, axis=-1, keepdims=True) - xhat * jnp.mean(scaled * xhat, axis=-1, keepdims=True)
    put(slot, rows, R.mgrad[rows, :] + inner * xscale)
class Refs:
    pass


VMEM = pl.BlockSpec(memory_space=pltpu.VMEM)
SMEM = pl.BlockSpec(memory_space=pltpu.SMEM)
ROOM = 62 * 2**20
CHUNK = 512


def named(names, refs):
    R = Refs()
    for name, ref in zip(names, refs):
        setattr(R, name, ref)
    return R


def plain_call(body, ins, outs, scratch, name):
    names = list(ins) + list(outs) + list(scratch)

    def kernel(*refs):
        body(named(names, refs))

    values = pl.pallas_call(
        kernel,
        out_shape=[jax.ShapeDtypeStruct(*spec) for spec in outs.values()],
        in_specs=[SMEM if key == "items" else VMEM for key in ins],
        out_specs=[VMEM for _ in outs],
        scratch_shapes=[pltpu.VMEM(*spec) for spec in scratch.values()],
        compiler_params=pltpu.CompilerParams(vmem_limit_bytes=ROOM),
        name=name,
    )(*ins.values())
    return dict(zip(outs, values))


def forward_body(R):
    complex_pairs(R.inner, R.win)
    complex_pairs(R.outer, R.wout)
    R.stats[...] = jnp.zeros_like(R.stats)
    R.sums[...] = jnp.zeros_like(R.sums)

    @pl.loop(0, R.tok.shape[0] // PATCHES)
    def _(slot):
        mixer_forward(R, slot)


def mlp_body(R):
    rows_all = R.feed.shape[0]
    hidden_all = R.we.shape[1]
    R.dbe[...] = jnp.zeros_like(R.dbe)
    for at in range(0, hidden_all, CHUNK):
        cols = slice(at, at + CHUNK)

        @pl.loop(0, rows_all // CHUNK)
        def _(i):
            mlp_chunk(R, pl.ds(pl.multiple_of(i * CHUNK, CHUNK), CHUNK), cols, at == 0)

        R.dwe[:, cols] = dot(R.feed[...], R.hgrad[...], TN).astype(BF16)

    @pl.loop(0, hidden_all // CHUNK)
    def _(i):
        cols = pl.ds(pl.multiple_of(i * CHUNK, CHUNK), CHUNK)
        R.dwc[:, cols] = dot(R.msk[...], R.hidden[:, cols], TN).astype(BF16)


def backward_body(R):
    R.stats[...] = jnp.zeros_like(R.stats)
    R.sums[...] = jnp.zeros_like(R.sums)
    R.dbias[...] = jnp.zeros_like(R.dbias)
    slots = R.tok.shape[0] // PATCHES

    @pl.loop(0, slots)
    def _(slot):
        mixer_backward_first(R, slot)

    def put_inner(j, value):
        R.dinner[pl.ds(128 * j, 128), :] = value

    def put_outer(j, value):
        R.douter[pl.ds(128 * j, 128), :] = value

    mixer_weight_gradients(R, put_inner, put_outer)

    def put(slot, rows, value):
        R.igrad_out[rows, :] = value

    @pl.loop(0, slots)
    def _(slot):
        mixer_backward_second(R, slot, put)


def pair_order(vector):
    parts = vector.reshape(NB, 2, BS)
    return parts[:, 0].reshape(1, WIDTH), parts[:, 1].reshape(1, WIDTH)


def body_by_collectives(
    tokens, cotangent, slot_items, filter_gain, filter_shift, inner_weight, inner_bias, outer_weight, outer_bias,
    feed_gain, feed_shift, expand_weight, expand_bias, contract_weight, contract_bias,
):
    def gather(x):
        return lax.all_gather(x, "fsdp", axis=0, tiled=True)

    vectors = (filter_gain, filter_shift, inner_bias, outer_bias, feed_gain, feed_shift, contract_bias, expand_bias)
    sizes = [v.shape[0] for v in vectors]
    packed = lax.all_gather(jnp.concatenate(vectors), "fsdp", axis=0)
    ends = np.cumsum([0] + sizes)
    g1, s1, bi, bo, g2, s2, bc, be = [packed[:, a:b].reshape(-1).astype(F32) for a, b in zip(ends, ends[1:])]
    vec = jnp.concatenate(
        [g1[None], s1[None], *pair_order(bi), *pair_order(bo), g2[None], s2[None], bc[None], jnp.zeros((7, WIDTH), F32)]
    )
    inner, outer, we, wc = gather(inner_weight), gather(outer_weight), gather(expand_weight), gather(contract_weight)
    n = tokens.shape[0] * PATCHES
    hidden = we.shape[1]
    tok, cot = tokens.reshape(n, WIDTH), cotangent.reshape(n, WIDTH)
    table = jnp.asarray(TABLES, BF16)
    wide = ((n, 2 * WIDTH), BF16)
    flat = ((n, WIDTH), BF16)
    full = ((n, WIDTH), F32)
    pairs = ((2 * WIDTH, 2 * 2 * BS), BF16)
    sums = ((40, WIDTH), F32)
    a = plain_call(
        forward_body,
        dict(items=slot_items, tok=tok, cot=cot, table=table, vec=vec, inner=inner, outer=outer),
        dict(spec=wide, act=wide, slope=wide, bent=wide, mid=full, feed=flat, msk=flat, win=pairs, wout=pairs, stats=sums, sums=sums),
        {},
        "mixer_forward",
    )
    b = plain_call(
        mlp_body,
        dict(feed=a["feed"], msk=a["msk"], we=we, wc=wc, be=be.reshape(1, hidden)),
        dict(br=full, fg=full, dwe=((WIDTH, hidden), BF16), dwc=((WIDTH, hidden), BF16), dbe=((8, hidden), F32)),
        dict(hidden=((n, hidden), BF16), hgrad=((n, CHUNK), BF16)),
        "mlp",
    )
    c = plain_call(
        backward_body,
        dict(
            items=slot_items, tok=tok, table=table, vec=vec, spec=a["spec"], act=a["act"], slope=a["slope"], bent=a["bent"],
            mid=a["mid"], msk=a["msk"], br=b["br"], fg=b["fg"], win=a["win"], wout=a["wout"],
        ),
        dict(
            out=flat, igrad_out=full, dinner=((WIDTH, 2 * BS), F32), douter=((WIDTH, 2 * BS), F32),
            dbias=((16, 2 * WIDTH), F32), sums=sums, stats=sums,
        ),
        dict(mgrad=full, ograd=wide, igrad=wide),
        "mixer_backward",
    )

    def scatter(x):
        return lax.psum_scatter(x, "fsdp", scatter_dimension=0, tiled=True)

    def rows_of(x, at):
        return jnp.sum(x[at : at + 8], axis=0)

    def bias_of(at):
        parts = rows_of(c["dbias"], at).reshape(PAIRS, 2, 2, BS)
        return jnp.swapaxes(parts, 1, 2).reshape(2 * WIDTH)

    sums_ = a["sums"] + c["sums"]
    stats_ = a["stats"] + c["stats"]
    small = [
        rows_of(sums_, 24), rows_of(sums_, 32), bias_of(8), bias_of(0), rows_of(sums_, 0), rows_of(sums_, 8),
        rows_of(sums_, 16), jnp.sum(b["dbe"], axis=0),
    ]
    fsdp = lax.axis_size("fsdp")
    small = jnp.concatenate([v.reshape(fsdp, -1) for v in small], axis=1)
    weights = jnp.concatenate([c["dinner"].reshape(fsdp, -1), c["douter"].reshape(fsdp, -1)], axis=1)
    weights = jnp.concatenate([weights, small], axis=1).astype(BF16)
    own_small = scatter(weights.reshape(-1))
    own_we = scatter(b["dwe"])
    own_wc = scatter(b["dwc"].T)
    own_small, own_we, own_wc = lax.psum((own_small, own_we, own_wc), "rep")
    own_small = own_small.astype(F32)
    cut = inner_weight.size
    own_iw, own_ow = own_small[:cut].reshape(inner_weight.shape), own_small[cut : 2 * cut].reshape(inner_weight.shape)
    own = [own_small[2 * cut + x : 2 * cut + y] for x, y in zip(ends, ends[1:])]
    kinds = slot_items[:, None]
    valid = jnp.where((kinds == 0) | (jnp.arange(4)[None] < kinds), 1.0, 0.0)
    local = jnp.concatenate([jnp.sum(stats_.reshape(5, -1), axis=1), jnp.sum(valid)[None] * (PATCHES // 4 * WIDTH)])
    total = lax.psum(local, ("rep", "fsdp"))
    statistics = jnp.sqrt(total[:5] / total[5])
    return (
        c["out"].reshape(tokens.shape), c["igrad_out"].reshape(tokens.shape), own[0], own[1], own_iw, own[2], own_ow, own[3],
        own[4], own[5], own_we.astype(F32), own[7], own_wc.astype(F32), own[6], statistics,
    )


def specs():
    items = P(("rep", "fsdp"))
    big = P(("rep", "fsdp"), None, None)
    one, two = P("fsdp"), P("fsdp", None)
    ins = (big, big, items, one, one, two, one, two, one, one, one, two, one, two, one)
    outs = (big, big, one, one, two, one, two, one, one, one, two, one, two, one, P())
    return ins, outs


def solution(mesh):
    ins, outs = specs()
    return jax.shard_map(body_by_collectives, mesh=mesh, in_specs=ins, out_specs=outs, check_vma=False)
```

```python
import functools
import math

import jax
import jax.numpy as jnp
import numpy as np
from jax import lax
from jax.experimental import pallas as pl
from jax.experimental.pallas import tpu as pltpu
from jax.sharding import PartitionSpec as P

BS = 64
NB = 8
SIDE = 16
PATCHES = SIDE * SIDE
WIDTH = NB * BS
HALF = PATCHES // 2
PAIRS = NB // 2
CHUNK = 512
EPSILON = 1e-05
SHRINK = 0.25
F32 = jnp.float32
BF16 = jnp.bfloat16
NT = (((1,), (1,)), ((), ()))
TN = (((0,), (0,)), ((), ()))
TABLE_SCALE = 1.132805


def frequency_order(side):
    pairs, selfs = [], []
    for a in range(side):
        for b in range(side):
            other = ((-a) % side, (-b) % side)
            if other == (a, b):
                selfs.append((a, b))
            elif (a, b) < other:
                pairs.append((a, b))
    return pairs, selfs


def spectrum_table(side):
    tiles = SIDE // side
    pairs, selfs = frequency_order(side)
    row = np.arange(PATCHES) // SIDE
    col = np.arange(PATCHES) % SIDE
    top, bottom = [], []
    for kind in ("pair", "self"):
        for qr in range(tiles):
            for qc in range(tiles):
                inside = (row // side == qr) & (col // side == qc)
                listed = pairs if kind == "pair" else selfs
                for at, (a, b) in enumerate(listed):
                    angle = 2.0 * math.pi / side * ((a * row + b * col) % side)
                    if kind == "pair":
                        top.append(np.where(inside, np.cos(angle), 0.0) / side)
                        bottom.append(np.where(inside, -np.sin(angle), 0.0) / side)
    extra = []
    for at in range(len(selfs)):
        for qr in range(tiles):
            for qc in range(tiles):
                inside = (row // side == qr) & (col // side == qc)
                a, b = selfs[at]
                angle = 2.0 * math.pi / side * ((a * row + b * col) % side)
                extra.append(np.where(inside, np.cos(angle), 0.0) / side)
    half = len(extra) // 2
    return np.array(top + extra[:half] + bottom + extra[half:]), len(top), tiles * tiles


WHOLE_TABLE, WHOLE_PAIRS, WHOLE_ZEROS = spectrum_table(SIDE)
PART_TABLE, PART_PAIRS, PART_ZEROS = spectrum_table(SIDE // 2)
TABLES = np.concatenate([WHOLE_TABLE * TABLE_SCALE, PART_TABLE], axis=0)


def dot(a, b, dims=(((1,), (0,)), ((), ()))):
    return lax.dot_general(a, b, dims, preferred_element_type=F32)


def sum8(values):
    return jnp.sum(values.reshape(-1, 8, values.shape[-1]), axis=0)


def gelu_and_slope(v):
    phi = 0.5 * lax.erf(v * 0.7071067811865476) + 0.5
    bell = jnp.exp2(v * v * (-0.5 / math.log(2.0))) * (1.0 / math.sqrt(2.0 * math.pi))
    return v * phi, phi + v * bell


def row_stats(values):
    centre = values - jnp.mean(values, axis=-1, keepdims=True)
    scale = lax.rsqrt(jnp.mean(centre * centre, axis=-1, keepdims=True) + EPSILON)
    return centre * scale, scale


def kind_of(R, slot, lanes=WIDTH):
    return jnp.full((1, lanes), R.items[slot], jnp.int32)


def slot_facts(kind):
    whole = kind == 0
    pairs = jnp.where(whole, WHOLE_PAIRS, PART_PAIRS)
    scale = jnp.where(whole, 1.0 / TABLE_SCALE, 1.0).astype(F32)
    return whole, pairs, scale


def table_of(R, kind):
    whole = jnp.where(kind[:, :PATCHES] == 0, 1.0, 0.0).astype(F32)
    first, second = whole.astype(BF16), (1.0 - whole).astype(BF16)
    return R.table[pl.ds(0, PATCHES), :] * first + R.table[pl.ds(PATCHES, PATCHES), :] * second


def spread(halves, pairs):
    top, bottom = halves[:HALF], halves[HALF:]
    is_pair = lax.broadcasted_iota(jnp.int32, top.shape, 0) < pairs[:, : top.shape[1]]
    imag = jnp.where(is_pair, bottom, 0.0)
    return top, imag, jnp.where(is_pair, top, bottom), -imag


def fold(block, pairs):
    ra, ia = block[:HALF, :128], block[:HALF, 128:]
    rb, ib = block[HALF:, :128], block[HALF:, 128:]
    is_pair = lax.broadcasted_iota(jnp.int32, ra.shape, 0) < pairs[:, : ra.shape[1]]
    return ra + jnp.where(is_pair, rb, 0.0), jnp.where(is_pair, ia - ib, rb)


def complex_pairs(weight_ref, out_ref):
    low = lax.broadcasted_iota(jnp.int32, (BS, 128), 1) < BS
    for j in range(PAIRS):
        first, second = weight_ref[2 * j].astype(F32), weight_ref[2 * j + 1].astype(F32)
        real = jnp.concatenate([jnp.where(low, first, 0.0), jnp.where(low, 0.0, pltpu.roll(second, BS, 1))], axis=0)
        imag = jnp.concatenate([jnp.where(low, pltpu.roll(first, BS, 1), 0.0), jnp.where(low, 0.0, second)], axis=0)
        out_ref[pl.ds(256 * j, 256), :] = jnp.concatenate(
            [jnp.concatenate([real, imag], axis=1), jnp.concatenate([-imag, real], axis=1)], axis=0
        ).astype(BF16)


def pair_gradient(product):
    real = product[:128, :128] + product[128:, 128:]
    imag = product[:128, 128:] - product[128:, :128]
    low = lax.broadcasted_iota(jnp.int32, (BS, 128), 1) < BS
    first = jnp.where(low, real[:BS], pltpu.roll(imag[:BS], BS, 1))
    second = jnp.where(low, pltpu.roll(real[BS:], BS, 1), imag[BS:])
    return jnp.concatenate([first, second], axis=0)


def masked_squares(values, kind):
    squares = values * values
    parts = jnp.sum(squares.reshape(2, 8, 2, 8, squares.shape[-1]), axis=1)
    total = parts[0, 0]
    for q in range(1, 4):
        valid = jnp.where((kind == 0) | (q < kind), 1.0, 0.0).astype(F32)
        total = total + valid * parts[q // 2, q % 2]
    return total


def masked(values, kind):
    position = lax.broadcasted_iota(jnp.int32, values.shape, 0)
    quadrant = (position >> 7) * 2 + ((position >> 3) & 1)
    return jnp.where((kind == 0) | (quadrant < kind), values, 0.0)


def mixer_forward(R, slot):
    kind = kind_of(R, slot)
    whole, pairs, scale = slot_facts(kind)
    rows = pl.ds(pl.multiple_of(slot * PATCHES, PATCHES), PATCHES)
    table = table_of(R, kind)
    x = R.tok[rows, :].astype(F32)
    xhat, _ = row_stats(x)
    R.stats[pl.ds(0, 8), :] += masked_squares(x, kind)
    spec = dot(table, xhat.astype(BF16)) * (R.vec[0:1, :] * scale)
    top = lax.broadcasted_iota(jnp.int32, (HALF, WIDTH), 0)
    at_zero = (top >= pairs) & (top < pairs + jnp.where(whole, WHOLE_ZEROS, PART_ZEROS))
    shift = R.vec[1:2, :] * jnp.where(whole, float(SIDE), float(SIDE // 2)).astype(F32)
    spec = jnp.concatenate([spec[:HALF] + jnp.where(at_zero, shift, 0.0), spec[HALF:]], axis=0)
    ra, ia, rb, ib = [part.astype(BF16) for part in spread(spec, pairs)]
    tops, bottoms = [], []
    for j in range(PAIRS):
        lanes = slice(256 * j, 256 * j + 256)
        cols = slice(128 * j, 128 * j + 128)
        low = jnp.concatenate(
            [
                jnp.concatenate([ra[:, cols], ia[:, cols]], axis=1),
                jnp.concatenate([rb[:, cols], ib[:, cols]], axis=1),
            ],
            axis=0,
        )
        R.spec[rows, lanes] = low
        pre = dot(low, R.win[pl.ds(256 * j, 256), :]) + jnp.concatenate([R.vec[2:3, cols], R.vec[3:4, cols]], axis=1)
        act, slope = gelu_and_slope(pre)
        act = act.astype(BF16)
        R.act[rows, lanes] = act
        R.slope[rows, lanes] = slope.astype(BF16)
        post = dot(act, R.wout[pl.ds(256 * j, 256), :]) + jnp.concatenate(
            [R.vec[4:5, cols], R.vec[5:6, cols]], axis=1
        )
        bent = jnp.tanh(post * (1.0 / SHRINK))
        R.bent[rows, lanes] = (bent * bent).astype(BF16)
        u, v = fold(post - SHRINK * bent, pairs)
        tops.append(u.astype(BF16))
        bottoms.append(v.astype(BF16))
    folded = jnp.concatenate([jnp.concatenate(tops, axis=1), jnp.concatenate(bottoms, axis=1)], axis=0)
    mixer_out = dot(table, folded, TN) * scale
    R.stats[pl.ds(8, 8), :] += masked_squares(mixer_out, kind)
    middle = x + mixer_out
    R.stats[pl.ds(16, 8), :] += masked_squares(middle, kind)
    R.mid[rows, :] = middle
    yhat, _ = row_stats(middle)
    R.feed[rows, :] = (yhat * R.vec[6:7, :] + R.vec[7:8, :]).astype(BF16)
    grad = masked(R.cot[rows, :].astype(F32), kind)
    R.sums[pl.ds(16, 8), :] += sum8(grad)
    R.msk[rows, :] = grad.astype(BF16)


def mlp_chunk(R, i, cols, first):
    rows = pl.ds(pl.multiple_of(i * CHUNK, CHUNK), CHUNK)
    feed, grad = R.feed[rows, :], R.msk[rows, :]
    hidden, slope = gelu_and_slope(dot(feed, R.we[:, cols]) + R.be[0:1, cols])
    hidden = hidden.astype(BF16)
    R.hidden[rows, cols] = hidden
    back = (dot(grad, R.wc[cols, :], NT) * slope).astype(BF16)
    R.hgrad[pl.ds(i * (CHUNK // PATCHES), CHUNK // PATCHES)] = back.reshape(-1, PATCHES, CHUNK)
    R.dbe[:, cols] += sum8(back.astype(F32))
    branch = dot(hidden, R.wc[cols, :])
    fgrad = dot(back, R.we[:, cols], NT)
    if first:
        R.br[rows, :] = branch
        R.fg[rows, :] = fgrad
    else:
        R.br[rows, :] += branch
        R.fg[rows, :] += fgrad


def mixer_backward_first(R, slot):
    kind = kind_of(R, slot)
    whole, pairs, scale = slot_facts(kind)
    rows = pl.ds(pl.multiple_of(slot * PATCHES, PATCHES), PATCHES)
    table = table_of(R, kind)
    branch = R.br[rows, :] + R.vec[8:9, :]
    middle = R.mid[rows, :]
    result = middle + branch
    R.stats[pl.ds(24, 8), :] += masked_squares(branch, kind)
    R.stats[pl.ds(32, 8), :] += masked_squares(result, kind)
    R.out[rows, :] = result.astype(BF16)
    feed_grad = R.fg[rows, :]
    yhat, yscale = row_stats(middle)
    R.sums[pl.ds(0, 8), :] += sum8(feed_grad * yhat)
    R.sums[pl.ds(8, 8), :] += sum8(feed_grad)
    scaled = feed_grad * R.vec[6:7, :]
    inner = scaled - jnp.mean(scaled, axis=-1, keepdims=True) - yhat * jnp.mean(scaled * yhat, axis=-1, keepdims=True)
    mgrad = R.msk[rows, :].astype(F32) + inner * yscale
    R.mgrad[rows, :] = mgrad
    parts = spread(dot(table, mgrad.astype(BF16)) * scale, pairs)
    for j in range(PAIRS):
        lanes = slice(256 * j, 256 * j + 256)
        cols = slice(128 * j, 128 * j + 128)
        ra, ia, rb, ib = [part[:, cols] for part in parts]
        grad = jnp.concatenate([jnp.concatenate([ra, ia], axis=1), jnp.concatenate([rb, ib], axis=1)], axis=0)
        grad = (grad * R.bent[rows, lanes].astype(F32)).astype(BF16)
        R.ograd[rows, lanes] = grad
        R.dbias[pl.ds(0, 8), lanes] += sum8(grad.astype(F32))
        grad = dot(grad, R.wout[pl.ds(256 * j, 256), :], NT) * R.slope[rows, lanes].astype(F32)
        grad = grad.astype(BF16)
        R.igrad[rows, lanes] = grad
        R.dbias[pl.ds(8, 8), lanes] += sum8(grad.astype(F32))


def mixer_weight_gradients(R, put_inner, put_outer):
    for j in range(PAIRS):
        lanes = slice(256 * j, 256 * j + 256)
        put_outer(j, pair_gradient(dot(R.act[:, lanes], R.ograd[:, lanes], TN)))
        put_inner(j, pair_gradient(dot(R.spec[:, lanes], R.igrad[:, lanes], TN)))


def mixer_backward_second(R, slot, put):
    kind = kind_of(R, slot)
    whole, pairs, scale = slot_facts(kind)
    rows = pl.ds(pl.multiple_of(slot * PATCHES, PATCHES), PATCHES)
    table = table_of(R, kind)
    tops, bottoms = [], []
    for j in range(PAIRS):
        lanes = slice(256 * j, 256 * j + 256)
        u, v = fold(dot(R.igrad[rows, lanes], R.win[pl.ds(256 * j, 256), :], NT), pairs)
        tops.append(u.astype(BF16))
        bottoms.append(v.astype(BF16))
    folded = jnp.concatenate([jnp.concatenate(tops, axis=1), jnp.concatenate(bottoms, axis=1)], axis=0)
    ngrad = dot(table, folded, TN) * scale
    xhat, xscale = row_stats(R.tok[rows, :].astype(F32))
    R.sums[pl.ds(24, 8), :] += sum8(ngrad * xhat)
    R.sums[pl.ds(32, 8), :] += sum8(ngrad)
    scaled = ngrad * R.vec[0:1, :]
    inner = scaled - jnp.mean(scaled, axis=-1, keepdims=True) - xhat * jnp.mean(scaled * xhat, axis=-1, keepdims=True)
    put(slot, rows, R.mgrad[rows, :] + inner * xscale)

class Refs:
    pass


VMEM = pl.BlockSpec(memory_space=pltpu.VMEM)
SMEM = pl.BlockSpec(memory_space=pltpu.SMEM)
ROOM = 127 * 2**19


def named(names, refs):
    R = Refs()
    for name, ref in zip(names, refs):
        setattr(R, name, ref)
    return R


def plain_call(body, ins, outs, scratch, name):
    names = list(ins) + list(outs) + list(scratch)

    def kernel(*refs):
        body(named(names, refs))

    values = pl.pallas_call(
        kernel,
        out_shape=[jax.ShapeDtypeStruct(*spec) for spec in outs.values()],
        in_specs=[SMEM if key == "items" else VMEM for key in ins],
        out_specs=[VMEM for _ in outs],
        scratch_shapes=[pltpu.VMEM(*spec) for spec in scratch.values()],
        compiler_params=pltpu.CompilerParams(vmem_limit_bytes=ROOM),
        name=name,
    )(*ins.values())
    return dict(zip(outs, values))


def forward_body(R):
    complex_pairs(R.inner, R.win)
    complex_pairs(R.outer, R.wout)
    R.stats[...] = jnp.zeros_like(R.stats)
    R.sums[...] = jnp.zeros_like(R.sums)

    @pl.loop(0, R.tok.shape[0] // PATCHES)
    def _(slot):
        mixer_forward(R, slot)


def mlp_body(R):
    rows_all = R.feed.shape[0]
    hidden_all = R.we.shape[1]
    R.dbe[...] = jnp.zeros_like(R.dbe)
    for at in range(0, hidden_all, CHUNK):
        cols = slice(at, at + CHUNK)

        @pl.loop(0, rows_all // CHUNK)
        def _(i):
            mlp_chunk(R, i, cols, at == 0)

        R.dwe[:, cols] = dot(R.feed[...], R.hgrad[...].reshape(-1, CHUNK), TN).astype(BF16)

    @pl.loop(0, hidden_all // CHUNK)
    def _(i):
        cols = pl.ds(pl.multiple_of(i * CHUNK, CHUNK), CHUNK)
        R.dwc[:, cols] = dot(R.msk[...], R.hidden[:, cols], TN).astype(BF16)


def backward_body(R):
    R.stats[...] = jnp.zeros_like(R.stats)
    R.sums[...] = jnp.zeros_like(R.sums)
    R.dbias[...] = jnp.zeros_like(R.dbias)
    slots = R.tok.shape[0] // PATCHES

    @pl.loop(0, slots)
    def _(slot):
        mixer_backward_first(R, slot)

    def put_inner(j, value):
        R.dinner[pl.ds(128 * j, 128), :] = value

    def put_outer(j, value):
        R.douter[pl.ds(128 * j, 128), :] = value

    mixer_weight_gradients(R, put_inner, put_outer)

    def put(slot, rows, value):
        R.igrad_out[rows, :] = value

    @pl.loop(0, slots)
    def _(slot):
        mixer_backward_second(R, slot, put)


def pair_order(vector):
    parts = vector.reshape(NB, 2, BS)
    return parts[:, 0].reshape(1, WIDTH), parts[:, 1].reshape(1, WIDTH)


def body_by_collectives(
    tokens, cotangent, slot_items, filter_gain, filter_shift, inner_weight, inner_bias, outer_weight, outer_bias,
    feed_gain, feed_shift, expand_weight, expand_bias, contract_weight, contract_bias,
):
    def gather(x):
        return lax.all_gather(x, "fsdp", axis=0, tiled=True)

    vectors = (filter_gain, filter_shift, inner_bias, outer_bias, feed_gain, feed_shift, contract_bias, expand_bias)
    sizes = [v.shape[0] for v in vectors]
    packed = lax.all_gather(jnp.concatenate(vectors), "fsdp", axis=0)
    ends = np.cumsum([0] + sizes)
    g1, s1, bi, bo, g2, s2, bc, be = [packed[:, a:b].reshape(-1).astype(F32) for a, b in zip(ends, ends[1:])]
    vec = jnp.concatenate(
        [g1[None], s1[None], *pair_order(bi), *pair_order(bo), g2[None], s2[None], bc[None], jnp.zeros((7, WIDTH), F32)]
    )
    inner, outer, we, wc = gather(inner_weight), gather(outer_weight), gather(expand_weight), gather(contract_weight)
    n = tokens.shape[0] * PATCHES
    hidden = we.shape[1]
    tok, cot = tokens.reshape(n, WIDTH), cotangent.reshape(n, WIDTH)
    table = jnp.asarray(TABLES, BF16)
    wide = ((n, 2 * WIDTH), BF16)
    flat = ((n, WIDTH), BF16)
    full = ((n, WIDTH), F32)
    pairs = ((2 * WIDTH, 2 * 2 * BS), BF16)
    sums = ((40, WIDTH), F32)
    a = plain_call(
        forward_body,
        dict(items=slot_items, tok=tok, cot=cot, table=table, vec=vec, inner=inner.reshape(NB, BS, 2 * BS), outer=outer.reshape(NB, BS, 2 * BS)),
        dict(spec=wide, act=wide, slope=wide, bent=wide, mid=full, feed=flat, msk=flat, win=pairs, wout=pairs, stats=sums, sums=sums),
        {},
        "mixer_forward",
    )
    b = plain_call(
        mlp_body,
        dict(feed=a["feed"], msk=a["msk"], we=we, wc=wc, be=be.reshape(1, hidden)),
        dict(br=full, fg=full, dwe=((WIDTH, hidden), BF16), dwc=((WIDTH, hidden), BF16), dbe=((8, hidden), F32)),
        dict(hidden=((n, hidden), BF16), hgrad=((n // PATCHES, PATCHES, CHUNK), BF16)),
        "mlp",
    )
    c = plain_call(
        backward_body,
        dict(
            items=slot_items, tok=tok, table=table, vec=vec, spec=a["spec"], act=a["act"], slope=a["slope"], bent=a["bent"],
            mid=a["mid"], msk=a["msk"], br=b["br"], fg=b["fg"], win=a["win"], wout=a["wout"],
        ),
        dict(
            out=flat, igrad_out=full, dinner=((WIDTH, 2 * BS), F32), douter=((WIDTH, 2 * BS), F32),
            dbias=((16, 2 * WIDTH), F32), sums=sums, stats=sums,
        ),
        dict(mgrad=full, ograd=wide, igrad=wide),
        "mixer_backward",
    )

    def scatter(x):
        return lax.psum_scatter(x, "fsdp", scatter_dimension=0, tiled=True)

    def rows_of(x, at):
        return jnp.sum(x[at : at + 8], axis=0)

    def bias_of(at):
        parts = rows_of(c["dbias"], at).reshape(PAIRS, 2, 2, BS)
        return jnp.swapaxes(parts, 1, 2).reshape(2 * WIDTH)

    sums_ = a["sums"] + c["sums"]
    stats_ = a["stats"] + c["stats"]
    small = [
        rows_of(sums_, 24), rows_of(sums_, 32), bias_of(8), bias_of(0), rows_of(sums_, 0), rows_of(sums_, 8),
        rows_of(sums_, 16), jnp.sum(b["dbe"], axis=0),
    ]
    fsdp = lax.axis_size("fsdp")
    small = jnp.concatenate([v.reshape(fsdp, -1) for v in small], axis=1)
    weights = jnp.concatenate([c["dinner"].reshape(fsdp, -1), c["douter"].reshape(fsdp, -1)], axis=1)
    weights = jnp.concatenate([weights, small], axis=1).astype(BF16)
    own_small = scatter(weights.reshape(-1))
    own_we = scatter(b["dwe"])
    own_wc = scatter(b["dwc"].T)
    own_small, own_we, own_wc = lax.psum((own_small, own_we, own_wc), "rep")
    own_small = own_small.astype(F32)
    cut = inner_weight.size
    own_iw, own_ow = own_small[:cut].reshape(inner_weight.shape), own_small[cut : 2 * cut].reshape(inner_weight.shape)
    own = [own_small[2 * cut + x : 2 * cut + y] for x, y in zip(ends, ends[1:])]
    kinds = slot_items[:, None]
    valid = jnp.where((kinds == 0) | (jnp.arange(4)[None] < kinds), 1.0, 0.0)
    local = jnp.concatenate([jnp.sum(stats_.reshape(5, -1), axis=1), jnp.sum(valid)[None] * (PATCHES // 4 * WIDTH)])
    total = lax.psum(local, ("rep", "fsdp"))
    statistics = jnp.sqrt(total[:5] / total[5])
    return (
        c["out"].reshape(tokens.shape), c["igrad_out"].reshape(tokens.shape), own[0], own[1], own_iw, own[2], own_ow, own[3],
        own[4], own[5], own_we.astype(F32), own[7], own_wc.astype(F32), own[6], statistics,
    )


def specs():
    items = P(("rep", "fsdp"))
    big = P(("rep", "fsdp"), None, None)
    one, two = P("fsdp"), P("fsdp", None)
    ins = (big, big, items, one, one, two, one, two, one, one, one, two, one, two, one)
    outs = (big, big, one, one, two, one, two, one, one, one, two, one, two, one, P())
    return ins, outs


MESH = pl.DeviceIdType.MESH
ANY = pl.BlockSpec(memory_space=pl.ANY)
FSDP = 8
FIRST = 512


def multiple(value, by):
    return pl.multiple_of(value * by, by)


class Place:
    def __init__(self, copies):
        self.z, self.f = lax.axis_index("rep"), lax.axis_index("fsdp")
        self.core, self.chip = self.f & 1, self.f >> 1
        self.copies = copies

    def peer(self, mask):
        return (self.z, self.f ^ mask)

    def floor(self, offset):
        return (lax.rem(self.z + offset, self.copies), self.f)


def remote(src, dst, sems, at, device):
    send, recv = sems
    return pltpu.make_async_remote_copy(
        src_ref=src, dst_ref=dst, send_sem=send.at[at], recv_sem=recv.at[at], device_id=device, device_id_type=MESH
    )


class Sum:
    def __init__(self, place, own, from_core, from_chips, total, from_floors, done, sems):
        self.p, self.own, self.from_core, self.from_chips = place, own, from_core, from_chips
        self.total, self.from_floors, self.done = total, from_floors, done
        self.core_sems, self.chip_sems, self.floor_sems, self.last_sems = sems
        self.rows = done.shape[1] // place.copies

    def core_copy(self, t):
        other = 1 - self.p.core
        return remote(self.own(t, pl.ds(0, FSDP // 2), other), self.from_core.at[t], self.core_sems, t, self.p.peer(1))

    def chip_copy(self, t, k):
        src = self.own(t, self.p.chip ^ k, self.p.core)
        return remote(src, self.from_chips.at[t, k - 1], self.chip_sems, (t, k - 1), self.p.peer(2 * k))

    def piece(self, floor):
        return pl.ds(multiple(floor, self.rows), self.rows)

    def floor_copy(self, t, d):
        device = self.p.floor(d)
        src = self.total.at[t, self.piece(device[0])]
        return remote(src, self.from_floors.at[t, d - 1], self.floor_sems, (t, d - 1), device)

    def last_copy(self, t, d):
        mine = self.done.at[t, self.piece(self.p.z)]
        return remote(mine, mine, self.last_sems, (t, d - 1), self.p.floor(d))

    def last_arrival(self, t, d):
        source = lax.rem(self.p.z + self.p.copies - d, self.p.copies)
        theirs = self.done.at[t, self.piece(source)]
        return remote(theirs, theirs, self.last_sems, (t, d - 1), self.p.floor(d))

    def offsets(self):
        return range(1, self.p.copies)

    def start(self, t):
        self.core_copy(t).start()

    def to_chips(self, t):
        self.core_copy(t).wait_recv()
        for k in (3, 1, 2, 0):
            at = self.p.chip ^ k
            view = self.own(t, at, self.p.core)
            view[...] = (view[...].astype(F32) + self.from_core[t, at].astype(F32)).astype(BF16)
            if k:
                self.chip_copy(t, k).start()

    def to_floors(self, t):
        total = self.own(t, self.p.chip, self.p.core)[...].astype(F32)
        for k in (1, 2, 3):
            self.chip_copy(t, k).wait_recv()
            total = total + self.from_chips[t, k - 1].astype(F32)
        self.total[t] = total.astype(BF16)
        for d in self.offsets():
            self.floor_copy(t, d).start()

    def to_all(self, t):
        mine = self.piece(self.p.z)
        total = self.total[t, mine, :].astype(F32)
        for d in self.offsets():
            self.floor_copy(t, d).wait_recv()
            total = total + self.from_floors[t, d - 1].astype(F32)
        self.done[t, mine, :] = total.astype(BF16)
        for d in self.offsets():
            self.last_copy(t, d).start()

    def finish(self, t):
        for d in self.offsets():
            self.last_arrival(t, d).wait_recv()

    def sent(self, t):
        self.core_copy(t).wait_send()
        for k in (1, 2, 3):
            self.chip_copy(t, k).wait_send()
        for d in self.offsets():
            self.floor_copy(t, d).wait_send()
            self.last_copy(t, d).wait_send()


class Gather:
    def __init__(self, R, place):
        self.R, self.p = R, place
        self.deep, self.tall = R.we_in.shape[0], R.wc_in.shape[0]

    def view(self, part, owner):
        if part == 1:
            return self.R.wc.at[pl.ds(multiple(owner, self.tall), self.tall), :]
        cols = slice(0, FIRST) if part == 0 else slice(FIRST, None)
        return self.R.we.at[pl.ds(multiple(owner, self.deep), self.deep), cols]

    def copy(self, part, mask, target):
        view = self.view(part, self.p.f ^ mask)
        return pltpu.make_async_remote_copy(
            src_ref=view,
            dst_ref=view,
            send_sem=self.R.gather_send.at[part, mask, target >> 1],
            recv_sem=self.R.gather_recv.at[part, mask ^ target],
            device_id=self.p.peer(target),
            device_id_type=MESH,
        )

    def arrival(self, part, mask):
        view = self.view(part, self.p.f ^ mask)
        return pltpu.make_async_remote_copy(
            src_ref=view,
            dst_ref=view,
            send_sem=self.R.gather_send.at[part, 0, 0],
            recv_sem=self.R.gather_recv.at[part, mask],
            device_id=self.p.peer(1),
            device_id_type=MESH,
        )

    def start(self):
        R, p = self.R, self.p
        R.we[pl.ds(multiple(p.f, self.deep), self.deep), :] = R.we_in[...]
        R.wc[pl.ds(multiple(p.f, self.tall), self.tall), :] = R.wc_in[...]
        for part in (0, 1, 2):
            for target in (6, 2, 4, 1):
                self.copy(part, 0, target).start()

    def pass_on(self, part):
        for mask in (2, 4, 6):
            self.arrival(part, mask).wait_recv()
            self.copy(part, mask, 1).start()

    def finish(self, part):
        for mask in (1, 3, 5, 7):
            self.arrival(part, mask).wait_recv()

    def sent(self):
        for part in (0, 1, 2):
            for target in (6, 2, 4, 1):
                self.copy(part, 0, target).wait_send()
            for mask in (2, 4, 6):
                self.copy(part, mask, 1).wait_send()


def interleave(first, second):
    low = lax.broadcasted_iota(jnp.int32, first.shape, 1) < BS
    return (
        jnp.where(low, first, pltpu.roll(second, BS, 1)),
        jnp.where(low, pltpu.roll(first, BS, 1), second),
    )


def pack_small(R):
    R.small[pl.ds(0, BS), :] = R.inner_in[...]
    R.small[pl.ds(BS, BS), :] = R.outer_in[...]

    def row(*refs):
        return jnp.concatenate([ref[...].astype(F32) for ref in refs], axis=1)

    none = jnp.zeros((1, BS), F32)
    rows = [
        row(R.fg_in, R.fs_in), R.ib_in[...].astype(F32), R.ob_in[...].astype(F32), row(R.gg_in, R.gs_in),
        jnp.concatenate([R.cb_in[...].astype(F32), none], axis=1),
        R.eb_in[:, :128].astype(F32), R.eb_in[:, 128:].astype(F32), jnp.zeros((9, 128), F32),
    ]
    R.small[pl.ds(2 * BS, 16), :] = jnp.concatenate(rows, axis=0).astype(BF16)


def unpack_small(R):
    for j in range(PAIRS):
        cols = slice(128 * j, 128 * j + 128)
        even = R.smalls[2 * j, pl.ds(2 * BS, 16), :].astype(F32)
        odd = R.smalls[2 * j + 1, pl.ds(2 * BS, 16), :].astype(F32)
        first, second = interleave(even, odd)
        for row, (part, at) in enumerate(
            [(first, 0), (second, 0), (first, 1), (second, 1), (first, 2), (second, 2), (first, 3), (second, 3), (first, 4)]
        ):
            R.vec[row : row + 1, cols] = part[at : at + 1]
        for k, block in ((2 * j, even), (2 * j + 1, odd)):
            R.be[0:1, 256 * k : 256 * k + 128] = block[5:6]
            R.be[0:1, 256 * k + 128 : 256 * k + 256] = block[6:7]
    for first, out in ((0, R.win), (BS, R.wout)):
        complex_pairs(R.smalls.at[:, pl.ds(first, BS), :], out)


def pack_sums(R):
    slots = R.tok.shape[0] // PATCHES

    def total(ref, at):
        return jnp.sum(ref[pl.ds(at, 8), :], axis=0, keepdims=True)

    feed_gain, feed_shift, contract, gain, shift = [total(R.sums, 8 * i) for i in range(5)]
    outer, inner, expand = total(R.dbias, 0), total(R.dbias, 8), total(R.dbe, 0)
    lane = lax.broadcasted_iota(jnp.int32, (1, 128), 1)
    facts = jnp.zeros((1, 128), F32)
    for i in range(5):
        facts = jnp.where(lane == i, jnp.sum(total(R.stats, 8 * i), axis=1, keepdims=True), facts)
    valid = jnp.zeros((1, 128), F32)
    for slot in range(slots):
        kind = kind_of(R, slot, 128)
        valid = valid + jnp.where(kind == 0, 4, kind).astype(F32) * float(PATCHES // 4 * WIDTH)
    facts = jnp.where(lane == 5, valid, facts)
    none = jnp.zeros((1, 128), F32)
    for j in range(PAIRS):
        cols = slice(128 * j, 128 * j + 128)
        real, imag = slice(256 * j, 256 * j + 128), slice(256 * j + 128, 256 * j + 256)
        rows = [
            interleave(gain[:, cols], shift[:, cols]),
            interleave(inner[:, real], inner[:, imag]),
            interleave(outer[:, real], outer[:, imag]),
            interleave(feed_gain[:, cols], feed_shift[:, cols]),
            interleave(contract[:, cols], none),
        ]
        for side in range(2):
            k = 2 * j + side
            R.vec_own[k] = jnp.concatenate(
                [row[side] for row in rows]
                + [expand[:, 256 * k : 256 * k + 128], expand[:, 256 * k + 128 : 256 * k + 256], facts],
                axis=0,
            )


class Share:
    def __init__(self, place, own, arrived, floors, sems):
        self.p, self.own, self.arrived, self.floors = place, own, arrived, floors
        self.peer_sems, self.floor_sems = sems

    def peer_copy(self, k):
        return remote(self.own.at[self.p.f ^ k], self.arrived.at[k - 1], self.peer_sems, k - 1, self.p.peer(k))

    def floor_copy(self, d):
        mine = self.floors.at[self.p.z]
        return remote(mine, mine, self.floor_sems, d - 1, self.p.floor(d))

    def floor_arrival(self, d):
        theirs = self.floors.at[lax.rem(self.p.z + self.p.copies - d, self.p.copies)]
        return remote(theirs, theirs, self.floor_sems, d - 1, self.p.floor(d))

    def start(self):
        for k in (6, 7, 2, 4, 3, 5, 1):
            self.peer_copy(k).start()

    def to_floors(self):
        total = self.own[self.p.f].astype(F32)
        for k in range(1, FSDP):
            self.peer_copy(k).wait_recv()
            total = total + self.arrived[k - 1].astype(F32)
        self.floors[self.p.z] = total.astype(self.floors.dtype)
        for d in range(1, self.p.copies):
            self.floor_copy(d).start()

    def finish(self):
        for d in range(1, self.p.copies):
            self.floor_arrival(d).wait_recv()
        total = self.floors[0].astype(F32)
        for z in range(1, self.p.copies):
            total = total + self.floors[z].astype(F32)
        return total

    def sent(self):
        for k in range(1, FSDP):
            self.peer_copy(k).wait_send()
        for d in range(1, self.p.copies):
            self.floor_copy(d).wait_send()


def layer(copies, R):
    p = Place(copies)
    n = R.tok.shape[0]
    slots = n // PATCHES
    hidden_all = R.we.shape[1]
    chunks = hidden_all // CHUNK
    blocks = n // CHUNK

    def slot_rows(slot):
        return pl.ds(multiple(slot, PATCHES), PATCHES)

    def load(which, slot):
        src, dst = ((R.tok_in, R.tok), (R.cot_in, R.msk))[which]
        rows = slot_rows(slot)
        return pltpu.make_async_copy(src.at[rows, :], dst.at[rows, :], R.load_sems.at[which, slot])

    def store(which, slot):
        src, dst = ((R.feed, R.out_ref), (R.fg, R.grad_ref))[which]
        rows = slot_rows(slot)
        return pltpu.make_async_copy(src.at[rows, :], dst.at[rows, :], R.store_sems.at[which, slot])

    @pl.loop(0, slots)
    def _(slot):
        load(0, slot).start()
        load(1, slot).start()

    barrier = pltpu.get_barrier_semaphore()
    for k in range(1, FSDP):
        pl.semaphore_signal(barrier, inc=1, device_id=p.peer(k), device_id_type=MESH)
    for d in range(1, copies):
        pl.semaphore_signal(barrier, inc=1, device_id=p.floor(d), device_id_type=MESH)
    pack_small(R)
    pl.semaphore_wait(barrier, FSDP - 1 + copies - 1)

    def small_copy(k):
        return remote(R.small, R.smalls.at[p.f], (R.small_send, R.small_recv), k - 1, p.peer(k))

    def small_arrival(k):
        return remote(R.small, R.smalls.at[p.f ^ k], (R.small_send, R.small_recv), k - 1, p.peer(k))

    for k in (6, 7, 2, 4, 3, 5, 1):
        small_copy(k).start()
    gather = Gather(R, p)
    gather.start()
    R.smalls[p.f] = R.small[...]
    R.stats[...] = jnp.zeros_like(R.stats)
    R.sums[...] = jnp.zeros_like(R.sums)
    R.dbias[...] = jnp.zeros_like(R.dbias)
    R.dbe[...] = jnp.zeros_like(R.dbe)
    for k in range(1, FSDP):
        small_arrival(k).wait_recv()
    unpack_small(R)

    @pl.loop(0, slots)
    def _(slot):
        load(0, slot).wait()
        load(1, slot).wait()
        mixer_forward(R, slot)
        rows = slot_rows(slot)
        R.br[rows, :] = jnp.zeros((PATCHES, WIDTH), F32)
        R.fg[rows, :] = jnp.zeros((PATCHES, WIDTH), F32)

        @pl.when(slot == slots // 2)
        def _():
            gather.pass_on(0)

    gather.pass_on(1)
    gather.finish(0)
    gather.finish(1)

    expand = Sum(
        p, lambda t, chips, core: R.ew_own.at[t, chips, core], R.ew_core, R.ew_chips, R.ew_total, R.ew_floors, R.ew_done,
        ((R.ew_s0, R.ew_r0), (R.ew_s1, R.ew_r1), (R.ew_s2, R.ew_r2), (R.ew_s3, R.ew_r3)),
    )

    @pl.loop(0, chunks)
    def _(t):
        cols = pl.ds(multiple(t, CHUNK), CHUNK)

        @pl.loop(0, blocks)
        def _(i):
            @pl.when((t > 0) & (i == 1))
            def _():
                expand.to_chips(t - 1)

            @pl.when((t > 0) & (i == 3))
            def _():
                expand.to_floors(t - 1)

            @pl.when((t > 1) & (i == 1))
            def _():
                expand.to_all(t - 2)

            mlp_chunk(R, i, cols, False)

            @pl.when((t == 0) & (i == 1))
            def _():
                gather.pass_on(2)

        @pl.when(t == 0)
        def _():
            gather.finish(2)

        piece = dot(R.feed[...], R.hgrad[...].reshape(-1, CHUNK), TN).astype(BF16)
        for k in range(FSDP):
            R.ew_own[t, k // 2, k % 2] = piece[k * BS : (k + 1) * BS]
        expand.start(t)

    deep, tall = R.cw_done.shape[1:]

    def contract_view(t, chips, core):
        lanes = pl.ds(multiple(core, tall), tall)
        if isinstance(chips, pl.Slice):
            return R.hgrad.at[pl.ds(t * (FSDP // 2), FSDP // 2), :, lanes]
        return R.hgrad.at[t * (FSDP // 2) + chips, :, lanes]

    contract = Sum(
        p, contract_view, R.cw_core, R.cw_chips, R.cw_total, R.cw_floors, R.cw_done,
        ((R.cw_s0, R.cw_r0), (R.cw_s1, R.cw_r1), (R.cw_s2, R.cw_r2), (R.cw_s3, R.cw_r3)),
    )
    @pl.loop(0, 2)
    def _(t):
        @pl.loop(0, FSDP // 2)
        def _(chip):
            cols = pl.ds(multiple(chip, 2 * tall), 2 * tall)
            piece = dot(R.msk[:, pl.ds(multiple(t, deep), deep)], R.hidden[:, cols], TN).astype(BF16)
            R.hgrad[t * (FSDP // 2) + chip] = piece

        contract.start(t)

        @pl.when(t == 0)
        def _():
            expand.to_chips(chunks - 1)
            expand.to_all(chunks - 2)

        @pl.when(t == 1)
        def _():
            contract.to_chips(0)

    contract.to_chips(1)

    @pl.loop(0, slots)
    def _(slot):
        mixer_backward_first(R, slot)
        store(0, slot).start()

        @pl.when(slot == 1)
        def _():
            expand.to_floors(chunks - 1)

        @pl.when(slot == 3)
        def _():
            contract.to_floors(0)
            expand.to_all(chunks - 1)

        @pl.when(slot == 6)
        def _():
            contract.to_floors(1)
            contract.to_all(0)

    def put_inner(j, value):
        for side in range(2):
            R.mix_own[2 * j + side, pl.ds(0, BS), :] = value[side * BS : (side + 1) * BS].astype(BF16)

    def put_outer(j, value):
        for side in range(2):
            R.mix_own[2 * j + side, pl.ds(BS, BS), :] = value[side * BS : (side + 1) * BS].astype(BF16)

    mixer_weight_gradients(R, put_inner, put_outer)
    mixing = Share(p, R.mix_own, R.mix_peers, R.mix_floors, ((R.mix_s0, R.mix_r0), (R.mix_s1, R.mix_r1)))
    mixing.start()

    def put(slot, rows, value):
        R.fg[rows, :] = value
        store(1, slot).start()

    @pl.loop(0, slots)
    def _(slot):
        mixer_backward_second(R, slot, put)

        @pl.when(slot == 4)
        def _():
            contract.to_all(1)
            mixing.to_floors()

    pack_sums(R)
    vectors = Share(p, R.vec_own, R.vec_peers, R.vec_floors, ((R.vec_s0, R.vec_r0), (R.vec_s1, R.vec_r1)))
    vectors.start()
    for t in range(chunks):
        expand.finish(t)
        R.ew_ref[:, t * CHUNK : (t + 1) * CHUNK] = R.ew_done[t].astype(F32)
    for t in range(2):
        contract.finish(t)
        R.cw_ref[:, t * deep : (t + 1) * deep] = jnp.transpose(R.cw_done[t].astype(F32))
    R.mix_ref[...] = mixing.finish()
    vectors.to_floors()
    R.vec_ref[...] = vectors.finish()
    gather.sent()
    for k in range(1, FSDP):
        small_copy(k).wait_send()

    @pl.loop(0, chunks)
    def _(t):
        expand.sent(t)

    @pl.loop(0, 2)
    def _(t):
        contract.sent(t)

    mixing.sent()
    vectors.sent()

    @pl.loop(0, slots)
    def _(slot):
        store(0, slot).wait()
        store(1, slot).wait()


def body_in_one(
    copies, tokens, cotangent, slot_items, filter_gain, filter_shift, inner_weight, inner_bias, outer_weight, outer_bias,
    feed_gain, feed_shift, expand_weight, expand_bias, contract_weight, contract_bias,
):
    slots = tokens.shape[0]
    n = slots * PATCHES
    deep, hidden = expand_weight.shape
    tall = contract_weight.shape[0]
    chunks = hidden // CHUNK
    floors = copies - 1
    ins = dict(
        items=slot_items, tok_in=tokens.reshape(n, WIDTH), cot_in=cotangent.reshape(n, WIDTH), table=jnp.asarray(TABLES, BF16),
        inner_in=inner_weight, outer_in=outer_weight, we_in=expand_weight, wc_in=contract_weight,
        fg_in=filter_gain[None], fs_in=filter_shift[None], ib_in=inner_bias[None], ob_in=outer_bias[None],
        gg_in=feed_gain[None], gs_in=feed_shift[None], cb_in=contract_bias[None], eb_in=expand_bias[None],
    )
    in_specs = [{"items": SMEM, "tok_in": ANY, "cot_in": ANY}.get(key, VMEM) for key in ins]
    outs = dict(
        out_ref=((n, WIDTH), BF16), grad_ref=((n, WIDTH), F32), ew_ref=((deep, hidden), F32), cw_ref=((tall, WIDTH), F32),
        mix_ref=((2 * BS, 2 * BS), F32), vec_ref=((8, 128), F32),
    )
    out_specs = [{"out_ref": ANY, "grad_ref": ANY}.get(key, VMEM) for key in outs]
    wide, flat, full = ((n, 2 * WIDTH), BF16), ((n, WIDTH), BF16), ((n, WIDTH), F32)
    pairs, sums = ((2 * WIDTH, 4 * BS), BF16), ((40, WIDTH), F32)
    memory = dict(
        tok=flat, msk=flat, spec=wide, act=wide, slope=wide, bent=wide, mid=full, feed=flat, br=full, fg=full,
        hidden=((n, hidden), BF16), hgrad=((n // PATCHES, PATCHES, CHUNK), BF16), we=((WIDTH, hidden), BF16), wc=((hidden, WIDTH), BF16),
        win=pairs, wout=pairs, vec=((16, WIDTH), F32), be=((8, hidden), F32), stats=sums, sums=sums,
        dbias=((16, 2 * WIDTH), F32), dbe=((8, hidden), F32),
        small=((144, 128), BF16), smalls=((FSDP, 144, 128), BF16),
        ew_own=((chunks, 4, 2, deep, CHUNK), BF16), ew_core=((chunks, 4, deep, CHUNK), BF16),
        ew_chips=((chunks, 3, deep, CHUNK), BF16), ew_total=((chunks, deep, CHUNK), BF16),
        ew_floors=((chunks, floors, deep // copies, CHUNK), BF16), ew_done=((chunks, deep, CHUNK), BF16),
        cw_core=((2, 4, WIDTH // 2, tall), BF16),
        cw_chips=((2, 3, WIDTH // 2, tall), BF16), cw_total=((2, WIDTH // 2, tall), BF16),
        cw_floors=((2, floors, WIDTH // 2 // copies, tall), BF16), cw_done=((2, WIDTH // 2, tall), BF16),
        mix_own=((FSDP, 128, 128), BF16), mix_peers=((FSDP - 1, 128, 128), BF16), mix_floors=((copies, 128, 128), BF16),
        vec_own=((FSDP, 8, 128), F32), vec_peers=((FSDP - 1, 8, 128), F32), vec_floors=((copies, 8, 128), F32),
    )
    sems = dict(
        load_sems=(2, slots), store_sems=(2, slots), small_send=(7,), small_recv=(7,),
        gather_send=(3, 8, 4), gather_recv=(3, 8),
    )
    for key, parts in (("ew", chunks), ("cw", 2)):
        for step, shape in enumerate(((parts,), (parts, 3), (parts, floors), (parts, floors))):
            sems[f"{key}_s{step}"] = sems[f"{key}_r{step}"] = shape
    for key in ("mix", "vec"):
        for step, shape in enumerate(((FSDP - 1,), (floors,))):
            sems[f"{key}_s{step}"] = sems[f"{key}_r{step}"] = shape
    names = list(ins) + list(outs) + list(memory) + list(sems)

    def kernel(*refs):
        R = named(names, refs)
        R.mgrad, R.out, R.ograd, R.igrad, R.cot = R.fg, R.feed, R.bent, R.slope, R.msk
        layer(copies, R)

    o = dict(
        zip(
            outs,
            pl.pallas_call(
                kernel,
                out_shape=[jax.ShapeDtypeStruct(*spec) for spec in outs.values()],
                in_specs=in_specs,
                out_specs=out_specs,
                scratch_shapes=[pltpu.VMEM(*spec) for spec in memory.values()]
                + [pltpu.SemaphoreType.DMA(shape) for shape in sems.values()],
                compiler_params=pltpu.CompilerParams(vmem_limit_bytes=ROOM, collective_id=0, has_side_effects=True),
                name="mega",
            )(*ins.values()),
        )
    )
    vec = o["vec_ref"]
    return (
        o["out_ref"].reshape(tokens.shape), o["grad_ref"].reshape(tokens.shape), vec[0, :BS], vec[0, BS:], o["mix_ref"][:BS],
        vec[1], o["mix_ref"][BS:], vec[2], vec[3, :BS], vec[3, BS:], o["ew_ref"], vec[5:7].reshape(-1), o["cw_ref"],
        vec[4, :BS], jnp.sqrt(vec[7, :5] / vec[7, 5]),
    )


def solution(mesh):
    ins, outs = specs()
    whole = body_by_collectives
    if mesh.shape["fsdp"] == FSDP and mesh.shape["rep"] in (2, 4):
        whole = functools.partial(body_in_one, mesh.shape["rep"])
    return jax.shard_map(whole, mesh=mesh, in_specs=ins, out_specs=outs, check_vma=False)
```

```python
import functools
import math

import jax
import jax.numpy as jnp
import numpy as np
from jax import lax
from jax.experimental import pallas as pl
from jax.experimental.pallas import tpu as pltpu
from jax.sharding import PartitionSpec as P

BS = 64
NB = 8
SIDE = 16
PATCHES = SIDE * SIDE
WIDTH = NB * BS
HALF = PATCHES // 2
PAIRS = NB // 2
CHUNK = 512
EPSILON = 1e-05
SHRINK = 0.25
F32 = jnp.float32
BF16 = jnp.bfloat16
NT = (((1,), (1,)), ((), ()))
TN = (((0,), (0,)), ((), ()))
TABLE_SCALE = 1.132805


def frequency_order(side):
    pairs, selfs = [], []
    for a in range(side):
        for b in range(side):
            other = ((-a) % side, (-b) % side)
            if other == (a, b):
                selfs.append((a, b))
            elif (a, b) < other:
                pairs.append((a, b))
    return pairs, selfs


def spectrum_table(side):
    tiles = SIDE // side
    pairs, selfs = frequency_order(side)
    row = np.arange(PATCHES) // SIDE
    col = np.arange(PATCHES) % SIDE
    top, bottom = [], []
    for kind in ("pair", "self"):
        for qr in range(tiles):
            for qc in range(tiles):
                inside = (row // side == qr) & (col // side == qc)
                listed = pairs if kind == "pair" else selfs
                for at, (a, b) in enumerate(listed):
                    angle = 2.0 * math.pi / side * ((a * row + b * col) % side)
                    if kind == "pair":
                        top.append(np.where(inside, np.cos(angle), 0.0) / side)
                        bottom.append(np.where(inside, -np.sin(angle), 0.0) / side)
    extra = []
    for at in range(len(selfs)):
        for qr in range(tiles):
            for qc in range(tiles):
                inside = (row // side == qr) & (col // side == qc)
                a, b = selfs[at]
                angle = 2.0 * math.pi / side * ((a * row + b * col) % side)
                extra.append(np.where(inside, np.cos(angle), 0.0) / side)
    half = len(extra) // 2
    return np.array(top + extra[:half] + bottom + extra[half:]), len(top), tiles * tiles


WHOLE_TABLE, WHOLE_PAIRS, WHOLE_ZEROS = spectrum_table(SIDE)
PART_TABLE, PART_PAIRS, PART_ZEROS = spectrum_table(SIDE // 2)
TABLES = np.concatenate([WHOLE_TABLE * TABLE_SCALE, PART_TABLE], axis=0)


def dot(a, b, dims=(((1,), (0,)), ((), ()))):
    return lax.dot_general(a, b, dims, preferred_element_type=F32)


def sum8(values):
    return jnp.sum(values.reshape(-1, 8, values.shape[-1]), axis=0)


def gelu_and_slope(v):
    phi = 0.5 * lax.erf(v * 0.7071067811865476) + 0.5
    bell = jnp.exp2(v * v * (-0.5 / math.log(2.0))) * (1.0 / math.sqrt(2.0 * math.pi))
    return v * phi, phi + v * bell


def row_stats(values):
    centre = values - jnp.mean(values, axis=-1, keepdims=True)
    scale = lax.rsqrt(jnp.mean(centre * centre, axis=-1, keepdims=True) + EPSILON)
    return centre * scale, scale


def kind_of(R, slot, lanes=WIDTH):
    return jnp.full((1, lanes), R.items[slot], jnp.int32)


def slot_facts(kind):
    whole = kind == 0
    pairs = jnp.where(whole, WHOLE_PAIRS, PART_PAIRS)
    scale = jnp.where(whole, 1.0 / TABLE_SCALE, 1.0).astype(F32)
    return whole, pairs, scale


def table_of(R, kind):
    whole = jnp.where(kind[:, :PATCHES] == 0, 1.0, 0.0).astype(F32)
    first, second = whole.astype(BF16), (1.0 - whole).astype(BF16)
    return R.table[pl.ds(0, PATCHES), :] * first + R.table[pl.ds(PATCHES, PATCHES), :] * second


def spread(halves, pairs):
    top, bottom = halves[:HALF], halves[HALF:]
    is_pair = lax.broadcasted_iota(jnp.int32, top.shape, 0) < pairs[:, : top.shape[1]]
    imag = jnp.where(is_pair, bottom, 0.0)
    return top, imag, jnp.where(is_pair, top, bottom), -imag


def fold(block, pairs):
    ra, ia = block[:HALF, :128], block[:HALF, 128:]
    rb, ib = block[HALF:, :128], block[HALF:, 128:]
    is_pair = lax.broadcasted_iota(jnp.int32, ra.shape, 0) < pairs[:, : ra.shape[1]]
    return ra + jnp.where(is_pair, rb, 0.0), jnp.where(is_pair, ia - ib, rb)


def interleave(first, second):
    low = lax.broadcasted_iota(jnp.int32, first.shape, 1) < BS
    return (
        jnp.where(low, first, pltpu.roll(second, BS, 1)),
        jnp.where(low, pltpu.roll(first, BS, 1), second),
    )


def complex_pairs(weight_ref, out_ref):
    low = lax.broadcasted_iota(jnp.int32, (BS, 128), 1) < BS
    for j in range(PAIRS):
        first, second = weight_ref[2 * j].astype(F32), weight_ref[2 * j + 1].astype(F32)
        real = jnp.concatenate([jnp.where(low, first, 0.0), jnp.where(low, 0.0, pltpu.roll(second, BS, 1))], axis=0)
        imag = jnp.concatenate([jnp.where(low, pltpu.roll(first, BS, 1), 0.0), jnp.where(low, 0.0, second)], axis=0)
        out_ref[pl.ds(256 * j, 256), :] = jnp.concatenate(
            [jnp.concatenate([real, imag], axis=1), jnp.concatenate([-imag, real], axis=1)], axis=0
        ).astype(BF16)


def pair_gradient(product):
    real = product[:128, :128] + product[128:, 128:]
    imag = product[:128, 128:] - product[128:, :128]
    low = lax.broadcasted_iota(jnp.int32, (BS, 128), 1) < BS
    first = jnp.where(low, real[:BS], pltpu.roll(imag[:BS], BS, 1))
    second = jnp.where(low, pltpu.roll(real[BS:], BS, 1), imag[BS:])
    return jnp.concatenate([first, second], axis=0)


def masked_squares(values, kind):
    squares = values * values
    parts = jnp.sum(squares.reshape(2, 8, 2, 8, squares.shape[-1]), axis=1)
    total = parts[0, 0]
    for q in range(1, 4):
        valid = jnp.where((kind == 0) | (q < kind), 1.0, 0.0).astype(F32)
        total = total + valid * parts[q // 2, q % 2]
    return total


def masked(values, kind):
    position = lax.broadcasted_iota(jnp.int32, values.shape, 0)
    quadrant = (position >> 7) * 2 + ((position >> 3) & 1)
    return jnp.where((kind == 0) | (quadrant < kind), values, 0.0)


def mixer_start(R, slot):
    kind = kind_of(R, slot)
    whole, pairs, scale = slot_facts(kind)
    rows = pl.ds(pl.multiple_of(slot * PATCHES, PATCHES), PATCHES)
    x = R.tok[rows, :].astype(F32)
    xhat, _ = row_stats(x)
    R.stats[pl.ds(0, 8), :] += masked_squares(x, kind)
    R.mid[rows, :] = dot(table_of(R, kind), xhat.astype(BF16))
    grad = masked(R.cot[rows, :].astype(F32), kind)
    R.sums[pl.ds(16, 8), :] += sum8(grad)
    R.msk[rows, :] = grad.astype(BF16)


def mixer_forward(R, slot):
    kind = kind_of(R, slot)
    whole, pairs, scale = slot_facts(kind)
    rows = pl.ds(pl.multiple_of(slot * PATCHES, PATCHES), PATCHES)
    spec = R.mid[rows, :] * (R.vec[0:1, :] * scale)
    top = lax.broadcasted_iota(jnp.int32, (HALF, WIDTH), 0)
    at_zero = (top >= pairs) & (top < pairs + jnp.where(whole, WHOLE_ZEROS, PART_ZEROS))
    shift = R.vec[1:2, :] * jnp.where(whole, float(SIDE), float(SIDE // 2)).astype(F32)
    spec = jnp.concatenate([spec[:HALF] + jnp.where(at_zero, shift, 0.0), spec[HALF:]], axis=0)
    ra, ia, rb, ib = [part.astype(BF16) for part in spread(spec, pairs)]
    tops, bottoms = [], []
    for j in range(PAIRS):
        lanes = slice(256 * j, 256 * j + 256)
        cols = slice(128 * j, 128 * j + 128)
        low = jnp.concatenate(
            [
                jnp.concatenate([ra[:, cols], ia[:, cols]], axis=1),
                jnp.concatenate([rb[:, cols], ib[:, cols]], axis=1),
            ],
            axis=0,
        )
        R.spec[rows, lanes] = low
        pre = dot(low, R.win[pl.ds(256 * j, 256), :]) + jnp.concatenate([R.vec[2:3, cols], R.vec[3:4, cols]], axis=1)
        act, slope = gelu_and_slope(pre)
        act = act.astype(BF16)
        R.act[rows, lanes] = act
        R.slope[rows, lanes] = slope.astype(BF16)
        post = dot(act, R.wout[pl.ds(256 * j, 256), :]) + jnp.concatenate(
            [R.vec[4:5, cols], R.vec[5:6, cols]], axis=1
        )
        bent = jnp.tanh(post * (1.0 / SHRINK))
        R.bent[rows, lanes] = (bent * bent).astype(BF16)
        u, v = fold(post - SHRINK * bent, pairs)
        tops.append(u.astype(BF16))
        bottoms.append(v.astype(BF16))
    folded = jnp.concatenate([jnp.concatenate(tops, axis=1), jnp.concatenate(bottoms, axis=1)], axis=0)
    mixer_out = dot(table_of(R, kind), folded, TN) * scale
    R.stats[pl.ds(8, 8), :] += masked_squares(mixer_out, kind)
    middle = R.tok[rows, :].astype(F32) + mixer_out
    R.stats[pl.ds(16, 8), :] += masked_squares(middle, kind)
    R.mid[rows, :] = middle
    yhat, _ = row_stats(middle)
    R.feed[rows, :] = (yhat * R.vec[6:7, :] + R.vec[7:8, :]).astype(BF16)


def mlp_front(R, i, cols, we, wc):
    rows = pl.ds(pl.multiple_of(i * CHUNK, CHUNK), CHUNK)
    hidden, slope = gelu_and_slope(dot(R.feed[rows, :], we) + R.be[0:1, cols])
    hidden = hidden.astype(BF16)
    R.hidden[rows, :] = hidden
    back = dot(R.msk[rows, :], wc, NT) * slope
    R.dbe[:, cols] += sum8(back)
    back = back.astype(BF16)
    R.hgrad[rows, :] = back
    return rows, hidden, back


def mlp_back(R, rows, hidden, back, we, wc):
    R.br[rows, :] += dot(hidden, wc)
    R.fg[rows, :] += dot(back, we, NT)


def mlp_chunk(R, i, cols, we, wc):
    rows, hidden, back = mlp_front(R, i, cols, we, wc)
    mlp_back(R, rows, hidden, back, we, wc)


def mixer_backward_first(R, slot):
    kind = kind_of(R, slot)
    whole, pairs, scale = slot_facts(kind)
    rows = pl.ds(pl.multiple_of(slot * PATCHES, PATCHES), PATCHES)
    table = table_of(R, kind)
    branch = R.br[rows, :] + R.vec[8:9, :]
    middle = R.mid[rows, :]
    result = middle + branch
    R.stats[pl.ds(24, 8), :] += masked_squares(branch, kind)
    R.stats[pl.ds(32, 8), :] += masked_squares(result, kind)
    R.out[rows, :] = result.astype(BF16)
    feed_grad = R.fg[rows, :]
    yhat, yscale = row_stats(middle)
    R.sums[pl.ds(0, 8), :] += sum8(feed_grad * yhat)
    R.sums[pl.ds(8, 8), :] += sum8(feed_grad)
    scaled = feed_grad * R.vec[6:7, :]
    inner = scaled - jnp.mean(scaled, axis=-1, keepdims=True) - yhat * jnp.mean(scaled * yhat, axis=-1, keepdims=True)
    mgrad = R.msk[rows, :].astype(F32) + inner * yscale
    R.mgrad[rows, :] = mgrad
    parts = spread(dot(table, mgrad.astype(BF16)) * scale, pairs)
    for j in range(PAIRS):
        lanes = slice(256 * j, 256 * j + 256)
        cols = slice(128 * j, 128 * j + 128)
        ra, ia, rb, ib = [part[:, cols] for part in parts]
        grad = jnp.concatenate([jnp.concatenate([ra, ia], axis=1), jnp.concatenate([rb, ib], axis=1)], axis=0)
        grad = (grad * R.bent[rows, lanes].astype(F32)).astype(BF16)
        R.ograd[rows, lanes] = grad
        R.dbias[pl.ds(0, 8), lanes] += sum8(grad.astype(F32))
        grad = dot(grad, R.wout[pl.ds(256 * j, 256), :], NT) * R.slope[rows, lanes].astype(F32)
        grad = grad.astype(BF16)
        R.igrad[rows, lanes] = grad
        R.dbias[pl.ds(8, 8), lanes] += sum8(grad.astype(F32))


def mixer_weight_gradients(R, put_inner, put_outer):
    for j in range(PAIRS):
        lanes = slice(256 * j, 256 * j + 256)
        put_outer(j, pair_gradient(dot(R.act[:, lanes], R.ograd[:, lanes], TN)))
        put_inner(j, pair_gradient(dot(R.spec[:, lanes], R.igrad[:, lanes], TN)))


def mixer_backward_second(R, slot, put):
    kind = kind_of(R, slot)
    whole, pairs, scale = slot_facts(kind)
    rows = pl.ds(pl.multiple_of(slot * PATCHES, PATCHES), PATCHES)
    table = table_of(R, kind)
    tops, bottoms = [], []
    for j in range(PAIRS):
        lanes = slice(256 * j, 256 * j + 256)
        u, v = fold(dot(R.igrad[rows, lanes], R.win[pl.ds(256 * j, 256), :], NT), pairs)
        tops.append(u.astype(BF16))
        bottoms.append(v.astype(BF16))
    folded = jnp.concatenate([jnp.concatenate(tops, axis=1), jnp.concatenate(bottoms, axis=1)], axis=0)
    ngrad = dot(table, folded, TN) * scale
    xhat, xscale = row_stats(R.tok[rows, :].astype(F32))
    R.sums[pl.ds(24, 8), :] += sum8(ngrad * xhat)
    R.sums[pl.ds(32, 8), :] += sum8(ngrad)
    scaled = ngrad * R.vec[0:1, :]
    inner = scaled - jnp.mean(scaled, axis=-1, keepdims=True) - xhat * jnp.mean(scaled * xhat, axis=-1, keepdims=True)
    put(slot, rows, R.mgrad[rows, :] + inner * xscale)

class Refs:
    pass


VMEM = pl.BlockSpec(memory_space=pltpu.VMEM)
SMEM = pl.BlockSpec(memory_space=pltpu.SMEM)
ROOM = 127 * 2**19


def named(names, refs):
    R = Refs()
    for name, ref in zip(names, refs):
        setattr(R, name, ref)
    return R


def plain_call(body, ins, outs, scratch, name):
    names = list(ins) + list(outs) + list(scratch)

    def kernel(*refs):
        body(named(names, refs))

    values = pl.pallas_call(
        kernel,
        out_shape=[jax.ShapeDtypeStruct(*spec) for spec in outs.values()],
        in_specs=[SMEM if key == "items" else VMEM for key in ins],
        out_specs=[VMEM for _ in outs],
        scratch_shapes=[pltpu.VMEM(*spec) for spec in scratch.values()],
        compiler_params=pltpu.CompilerParams(vmem_limit_bytes=ROOM),
        name=name,
    )(*ins.values())
    return dict(zip(outs, values))


def forward_body(R):
    complex_pairs(R.inner, R.win)
    complex_pairs(R.outer, R.wout)
    R.stats[...] = jnp.zeros_like(R.stats)
    R.sums[...] = jnp.zeros_like(R.sums)

    @pl.loop(0, R.tok.shape[0] // PATCHES)
    def _(slot):
        mixer_start(R, slot)
        mixer_forward(R, slot)


def mlp_body(R):
    R.dbe[...] = jnp.zeros_like(R.dbe)
    R.br[...] = jnp.zeros_like(R.br)
    R.fg[...] = jnp.zeros_like(R.fg)

    @pl.loop(0, R.we.shape[1] // CHUNK)
    def _(t):
        cols = pl.ds(pl.multiple_of(t * CHUNK, CHUNK), CHUNK)

        @pl.loop(0, R.feed.shape[0] // CHUNK)
        def _(i):
            mlp_chunk(R, i, cols, R.we[:, cols], R.wc[cols, :])

        R.dwe[:, cols] = dot(R.feed[...], R.hgrad[...], TN).astype(BF16)
        R.dwc[:, cols] = dot(R.msk[...], R.hidden[...], TN).astype(BF16)


def backward_body(R):
    R.stats[...] = jnp.zeros_like(R.stats)
    R.sums[...] = jnp.zeros_like(R.sums)
    R.dbias[...] = jnp.zeros_like(R.dbias)
    slots = R.tok.shape[0] // PATCHES

    @pl.loop(0, slots)
    def _(slot):
        mixer_backward_first(R, slot)

    def put_inner(j, value):
        R.dinner[pl.ds(128 * j, 128), :] = value

    def put_outer(j, value):
        R.douter[pl.ds(128 * j, 128), :] = value

    mixer_weight_gradients(R, put_inner, put_outer)

    def put(slot, rows, value):
        R.igrad_out[rows, :] = value

    @pl.loop(0, slots)
    def _(slot):
        mixer_backward_second(R, slot, put)


def pair_order(vector):
    parts = vector.reshape(NB, 2, BS)
    return parts[:, 0].reshape(1, WIDTH), parts[:, 1].reshape(1, WIDTH)


def body_by_collectives(
    tokens, cotangent, slot_items, filter_gain, filter_shift, inner_weight, inner_bias, outer_weight, outer_bias,
    feed_gain, feed_shift, expand_weight, expand_bias, contract_weight, contract_bias,
):
    def gather(x):
        return lax.all_gather(x, "fsdp", axis=0, tiled=True)

    vectors = (filter_gain, filter_shift, inner_bias, outer_bias, feed_gain, feed_shift, contract_bias, expand_bias)
    sizes = [v.shape[0] for v in vectors]
    packed = lax.all_gather(jnp.concatenate(vectors), "fsdp", axis=0)
    ends = np.cumsum([0] + sizes)
    g1, s1, bi, bo, g2, s2, bc, be = [packed[:, a:b].reshape(-1).astype(F32) for a, b in zip(ends, ends[1:])]
    vec = jnp.concatenate(
        [g1[None], s1[None], *pair_order(bi), *pair_order(bo), g2[None], s2[None], bc[None], jnp.zeros((7, WIDTH), F32)]
    )
    inner, outer, we, wc = gather(inner_weight), gather(outer_weight), gather(expand_weight), gather(contract_weight)
    n = tokens.shape[0] * PATCHES
    hidden = we.shape[1]
    tok, cot = tokens.reshape(n, WIDTH), cotangent.reshape(n, WIDTH)
    table = jnp.asarray(TABLES, BF16)
    wide = ((n, 2 * WIDTH), BF16)
    flat = ((n, WIDTH), BF16)
    full = ((n, WIDTH), F32)
    pairs = ((2 * WIDTH, 2 * 2 * BS), BF16)
    sums = ((40, WIDTH), F32)
    a = plain_call(
        forward_body,
        dict(items=slot_items, tok=tok, cot=cot, table=table, vec=vec, inner=inner.reshape(NB, BS, 2 * BS), outer=outer.reshape(NB, BS, 2 * BS)),
        dict(spec=wide, act=wide, slope=wide, bent=wide, mid=full, feed=flat, msk=flat, win=pairs, wout=pairs, stats=sums, sums=sums),
        {},
        "mixer_forward",
    )
    b = plain_call(
        mlp_body,
        dict(feed=a["feed"], msk=a["msk"], we=we, wc=wc, be=be.reshape(1, hidden)),
        dict(br=full, fg=full, dwe=((WIDTH, hidden), BF16), dwc=((WIDTH, hidden), BF16), dbe=((8, hidden), F32)),
        dict(hidden=((n, CHUNK), BF16), hgrad=((n, CHUNK), BF16)),
        "mlp",
    )
    c = plain_call(
        backward_body,
        dict(
            items=slot_items, tok=tok, table=table, vec=vec, spec=a["spec"], act=a["act"], slope=a["slope"], bent=a["bent"],
            mid=a["mid"], msk=a["msk"], br=b["br"], fg=b["fg"], win=a["win"], wout=a["wout"],
        ),
        dict(
            out=flat, igrad_out=full, dinner=((WIDTH, 2 * BS), F32), douter=((WIDTH, 2 * BS), F32),
            dbias=((16, 2 * WIDTH), F32), sums=sums, stats=sums,
        ),
        dict(mgrad=full, ograd=wide, igrad=wide),
        "mixer_backward",
    )

    def scatter(x):
        return lax.psum_scatter(x, "fsdp", scatter_dimension=0, tiled=True)

    def rows_of(x, at):
        return jnp.sum(x[at : at + 8], axis=0)

    def bias_of(at):
        parts = rows_of(c["dbias"], at).reshape(PAIRS, 2, 2, BS)
        return jnp.swapaxes(parts, 1, 2).reshape(2 * WIDTH)

    sums_ = a["sums"] + c["sums"]
    stats_ = a["stats"] + c["stats"]
    small = [
        rows_of(sums_, 24), rows_of(sums_, 32), bias_of(8), bias_of(0), rows_of(sums_, 0), rows_of(sums_, 8),
        rows_of(sums_, 16), jnp.sum(b["dbe"], axis=0),
    ]
    fsdp = lax.axis_size("fsdp")
    small = jnp.concatenate([v.reshape(fsdp, -1) for v in small], axis=1)
    weights = jnp.concatenate([c["dinner"].reshape(fsdp, -1), c["douter"].reshape(fsdp, -1)], axis=1)
    weights = jnp.concatenate([weights, small], axis=1).astype(BF16)
    own_small = scatter(weights.reshape(-1))
    own_we = scatter(b["dwe"])
    own_wc = scatter(b["dwc"].T)
    own_small, own_we, own_wc = lax.psum((own_small, own_we, own_wc), "rep")
    own_small = own_small.astype(F32)
    cut = inner_weight.size
    own_iw, own_ow = own_small[:cut].reshape(inner_weight.shape), own_small[cut : 2 * cut].reshape(inner_weight.shape)
    own = [own_small[2 * cut + x : 2 * cut + y] for x, y in zip(ends, ends[1:])]
    kinds = slot_items[:, None]
    valid = jnp.where((kinds == 0) | (jnp.arange(4)[None] < kinds), 1.0, 0.0)
    local = jnp.concatenate([jnp.sum(stats_.reshape(5, -1), axis=1), jnp.sum(valid)[None] * (PATCHES // 4 * WIDTH)])
    total = lax.psum(local, ("rep", "fsdp"))
    statistics = jnp.sqrt(total[:5] / total[5])
    return (
        c["out"].reshape(tokens.shape), c["igrad_out"].reshape(tokens.shape), own[0], own[1], own_iw, own[2], own_ow, own[3],
        own[4], own[5], own_we.astype(F32), own[7], own_wc.astype(F32), own[6], statistics,
    )


def specs():
    items = P(("rep", "fsdp"))
    big = P(("rep", "fsdp"), None, None)
    one, two = P("fsdp"), P("fsdp", None)
    ins = (big, big, items, one, one, two, one, two, one, one, one, two, one, two, one)
    outs = (big, big, one, one, two, one, two, one, one, one, two, one, two, one, P())
    return ins, outs


MESH = pl.DeviceIdType.MESH
ANY = pl.BlockSpec(memory_space=pl.ANY)
FSDP = 8
FIRST = 512
EARLY = 2


def multiple(value, by):
    return pl.multiple_of(value * by, by)


class Place:
    def __init__(self, copies):
        self.z, self.f = lax.axis_index("rep"), lax.axis_index("fsdp")
        self.core, self.chip = self.f & 1, self.f >> 1
        self.copies = copies

    def peer(self, mask):
        return (self.z, self.f ^ mask)

    def floor(self, offset):
        return (lax.rem(self.z + offset, self.copies), self.f)


def remote(src, dst, sems, at, device):
    send, recv = sems
    return pltpu.make_async_remote_copy(
        src_ref=src, dst_ref=dst, send_sem=send.at[at], recv_sem=recv.at[at], device_id=device, device_id_type=MESH
    )


class Sum:
    def __init__(self, place, R):
        self.p, self.R = place, R
        self.rows = R.sum_done.shape[1] // place.copies

    def core_copy(self, t):
        R = self.R
        other = 1 - self.p.core
        return remote(R.sum_own.at[t, :, other], R.sum_core.at[t], (R.sum_s0, R.sum_r0), t, self.p.peer(1))

    def chip_copy(self, t, k):
        R = self.R
        src = R.sum_own.at[t, self.p.chip ^ k, self.p.core]
        return remote(src, R.sum_chips.at[t, k - 1], (R.sum_s1, R.sum_r1), (t, k - 1), self.p.peer(2 * k))

    def piece(self, floor):
        return pl.ds(multiple(floor, self.rows), self.rows)

    def floor_copy(self, t, d):
        R = self.R
        device = self.p.floor(d)
        src = R.sum_total.at[t, self.piece(device[0])]
        return remote(src, R.sum_floors.at[t, d - 1], (R.sum_s2, R.sum_r2), (t, d - 1), device)

    def last_copy(self, t, d):
        R = self.R
        mine = R.sum_done.at[t, self.piece(self.p.z)]
        return remote(mine, mine, (R.sum_s3, R.sum_r3), (t, d - 1), self.p.floor(d))

    def last_arrival(self, t, d):
        R = self.R
        source = lax.rem(self.p.z + self.p.copies - d, self.p.copies)
        theirs = R.sum_done.at[t, self.piece(source)]
        return remote(theirs, theirs, (R.sum_s3, R.sum_r3), (t, d - 1), self.p.floor(d))

    def offsets(self):
        return range(1, self.p.copies)

    def start(self, t):
        self.core_copy(t).start()

    def to_chips(self, t):
        R = self.R
        self.core_copy(t).wait_recv()
        for k in (3, 1, 2, 0):
            at = self.p.chip ^ k
            mine = R.sum_own[t, at, self.p.core].astype(F32) + R.sum_core[t, at].astype(F32)
            R.sum_own[t, at, self.p.core] = mine.astype(BF16)
            if k:
                self.chip_copy(t, k).start()

    def to_floors(self, t):
        R = self.R
        total = R.sum_own[t, self.p.chip, self.p.core].astype(F32)
        for k in (1, 2, 3):
            self.chip_copy(t, k).wait_recv()
            total = total + R.sum_chips[t, k - 1].astype(F32)
        R.sum_total[t] = total.astype(BF16)
        for d in self.offsets():
            self.floor_copy(t, d).start()

    def to_all(self, t):
        R = self.R
        mine = self.piece(self.p.z)
        total = R.sum_total[t, mine, :].astype(F32)
        for d in self.offsets():
            self.floor_copy(t, d).wait_recv()
            total = total + R.sum_floors[t, d - 1].astype(F32)
        R.sum_done[t, mine, :] = total.astype(BF16)
        for d in self.offsets():
            self.last_copy(t, d).start()

    def finish(self, t):
        for d in self.offsets():
            self.last_arrival(t, d).wait_recv()

    def sent(self, t):
        self.core_copy(t).wait_send()
        for k in (1, 2, 3):
            self.chip_copy(t, k).wait_send()
        for d in self.offsets():
            self.floor_copy(t, d).wait_send()
            self.last_copy(t, d).wait_send()


class Gather:
    def __init__(self, R, place):
        self.R, self.p = R, place

    def lay(self):
        R, f = self.R, self.p.f
        deep = R.we_in.shape[0]
        chunks = R.w.shape[0]
        for t in range(chunks):
            R.w[t, f, :, CHUNK:] = R.wc_in[pl.ds(t * deep, deep), :]
        for t in range(0, chunks, 2):
            for m in range(CHUNK // 128):
                at = m * 4 * chunks * BS // 2 + t * BS
                even = R.we_in[:, at : at + 128].astype(F32)
                odd = R.we_in[:, at + chunks * BS : at + chunks * BS + 128].astype(F32)
                for side, part in enumerate(interleave(even, odd)):
                    R.w[t + side, f, :, 128 * m : 128 * m + 128] = part.astype(BF16)

    def copy(self, t, mask, target):
        view = self.R.w.at[t, self.p.f ^ mask]
        return pltpu.make_async_remote_copy(
            src_ref=view,
            dst_ref=view,
            send_sem=self.R.gather_send.at[t, mask, target >> 1],
            recv_sem=self.R.gather_recv.at[t, mask ^ target],
            device_id=self.p.peer(target),
            device_id_type=MESH,
        )

    def arrival(self, t, mask):
        view = self.R.w.at[t, self.p.f ^ mask]
        return pltpu.make_async_remote_copy(
            src_ref=view,
            dst_ref=view,
            send_sem=self.R.gather_send.at[t, 0, 0],
            recv_sem=self.R.gather_recv.at[t, mask],
            device_id=self.p.peer(1),
            device_id_type=MESH,
        )

    def start(self, t):
        for target in (6, 2, 4, 1):
            self.copy(t, 0, target).start()

    def pass_on(self, t):
        for mask in (2, 4, 6):
            self.arrival(t, mask).wait_recv()
            self.copy(t, mask, 1).start()

    def finish(self, t):
        for mask in (1, 3, 5, 7):
            self.arrival(t, mask).wait_recv()

    def sent(self, t):
        for target in (6, 2, 4, 1):
            self.copy(t, 0, target).wait_send()
        for mask in (2, 4, 6):
            self.copy(t, mask, 1).wait_send()


def pack_small(R):
    R.small[pl.ds(0, BS), :] = R.inner_in[...]
    R.small[pl.ds(BS, BS), :] = R.outer_in[...]

    def row(*refs):
        return jnp.concatenate([ref[...].astype(F32) for ref in refs], axis=1)

    none = jnp.zeros((1, BS), F32)
    rows = [
        row(R.fg_in, R.fs_in), R.ib_in[...].astype(F32), R.ob_in[...].astype(F32), row(R.gg_in, R.gs_in),
        jnp.concatenate([R.cb_in[...].astype(F32), none], axis=1),
        R.eb_in[...].astype(F32), jnp.zeros((9, 128), F32),
    ]
    R.small[pl.ds(2 * BS, 16), :] = jnp.concatenate(rows, axis=0).astype(BF16)


def unpack_small(R):
    for j in range(PAIRS):
        cols = slice(128 * j, 128 * j + 128)
        even = R.smalls[2 * j, pl.ds(2 * BS, 16), :].astype(F32)
        odd = R.smalls[2 * j + 1, pl.ds(2 * BS, 16), :].astype(F32)
        first, second = interleave(even, odd)
        for row, (part, at) in enumerate(
            [(first, 0), (second, 0), (first, 1), (second, 1), (first, 2), (second, 2), (first, 3), (second, 3), (first, 4)]
        ):
            R.vec[row : row + 1, cols] = part[at : at + 1]
        for t in range(R.be.shape[1] // CHUNK):
            R.be[0:1, t * CHUNK + 128 * j : t * CHUNK + 128 * j + 128] = (first, second)[t % 2][5 + t // 2 : 6 + t // 2]
    for first, out in ((0, R.win), (BS, R.wout)):
        complex_pairs(R.smalls.at[:, pl.ds(first, BS), :], out)


def pack_sums(R):
    slots = R.tok.shape[0] // PATCHES

    def total(ref, at):
        return jnp.sum(ref[pl.ds(at, 8), :], axis=0, keepdims=True)

    feed_gain, feed_shift, contract, gain, shift = [total(R.sums, 8 * i) for i in range(5)]
    outer, inner, expand = total(R.dbias, 0), total(R.dbias, 8), total(R.dbe, 0)
    lane = lax.broadcasted_iota(jnp.int32, (1, 128), 1)
    facts = jnp.zeros((1, 128), F32)
    for i in range(5):
        facts = jnp.where(lane == i, jnp.sum(total(R.stats, 8 * i), axis=1, keepdims=True), facts)
    valid = jnp.zeros((1, 128), F32)
    for slot in range(slots):
        kind = kind_of(R, slot, 128)
        valid = valid + jnp.where(kind == 0, 4, kind).astype(F32) * float(PATCHES // 4 * WIDTH)
    facts = jnp.where(lane == 5, valid, facts)
    none = jnp.zeros((1, 128), F32)
    for j in range(PAIRS):
        cols = slice(128 * j, 128 * j + 128)
        real, imag = slice(256 * j, 256 * j + 128), slice(256 * j + 128, 256 * j + 256)
        rows = [
            interleave(gain[:, cols], shift[:, cols]),
            interleave(inner[:, real], inner[:, imag]),
            interleave(outer[:, real], outer[:, imag]),
            interleave(feed_gain[:, cols], feed_shift[:, cols]),
            interleave(contract[:, cols], none),
        ]
        for t in range(0, R.be.shape[1] // CHUNK, 2):
            low, high = [expand[:, (t + s) * CHUNK + 128 * j : (t + s) * CHUNK + 128 * j + 128] for s in range(2)]
            rows.append(interleave(low, high))
        for side in range(2):
            R.vec_own[2 * j + side] = jnp.concatenate([row[side] for row in rows] + [facts], axis=0)


class Share:
    def __init__(self, place, own, arrived, floors, sems):
        self.p, self.own, self.arrived, self.floors = place, own, arrived, floors
        self.peer_sems, self.floor_sems = sems

    def peer_copy(self, k):
        return remote(self.own.at[self.p.f ^ k], self.arrived.at[k - 1], self.peer_sems, k - 1, self.p.peer(k))

    def floor_copy(self, d):
        mine = self.floors.at[self.p.z]
        return remote(mine, mine, self.floor_sems, d - 1, self.p.floor(d))

    def floor_arrival(self, d):
        theirs = self.floors.at[lax.rem(self.p.z + self.p.copies - d, self.p.copies)]
        return remote(theirs, theirs, self.floor_sems, d - 1, self.p.floor(d))

    def start(self):
        for k in (6, 7, 2, 4, 3, 5, 1):
            self.peer_copy(k).start()

    def to_floors(self):
        total = self.own[self.p.f].astype(F32)
        for k in range(1, FSDP):
            self.peer_copy(k).wait_recv()
            total = total + self.arrived[k - 1].astype(F32)
        self.floors[self.p.z] = total.astype(self.floors.dtype)
        for d in range(1, self.p.copies):
            self.floor_copy(d).start()

    def finish(self):
        for d in range(1, self.p.copies):
            self.floor_arrival(d).wait_recv()
        total = self.floors[0].astype(F32)
        for z in range(1, self.p.copies):
            total = total + self.floors[z].astype(F32)
        return total

    def sent(self):
        for k in range(1, FSDP):
            self.peer_copy(k).wait_send()
        for d in range(1, self.p.copies):
            self.floor_copy(d).wait_send()


def layer(copies, R):
    p = Place(copies)
    n = R.tok.shape[0]
    slots = n // PATCHES
    chunks = R.w.shape[0]
    blocks = n // CHUNK
    last = chunks - 1

    def slot_rows(slot):
        return pl.ds(multiple(slot, PATCHES), PATCHES)

    def load(which, slot):
        src, dst = ((R.tok_in, R.tok), (R.cot_in, R.msk))[which]
        rows = slot_rows(slot)
        return pltpu.make_async_copy(src.at[rows, :], dst.at[rows, :], R.load_sems.at[which, slot])

    def store(which, slot):
        src, dst = ((R.feed, R.out_ref), (R.fg, R.grad_ref))[which]
        rows = slot_rows(slot)
        return pltpu.make_async_copy(src.at[rows, :], dst.at[rows, :], R.store_sems.at[which, slot])

    barrier = pltpu.get_barrier_semaphore()
    for k in range(1, FSDP):
        pl.semaphore_signal(barrier, inc=1, device_id=p.peer(k), device_id_type=MESH)
    for d in range(1, copies):
        pl.semaphore_signal(barrier, inc=1, device_id=p.floor(d), device_id_type=MESH)
    for slot in range(slots):
        load(0, slot).start()
        load(1, slot).start()
    R.stats[...] = jnp.zeros_like(R.stats)
    R.sums[...] = jnp.zeros_like(R.sums)
    R.dbias[...] = jnp.zeros_like(R.dbias)
    R.dbe[...] = jnp.zeros_like(R.dbe)
    pack_small(R)
    R.smalls[p.f] = R.small[...]
    gather = Gather(R, p)
    gather.lay()

    def begin(slot):
        load(0, slot).wait()
        load(1, slot).wait()
        mixer_start(R, slot)
        rows = slot_rows(slot)
        R.br[rows, :] = jnp.zeros((PATCHES, WIDTH), F32)
        R.fg[rows, :] = jnp.zeros((PATCHES, WIDTH), F32)

    pl.loop(0, EARLY)(begin)
    pl.semaphore_wait(barrier, FSDP - 1 + copies - 1)

    def small_copy(k):
        return remote(R.small, R.smalls.at[p.f], (R.small_send, R.small_recv), k - 1, p.peer(k))

    def small_arrival(k):
        return remote(R.small, R.smalls.at[p.f ^ k], (R.small_send, R.small_recv), k - 1, p.peer(k))

    for k in (6, 7, 2, 4, 3, 5, 1):
        small_copy(k).start()
    gather.start(0)
    gather.start(1)
    pl.loop(EARLY, slots)(begin)
    for k in range(1, FSDP):
        small_arrival(k).wait_recv()
    unpack_small(R)

    @pl.loop(0, slots)
    def _(slot):
        mixer_forward(R, slot)

    gather.start(2)
    gather.start(3)
    gather.pass_on(0)
    gather.finish(0)
    sums = Sum(p, R)

    def weights(t):
        return [R.w[t, :, :, pl.ds(at, CHUNK)].reshape(-1, CHUNK) for at in (0, CHUNK)]

    def weight_gradients(t):
        for at, (left, right) in ((0, (R.feed, R.hgrad)), (CHUNK, (R.hidden, R.msk))):
            piece = dot(left[...], right[...], TN).astype(BF16)
            for k in range(FSDP):
                R.sum_own[t, k // 2, k % 2, :, at : at + CHUNK] = piece[k * BS : (k + 1) * BS]
        sums.start(t)

    @pl.loop(0, last)
    def _(t):
        cols = pl.ds(multiple(t, CHUNK), CHUNK)

        @pl.loop(0, blocks)
        def _(i):
            @pl.when((t > 0) & (i == 1))
            def _():
                sums.to_chips(t - 1)

            @pl.when((t > 1) & (i == 1))
            def _():
                sums.to_floors(t - 2)

            mlp_chunk(R, i, cols, *weights(t))

            @pl.when(i == 2)
            def _():
                gather.pass_on(t + 1)

        weight_gradients(t)
        gather.finish(t + 1)

    cols = slice(last * CHUNK, (last + 1) * CHUNK)

    @pl.loop(0, blocks)
    def _(i):
        @pl.when(i == 1)
        def _():
            sums.to_all(last - 3)
            sums.to_chips(last - 1)
            sums.to_floors(last - 2)

        mlp_front(R, i, cols, *weights(last))

    weight_gradients(last)

    @pl.loop(0, blocks)
    def _(i):
        rows = pl.ds(multiple(i, CHUNK), CHUNK)
        mlp_back(R, rows, R.hidden[rows, :], R.hgrad[rows, :], *weights(last))

        @pl.when(i == 1)
        def _():
            sums.to_chips(last)
            sums.to_floors(last - 1)
            sums.to_all(last - 2)

    @pl.loop(0, slots)
    def _(slot):
        mixer_backward_first(R, slot)
        store(0, slot).start()

        @pl.when(slot == 2)
        def _():
            sums.to_all(last - 1)

        @pl.when(slot == 5)
        def _():
            sums.to_floors(last)

    def put(first):
        def write(j, value):
            for side in range(2):
                R.mix_own[2 * j + side, pl.ds(first, BS), :] = value[side * BS : (side + 1) * BS].astype(BF16)

        return write

    mixer_weight_gradients(R, put(0), put(BS))
    mixing = Share(p, R.mix_own, R.mix_peers, R.mix_floors, ((R.mix_s0, R.mix_r0), (R.mix_s1, R.mix_r1)))
    mixing.start()

    def put_grad(slot, rows, value):
        R.fg[rows, :] = value
        store(1, slot).start()

    @pl.loop(0, slots)
    def _(slot):
        mixer_backward_second(R, slot, put_grad)

        @pl.when(slot == 3)
        def _():
            sums.to_all(last)

    pack_sums(R)
    vectors = Share(p, R.vec_own, R.vec_peers, R.vec_floors, ((R.vec_s0, R.vec_r0), (R.vec_s1, R.vec_r1)))
    vectors.start()
    mixing.to_floors()
    vectors.to_floors()
    R.mix_ref[...] = mixing.finish()
    for t in range(chunks):
        sums.finish(t)
    done_out = pltpu.make_async_copy(R.sum_done, R.done_ref, R.keep_sems.at[0])
    done_out.start()
    R.vec_ref[...] = vectors.finish()
    for k in range(1, FSDP):
        small_copy(k).wait_send()
    for t in range(chunks):
        gather.sent(t)
        sums.sent(t)
    mixing.sent()
    vectors.sent()

    @pl.loop(0, slots)
    def _(slot):
        store(0, slot).wait()
        store(1, slot).wait()

    done_out.wait()


def body_in_one(
    copies, tokens, cotangent, slot_items, filter_gain, filter_shift, inner_weight, inner_bias, outer_weight, outer_bias,
    feed_gain, feed_shift, expand_weight, expand_bias, contract_weight, contract_bias,
):
    slots = tokens.shape[0]
    n = slots * PATCHES
    deep, hidden = expand_weight.shape
    tall = contract_weight.shape[0]
    chunks = hidden // CHUNK
    floors = copies - 1
    ins = dict(
        items=slot_items, tok_in=tokens.reshape(n, WIDTH), cot_in=cotangent.reshape(n, WIDTH), table=jnp.asarray(TABLES, BF16),
        inner_in=inner_weight, outer_in=outer_weight, we_in=expand_weight, wc_in=contract_weight,
        fg_in=filter_gain[None], fs_in=filter_shift[None], ib_in=inner_bias[None], ob_in=outer_bias[None],
        gg_in=feed_gain[None], gs_in=feed_shift[None], cb_in=contract_bias[None], eb_in=expand_bias.reshape(2, 128),
    )
    places = dict.fromkeys(("tok_in", "cot_in", "out_ref", "grad_ref", "done_ref"), ANY)
    places["items"] = SMEM
    outs = dict(
        out_ref=((n, WIDTH), BF16), grad_ref=((n, WIDTH), F32), done_ref=((chunks, deep, 2 * CHUNK), BF16),
        mix_ref=((2 * BS, 2 * BS), F32), vec_ref=((8, 128), F32),
    )
    wide, flat, full = ((n, 2 * WIDTH), BF16), ((n, WIDTH), BF16), ((n, WIDTH), F32)
    pairs, sums = ((2 * WIDTH, 4 * BS), BF16), ((40, WIDTH), F32)
    both = 2 * CHUNK
    memory = dict(
        tok=flat, msk=flat, spec=wide, act=wide, slope=wide, bent=wide, mid=full, feed=flat, br=full, fg=full,
        hidden=((n, CHUNK), BF16), hgrad=((n, CHUNK), BF16), w=((chunks, FSDP, deep, both), BF16),
        win=pairs, wout=pairs, vec=((16, WIDTH), F32), be=((8, hidden), F32), stats=sums, sums=sums,
        dbias=((16, 2 * WIDTH), F32), dbe=((8, hidden), F32),
        small=((144, 128), BF16), smalls=((FSDP, 144, 128), BF16),
        sum_own=((chunks, 4, 2, deep, both), BF16), sum_core=((chunks, 4, deep, both), BF16),
        sum_chips=((chunks, 3, deep, both), BF16), sum_total=((chunks, deep, both), BF16),
        sum_floors=((chunks, floors, deep // copies, both), BF16), sum_done=((chunks, deep, both), BF16),
        mix_own=((FSDP, 128, 128), BF16), mix_peers=((FSDP - 1, 128, 128), BF16), mix_floors=((copies, 128, 128), BF16),
        vec_own=((FSDP, 8, 128), F32), vec_peers=((FSDP - 1, 8, 128), F32), vec_floors=((copies, 8, 128), F32),
    )
    sems = dict(
        load_sems=(2, slots), store_sems=(2, slots), small_send=(7,), small_recv=(7,), keep_sems=(1,),
        gather_send=(chunks, 8, 4), gather_recv=(chunks, 8),
    )
    for step, shape in enumerate(((chunks,), (chunks, 3), (chunks, floors), (chunks, floors))):
        sems[f"sum_s{step}"] = sems[f"sum_r{step}"] = shape
    for key in ("mix", "vec"):
        for step, shape in enumerate(((FSDP - 1,), (floors,))):
            sems[f"{key}_s{step}"] = sems[f"{key}_r{step}"] = shape
    names = list(ins) + list(outs) + list(memory) + list(sems)

    def kernel(*refs):
        R = named(names, refs)
        R.mgrad, R.out, R.ograd, R.igrad, R.cot = R.fg, R.feed, R.bent, R.slope, R.msk
        layer(copies, R)

    o = dict(
        zip(
            outs,
            pl.pallas_call(
                kernel,
                out_shape=[jax.ShapeDtypeStruct(*spec) for spec in outs.values()],
                in_specs=[places.get(key, VMEM) for key in ins],
                out_specs=[places.get(key, VMEM) for key in outs],
                scratch_shapes=[pltpu.VMEM(*spec) for spec in memory.values()]
                + [pltpu.SemaphoreType.DMA(shape) for shape in sems.values()],
                compiler_params=pltpu.CompilerParams(vmem_limit_bytes=ROOM, collective_id=0, has_side_effects=True),
                name="mega",
            )(*ins.values()),
        )
    )
    return finishing(tokens.shape, o, deep, hidden, tall)


PIECES = 8


def finishing(shape, o, deep, hidden, tall):
    ends = dict(
        out=(o["out_ref"].shape, BF16), grad=(o["grad_ref"].shape, F32), fg=((1, BS), F32), fs=((1, BS), F32),
        inner=((BS, 2 * BS), F32), ib=((1, 128), F32), outer=((BS, 2 * BS), F32), ob=((1, 128), F32), gg=((1, BS), F32),
        gs=((1, BS), F32), ew=((deep, hidden), F32), eb=((2, 128), F32), cw=((tall, WIDTH), F32), cb=((1, BS), F32),
        stat=((1, 5), F32),
    )
    names = list(o) + list(ends) + ["grad_held", "out_held", "sems"]

    def kernel(*refs):
        R = named(names, refs)
        ways = []
        for which, (src, held, dst) in enumerate(((R.grad_ref, R.grad_held, R.grad), (R.out_ref, R.out_held, R.out))):
            size = src.shape[0] // PIECES
            for i in range(PIECES):
                rows = pl.ds(i * size, size)
                ways.append(
                    (
                        pltpu.make_async_copy(src.at[rows], held.at[rows], R.sems.at[0, which, i]),
                        pltpu.make_async_copy(held.at[rows], dst.at[rows], R.sems.at[1, which, i]),
                    )
                )
        for come, _ in ways:
            come.start()
        for come, go in ways:
            come.wait()
            go.start()
        chunks, deep = R.done_ref.shape[:2]
        for t in range(0, chunks, 2):
            for m in range(CHUNK // 128):
                low, high = [R.done_ref[t + side, :, 128 * m : 128 * m + 128].astype(F32) for side in range(2)]
                at = m * 4 * chunks * BS // 2 + t * BS
                for side, part in enumerate(interleave(low, high)):
                    R.ew[:, at + side * chunks * BS : at + side * chunks * BS + 128] = part
        for t in range(chunks):
            R.cw[pl.ds(t * deep, deep), :] = R.done_ref[t, :, CHUNK:].astype(F32)
        R.inner[...], R.outer[...] = R.mix_ref[:BS], R.mix_ref[BS:]
        vec = R.vec_ref[...]
        R.fg[...], R.fs[...] = vec[0:1, :BS], vec[0:1, BS:]
        R.ib[...], R.ob[...] = vec[1:2], vec[2:3]
        R.gg[...], R.gs[...] = vec[3:4, :BS], vec[3:4, BS:]
        R.cb[...], R.eb[...] = vec[4:5, :BS], vec[5:7]
        lane = lax.broadcasted_iota(jnp.int32, (1, 128), 1)
        total = jnp.sum(jnp.where(lane == 5, vec[7:8], 0.0), axis=1, keepdims=True)
        R.stat[...] = jnp.sqrt(vec[7:8] / total)[:, :5]
        for _, go in ways:
            go.wait()

    places = dict.fromkeys(("out_ref", "grad_ref", "out", "grad"), ANY)
    values = pl.pallas_call(
        kernel,
        out_shape=[jax.ShapeDtypeStruct(*spec) for spec in ends.values()],
        in_specs=[places.get(key, VMEM) for key in o],
        out_specs=[places.get(key, VMEM) for key in ends],
        scratch_shapes=[
            pltpu.VMEM(o["grad_ref"].shape, F32), pltpu.VMEM(o["out_ref"].shape, BF16), pltpu.SemaphoreType.DMA((2, 2, PIECES)),
        ],
        compiler_params=pltpu.CompilerParams(vmem_limit_bytes=ROOM),
        name="finishing",
    )(*o.values())
    e = dict(zip(ends, values))
    for key in ("out", "grad"):
        e[key] = e[key].reshape(shape)
    for key in ("fg", "fs", "ib", "ob", "gg", "gs", "eb", "cb", "stat"):
        e[key] = e[key].reshape(-1)
    return tuple(e.values())


def solution(mesh):
    ins, outs = specs()
    whole = body_by_collectives
    if mesh.shape["fsdp"] == FSDP and mesh.shape["rep"] in (2, 4):
        whole = functools.partial(body_in_one, mesh.shape["rep"])
    return jax.shard_map(whole, mesh=mesh, in_specs=ins, out_specs=outs, check_vma=False)
```

```python
import functools
import math

import jax
import jax.numpy as jnp
import numpy as np
from jax import lax
from jax.experimental import pallas as pl
from jax.experimental.pallas import tpu as pltpu
from jax.sharding import PartitionSpec as P

BS = 64
NB = 8
SIDE = 16
PATCHES = SIDE * SIDE
WIDTH = NB * BS
HALF = PATCHES // 2
TAIL = 16
PAIRS = NB // 2
CHUNK = 512
EPSILON = 1e-05
SHRINK = 0.25
F32 = jnp.float32
BF16 = jnp.bfloat16
NT = (((1,), (1,)), ((), ()))
TN = (((0,), (0,)), ((), ()))
TABLE_SCALE = 1.132805


def frequency_order(side):
    pairs, selfs = [], []
    for a in range(side):
        for b in range(side):
            other = ((-a) % side, (-b) % side)
            if other == (a, b):
                selfs.append((a, b))
            elif (a, b) < other:
                pairs.append((a, b))
    return pairs, selfs


def spectrum_table(side):
    tiles = SIDE // side
    pairs, selfs = frequency_order(side)
    row = np.arange(PATCHES) // SIDE
    col = np.arange(PATCHES) % SIDE
    top, bottom = [], []
    for kind in ("pair", "self"):
        for qr in range(tiles):
            for qc in range(tiles):
                inside = (row // side == qr) & (col // side == qc)
                listed = pairs if kind == "pair" else selfs
                for at, (a, b) in enumerate(listed):
                    angle = 2.0 * math.pi / side * ((a * row + b * col) % side)
                    if kind == "pair":
                        top.append(np.where(inside, np.cos(angle), 0.0) / side)
                        bottom.append(np.where(inside, -np.sin(angle), 0.0) / side)
    extra = []
    for at in range(len(selfs)):
        for qr in range(tiles):
            for qc in range(tiles):
                inside = (row // side == qr) & (col // side == qc)
                a, b = selfs[at]
                angle = 2.0 * math.pi / side * ((a * row + b * col) % side)
                extra.append(np.where(inside, np.cos(angle), 0.0) / side)
    half = len(extra) // 2
    return np.array(top + extra[:half] + bottom + extra[half:]), len(top), tiles * tiles


WHOLE_TABLE, WHOLE_PAIRS, WHOLE_ZEROS = spectrum_table(SIDE)
PART_TABLE, PART_PAIRS, PART_ZEROS = spectrum_table(SIDE // 2)
TABLES = np.concatenate([WHOLE_TABLE * TABLE_SCALE, PART_TABLE], axis=0)


def dot(a, b, dims=(((1,), (0,)), ((), ()))):
    return lax.dot_general(a, b, dims, preferred_element_type=F32)


def sum8(values):
    return jnp.sum(values.reshape(-1, 8, values.shape[-1]), axis=0)


def gelu_and_slope(v):
    phi = 0.5 * lax.erf(v * 0.7071067811865476) + 0.5
    bell = jnp.exp2(v * v * (-0.5 / math.log(2.0))) * (1.0 / math.sqrt(2.0 * math.pi))
    return v * phi, phi + v * bell


def row_stats(values):
    mean = jnp.mean(values, axis=-1, keepdims=True)
    centre = values - mean
    spread = jnp.mean(centre * centre, axis=-1, keepdims=True)
    scale = lax.rsqrt(spread + EPSILON)
    return centre * scale, scale, spread + mean * mean


def turns(*steps):
    left = list(steps)
    while left:
        for step in list(left):
            if next(step, None) is None:
                left.remove(step)
        yield True


def run(*steps):
    for _ in turns(*steps):
        pass


def chain(*steps):
    for step in steps:
        yield from step


def weave(first, count, second):
    ended = False
    while not ended:
        for _ in range(count):
            if next(first, None) is None:
                ended = True
        next(second, None)
    for _ in second:
        pass


def kind_of(R, slot, lanes=WIDTH):
    return jnp.full((1, lanes), R.items[slot], jnp.int32)


def slot_facts(kind):
    whole = kind == 0
    pairs = jnp.where(whole, WHOLE_PAIRS, PART_PAIRS)
    scale = jnp.where(whole, 1.0 / TABLE_SCALE, 1.0).astype(F32)
    return whole, pairs, scale


def table_of(R, kind):
    whole = jnp.where(kind[:, :PATCHES] == 0, 1.0, 0.0).astype(F32)
    first, second = whole.astype(BF16), (1.0 - whole).astype(BF16)
    return R.table[pl.ds(0, PATCHES), :] * first + R.table[pl.ds(PATCHES, PATCHES), :] * second


def tail_pairs(pairs, lanes):
    row = lax.broadcasted_iota(jnp.int32, (TAIL, lanes), 0) + (HALF - TAIL)
    return row < pairs[:, :lanes]


def spread(halves, pairs):
    head = HALF - TAIL
    is_pair = tail_pairs(pairs, halves.shape[1])
    top, bottom = halves[:HALF], halves[HALF:]
    low_imag = jnp.where(is_pair, bottom[head:], 0.0)
    low_real = jnp.where(is_pair, top[head:], bottom[head:])
    imag = jnp.concatenate([bottom[:head], low_imag], axis=0)
    return top, imag, jnp.concatenate([top[:head], low_real], axis=0)


def fold(block, pairs):
    head = HALF - TAIL
    is_pair = tail_pairs(pairs, 128)
    ra, ia = block[:HALF, :128], block[:HALF, 128:]
    rb, ib = block[HALF:, :128], block[HALF:, 128:]
    top = [ra[:head] + rb[:head], ra[head:] + jnp.where(is_pair, rb[head:], 0.0)]
    bottom = [ia[:head] - ib[:head], jnp.where(is_pair, ia[head:] - ib[head:], rb[head:])]
    return jnp.concatenate(top, axis=0), jnp.concatenate(bottom, axis=0)


def interleave(first, second):
    low = lax.broadcasted_iota(jnp.int32, first.shape, 1) < BS
    return (
        jnp.where(low, first, pltpu.roll(second, BS, 1)),
        jnp.where(low, pltpu.roll(first, BS, 1), second),
    )


def complex_pairs(weight_ref, out_ref, up_ref=None):
    low = lax.broadcasted_iota(jnp.int32, (BS, 128), 1) < BS
    for j in range(PAIRS):
        first, second = weight_ref[2 * j].astype(F32), weight_ref[2 * j + 1].astype(F32)
        real = jnp.concatenate([jnp.where(low, first, 0.0), jnp.where(low, 0.0, pltpu.roll(second, BS, 1))], axis=0)
        imag = jnp.concatenate([jnp.where(low, pltpu.roll(first, BS, 1), 0.0), jnp.where(low, 0.0, second)], axis=0)
        matrix = jnp.concatenate(
            [jnp.concatenate([real, imag], axis=1), jnp.concatenate([-imag, real], axis=1)], axis=0
        )
        out_ref[pl.ds(256 * j, 256), :] = matrix.astype(BF16)
        if up_ref is not None:
            up_ref[pl.ds(256 * j, 256), :] = (matrix * (1.0 / SHRINK)).astype(BF16)


def pair_gradient(product):
    real = product[:128, :128] + product[128:, 128:]
    imag = product[:128, 128:] - product[128:, :128]
    low = lax.broadcasted_iota(jnp.int32, (BS, 128), 1) < BS
    first = jnp.where(low, real[:BS], pltpu.roll(imag[:BS], BS, 1))
    second = jnp.where(low, pltpu.roll(real[BS:], BS, 1), imag[BS:])
    return jnp.concatenate([first, second], axis=0)


def masked_squares(values, kind):
    squares = values * values
    parts = jnp.sum(squares.reshape(2, 8, 2, 8, squares.shape[-1]), axis=1)
    total = parts[0, 0]
    for q in range(1, 4):
        valid = jnp.where((kind == 0) | (q < kind), 1.0, 0.0).astype(F32)
        total = total + valid * parts[q // 2, q % 2]
    return total


def quadrant_of(shape):
    position = lax.broadcasted_iota(jnp.int32, shape, 0)
    return (position >> 7) * 2 + ((position >> 3) & 1)


def masked(values, kind):
    kind = kind[:, : values.shape[1]]
    return jnp.where((kind == 0) | (quadrant_of(values.shape) < kind), values, 0.0)


def add_mean_squares(R, at, means, kind):
    R.stats[pl.ds(at, 8), 0:1] += sum8(masked(means, kind)) * float(WIDTH)


def mixer_start(R, slot):
    kind = kind_of(R, slot)
    whole, pairs, scale = slot_facts(kind)
    rows = pl.ds(pl.multiple_of(slot * PATCHES, PATCHES), PATCHES)
    x = R.tok[rows, :].astype(F32)
    xhat, _, means = row_stats(x)
    add_mean_squares(R, 0, means, kind)
    R.mid[rows, :] = dot(table_of(R, kind), xhat.astype(BF16))
    grad = masked(R.cot[rows, :].astype(F32), kind)
    R.sums[pl.ds(16, 8), :] += sum8(grad)
    R.msk[rows, :] = grad.astype(BF16)


def mixer_forward(R, slot):
    kind = kind_of(R, slot)
    whole, pairs, scale = slot_facts(kind)
    rows = pl.ds(pl.multiple_of(slot * PATCHES, PATCHES), PATCHES)
    spec = R.mid[rows, :] * (R.vec[0:1, :] * scale)
    row = lax.broadcasted_iota(jnp.int32, (TAIL, WIDTH), 0) + (HALF - TAIL)
    at_zero = (row >= pairs) & (row < pairs + jnp.where(whole, WHOLE_ZEROS, PART_ZEROS))
    shift = R.vec[1:2, :] * jnp.where(whole, float(SIDE), float(SIDE // 2)).astype(F32)
    zeros = spec[HALF - TAIL : HALF] + jnp.where(at_zero, shift, 0.0)
    spec = jnp.concatenate([spec[: HALF - TAIL], zeros, spec[HALF:]], axis=0)
    ra, ia, rb = [part.astype(BF16) for part in spread(spec, pairs)]
    tops, bottoms = [], []
    for j in range(PAIRS):
        lanes = slice(256 * j, 256 * j + 256)
        cols = slice(128 * j, 128 * j + 128)
        low = jnp.concatenate(
            [
                jnp.concatenate([ra[:, cols], ia[:, cols]], axis=1),
                jnp.concatenate([rb[:, cols], -ia[:, cols]], axis=1),
            ],
            axis=0,
        )
        R.spec[rows, lanes] = low
        yield True
        pre = dot(low, R.win[pl.ds(256 * j, 256), :]) + jnp.concatenate([R.vec[2:3, cols], R.vec[3:4, cols]], axis=1)
        act, slope = gelu_and_slope(pre)
        act = act.astype(BF16)
        R.act[rows, lanes] = act
        R.slope[rows, lanes] = slope.astype(BF16)
        yield True
        post = dot(act, R.wout_up[pl.ds(256 * j, 256), :]) + jnp.concatenate(
            [R.vec[4:5, cols], R.vec[5:6, cols]], axis=1
        )
        bent = jnp.tanh(post)
        R.bent[rows, lanes] = (bent * bent).astype(BF16)
        u, v = fold(post - bent, pairs)
        tops.append(u.astype(BF16))
        bottoms.append(v.astype(BF16))
    yield True
    folded = jnp.concatenate([jnp.concatenate(tops, axis=1), jnp.concatenate(bottoms, axis=1)], axis=0)
    mixer_out = dot(table_of(R, kind), folded, TN) * (scale * SHRINK)
    R.stats[pl.ds(8, 8), :] += masked_squares(mixer_out, kind)
    middle = R.tok[rows, :].astype(F32) + mixer_out
    R.mid[rows, :] = middle
    yield True
    yhat, _, means = row_stats(middle)
    add_mean_squares(R, 16, means, kind)
    R.feed[rows, :] = (yhat * R.vec[6:7, :] + R.vec[7:8, :]).astype(BF16)
    yield True


def mlp_front(R, i, cols, we, wc):
    rows = pl.ds(pl.multiple_of(i * CHUNK, CHUNK), CHUNK)
    hidden, slope = gelu_and_slope(dot(R.feed[rows, :], we) + R.be[0:1, cols])
    hidden = hidden.astype(BF16)
    R.hidden[rows, :] = hidden
    yield True
    back = dot(R.msk[rows, :], wc, NT) * slope
    R.dbe[:, cols] += sum8(back)
    back = back.astype(BF16)
    R.hgrad[rows, :] = back
    yield True


def mlp_back(R, i, we, wc, first=False):
    rows = pl.ds(pl.multiple_of(i * CHUNK, CHUNK), CHUNK)
    branch = dot(R.hidden[rows, :], wc)
    R.br[rows, :] = branch if first else R.br[rows, :] + branch
    yield True
    grad = dot(R.hgrad[rows, :], we, NT)
    R.fg[rows, :] = grad if first else R.fg[rows, :] + grad
    yield True


def mlp_chunk(R, i, cols, we, wc, first=False):
    return chain(mlp_front(R, i, cols, we, wc), mlp_back(R, i, we, wc, first))


def mixer_backward_first(R, slot):
    kind = kind_of(R, slot)
    whole, pairs, scale = slot_facts(kind)
    rows = pl.ds(pl.multiple_of(slot * PATCHES, PATCHES), PATCHES)
    feed_grad = R.fg[rows, :]
    yhat, yscale, _ = row_stats(R.mid[rows, :])
    R.sums[pl.ds(0, 8), :] += sum8(feed_grad * yhat)
    R.sums[pl.ds(8, 8), :] += sum8(feed_grad)
    scaled = feed_grad * R.vec[6:7, :]
    yield True
    inner = scaled - jnp.mean(scaled, axis=-1, keepdims=True) - yhat * jnp.mean(scaled * yhat, axis=-1, keepdims=True)
    mgrad = R.msk[rows, :].astype(F32) + inner * yscale
    R.mgrad[rows, :] = mgrad
    yield True
    ra_all, ia_all, rb_all = spread(dot(table_of(R, kind), mgrad.astype(BF16)) * scale, pairs)
    for j in range(PAIRS):
        lanes = slice(256 * j, 256 * j + 256)
        cols = slice(128 * j, 128 * j + 128)
        ra, ia, rb = ra_all[:, cols], ia_all[:, cols], rb_all[:, cols]
        grad = jnp.concatenate([jnp.concatenate([ra, ia], axis=1), jnp.concatenate([rb, -ia], axis=1)], axis=0)
        grad = grad * R.bent[rows, lanes].astype(F32)
        R.dbias[pl.ds(0, 8), lanes] += sum8(grad)
        grad = grad.astype(BF16)
        R.dmix[1, j] += dot(R.act[rows, lanes], grad, TN)
        yield True
        grad = dot(grad, R.wout[pl.ds(256 * j, 256), :], NT) * R.slope[rows, lanes].astype(F32)
        R.dbias[pl.ds(8, 8), lanes] += sum8(grad)
        grad = grad.astype(BF16)
        R.igrad[rows, lanes] = grad
        R.dmix[0, j] += dot(R.spec[rows, lanes], grad, TN)
        yield True


def block_result(R, slot):
    kind = kind_of(R, slot)
    rows = pl.ds(pl.multiple_of(slot * PATCHES, PATCHES), PATCHES)
    branch = R.br[rows, :] + R.vec[8:9, :]
    result = R.mid[rows, :] + branch
    R.stats[pl.ds(24, 8), :] += masked_squares(branch, kind)
    R.stats[pl.ds(32, 8), :] += masked_squares(result, kind)
    R.out[rows, :] = result.astype(BF16)
    yield True


def mixer_weight_gradients(R, put):
    for j in range(PAIRS):
        for which in range(2):
            put(which, j, pair_gradient(R.dmix[which, j]))


def mixer_backward_second(R, slot):
    kind = kind_of(R, slot)
    whole, pairs, scale = slot_facts(kind)
    rows = pl.ds(pl.multiple_of(slot * PATCHES, PATCHES), PATCHES)
    tops, bottoms = [], []
    for j in range(PAIRS):
        lanes = slice(256 * j, 256 * j + 256)
        u, v = fold(dot(R.igrad[rows, lanes], R.win[pl.ds(256 * j, 256), :], NT), pairs)
        tops.append(u.astype(BF16))
        bottoms.append(v.astype(BF16))
        yield True
    folded = jnp.concatenate([jnp.concatenate(tops, axis=1), jnp.concatenate(bottoms, axis=1)], axis=0)
    ngrad = dot(table_of(R, kind), folded, TN) * scale
    R.ngrad[rows, :] = ngrad
    xhat, _, _ = row_stats(R.tok[rows, :].astype(F32))
    yield True
    R.sums[pl.ds(24, 8), :] += sum8(ngrad * xhat)
    R.sums[pl.ds(32, 8), :] += sum8(ngrad)
    yield True


def norm_backward(R, slot):
    rows = pl.ds(pl.multiple_of(slot * PATCHES, PATCHES), PATCHES)
    xhat, xscale, _ = row_stats(R.tok[rows, :].astype(F32))
    scaled = R.ngrad[rows, :] * R.vec[0:1, :]
    yield True
    inner = scaled - jnp.mean(scaled, axis=-1, keepdims=True) - xhat * jnp.mean(scaled * xhat, axis=-1, keepdims=True)
    R.igrad_out[rows, :] = R.mgrad[rows, :] + inner * xscale
    yield True

class Refs:
    pass


VMEM = pl.BlockSpec(memory_space=pltpu.VMEM)
SMEM = pl.BlockSpec(memory_space=pltpu.SMEM)
ROOM = 127 * 2**19


def named(names, refs):
    R = Refs()
    for name, ref in zip(names, refs):
        setattr(R, name, ref)
    return R


def plain_call(body, ins, outs, scratch, name):
    names = list(ins) + list(outs) + list(scratch)

    def kernel(*refs):
        body(named(names, refs))

    values = pl.pallas_call(
        kernel,
        out_shape=[jax.ShapeDtypeStruct(*spec) for spec in outs.values()],
        in_specs=[SMEM if key == "items" else VMEM for key in ins],
        out_specs=[VMEM for _ in outs],
        scratch_shapes=[pltpu.VMEM(*spec) for spec in scratch.values()],
        compiler_params=pltpu.CompilerParams(vmem_limit_bytes=ROOM),
        name=name,
    )(*ins.values())
    return dict(zip(outs, values))


def forward_body(R):
    complex_pairs(R.inner, R.win)
    complex_pairs(R.outer, R.wout, R.wout_up)
    R.stats[...] = jnp.zeros_like(R.stats)
    R.sums[...] = jnp.zeros_like(R.sums)

    @pl.loop(0, R.tok.shape[0] // PATCHES)
    def _(slot):
        mixer_start(R, slot)
        run(mixer_forward(R, slot))


def mlp_body(R):
    R.dbe[...] = jnp.zeros_like(R.dbe)
    R.br[...] = jnp.zeros_like(R.br)
    R.fg[...] = jnp.zeros_like(R.fg)

    @pl.loop(0, R.we.shape[1] // CHUNK)
    def _(t):
        cols = pl.ds(pl.multiple_of(t * CHUNK, CHUNK), CHUNK)

        @pl.loop(0, R.feed.shape[0] // CHUNK)
        def _(i):
            run(mlp_chunk(R, i, cols, R.we[:, cols], R.wc[cols, :]))

        R.dwe[:, cols] = dot(R.feed[...], R.hgrad[...], TN).astype(BF16)
        R.dwc[:, cols] = dot(R.msk[...], R.hidden[...], TN).astype(BF16)


def backward_body(R):
    R.stats[...] = jnp.zeros_like(R.stats)
    R.sums[...] = jnp.zeros_like(R.sums)
    R.dbias[...] = jnp.zeros_like(R.dbias)
    R.dmix[...] = jnp.zeros_like(R.dmix)
    slots = R.tok.shape[0] // PATCHES

    @pl.loop(0, slots)
    def _(slot):
        run(block_result(R, slot), mixer_backward_first(R, slot))

    def put_mix(which, j, value):
        (R.dinner, R.douter)[which][pl.ds(128 * j, 128), :] = value

    mixer_weight_gradients(R, put_mix)

    @pl.loop(0, slots)
    def _(slot):
        run(chain(mixer_backward_second(R, slot), norm_backward(R, slot)))


def pair_order(vector):
    parts = vector.reshape(NB, 2, BS)
    return parts[:, 0].reshape(1, WIDTH), parts[:, 1].reshape(1, WIDTH)


def body_by_collectives(
    tokens, cotangent, slot_items, filter_gain, filter_shift, inner_weight, inner_bias, outer_weight, outer_bias,
    feed_gain, feed_shift, expand_weight, expand_bias, contract_weight, contract_bias,
):
    def gather(x):
        return lax.all_gather(x, "fsdp", axis=0, tiled=True)

    vectors = (filter_gain, filter_shift, inner_bias, outer_bias, feed_gain, feed_shift, contract_bias, expand_bias)
    sizes = [v.shape[0] for v in vectors]
    packed = lax.all_gather(jnp.concatenate(vectors), "fsdp", axis=0)
    ends = np.cumsum([0] + sizes)
    g1, s1, bi, bo, g2, s2, bc, be = [packed[:, a:b].reshape(-1).astype(F32) for a, b in zip(ends, ends[1:])]
    vec = jnp.concatenate(
        [g1[None], s1[None], *pair_order(bi), *pair_order(bo / SHRINK), g2[None], s2[None], bc[None], jnp.zeros((7, WIDTH), F32)]
    )
    inner, outer, we, wc = gather(inner_weight), gather(outer_weight), gather(expand_weight), gather(contract_weight)
    n = tokens.shape[0] * PATCHES
    hidden = we.shape[1]
    tok, cot = tokens.reshape(n, WIDTH), cotangent.reshape(n, WIDTH)
    table = jnp.asarray(TABLES, BF16)
    wide = ((n, 2 * WIDTH), BF16)
    flat = ((n, WIDTH), BF16)
    full = ((n, WIDTH), F32)
    pairs = ((2 * WIDTH, 2 * 2 * BS), BF16)
    sums = ((40, WIDTH), F32)
    a = plain_call(
        forward_body,
        dict(items=slot_items, tok=tok, cot=cot, table=table, vec=vec, inner=inner.reshape(NB, BS, 2 * BS), outer=outer.reshape(NB, BS, 2 * BS)),
        dict(spec=wide, act=wide, slope=wide, bent=wide, mid=full, feed=flat, msk=flat, win=pairs, wout=pairs, stats=sums, sums=sums),
        dict(wout_up=pairs),
        "mixer_forward",
    )
    b = plain_call(
        mlp_body,
        dict(feed=a["feed"], msk=a["msk"], we=we, wc=wc, be=be.reshape(1, hidden)),
        dict(br=full, fg=full, dwe=((WIDTH, hidden), BF16), dwc=((WIDTH, hidden), BF16), dbe=((8, hidden), F32)),
        dict(hidden=((n, CHUNK), BF16), hgrad=((n, CHUNK), BF16)),
        "mlp",
    )
    c = plain_call(
        backward_body,
        dict(
            items=slot_items, tok=tok, table=table, vec=vec, spec=a["spec"], act=a["act"], slope=a["slope"], bent=a["bent"],
            mid=a["mid"], msk=a["msk"], br=b["br"], fg=b["fg"], win=a["win"], wout=a["wout"],
        ),
        dict(
            out=flat, igrad_out=full, dinner=((WIDTH, 2 * BS), F32), douter=((WIDTH, 2 * BS), F32),
            dbias=((16, 2 * WIDTH), F32), sums=sums, stats=sums,
        ),
        dict(mgrad=full, igrad=wide, ngrad=full, dmix=((2, PAIRS, 256, 256), F32)),
        "mixer_backward",
    )

    def scatter(x):
        return lax.psum_scatter(x, "fsdp", scatter_dimension=0, tiled=True)

    def rows_of(x, at):
        return jnp.sum(x[at : at + 8], axis=0)

    def bias_of(at):
        parts = rows_of(c["dbias"], at).reshape(PAIRS, 2, 2, BS)
        return jnp.swapaxes(parts, 1, 2).reshape(2 * WIDTH)

    sums_ = a["sums"] + c["sums"]
    stats_ = a["stats"] + c["stats"]
    small = [
        rows_of(sums_, 24), rows_of(sums_, 32), bias_of(8), bias_of(0), rows_of(sums_, 0), rows_of(sums_, 8),
        rows_of(sums_, 16), jnp.sum(b["dbe"], axis=0),
    ]
    fsdp = lax.axis_size("fsdp")
    small = jnp.concatenate([v.reshape(fsdp, -1) for v in small], axis=1)
    weights = jnp.concatenate([c["dinner"].reshape(fsdp, -1), c["douter"].reshape(fsdp, -1)], axis=1)
    weights = jnp.concatenate([weights, small], axis=1).astype(BF16)
    own_small = scatter(weights.reshape(-1))
    own_we = scatter(b["dwe"])
    own_wc = scatter(b["dwc"].T)
    own_small, own_we, own_wc = lax.psum((own_small, own_we, own_wc), "rep")
    own_small = own_small.astype(F32)
    cut = inner_weight.size
    own_iw, own_ow = own_small[:cut].reshape(inner_weight.shape), own_small[cut : 2 * cut].reshape(inner_weight.shape)
    own = [own_small[2 * cut + x : 2 * cut + y] for x, y in zip(ends, ends[1:])]
    kinds = slot_items[:, None]
    valid = jnp.where((kinds == 0) | (jnp.arange(4)[None] < kinds), 1.0, 0.0)
    local = jnp.concatenate([jnp.sum(stats_.reshape(5, -1), axis=1), jnp.sum(valid)[None] * (PATCHES // 4 * WIDTH)])
    total = lax.psum(local, ("rep", "fsdp"))
    statistics = jnp.sqrt(total[:5] / total[5])
    return (
        c["out"].reshape(tokens.shape), c["igrad_out"].reshape(tokens.shape), own[0], own[1], own_iw, own[2], own_ow, own[3],
        own[4], own[5], own_we.astype(F32), own[7], own_wc.astype(F32), own[6], statistics,
    )


def specs():
    items = P(("rep", "fsdp"))
    big = P(("rep", "fsdp"), None, None)
    one, two = P("fsdp"), P("fsdp", None)
    ins = (big, big, items, one, one, two, one, two, one, one, one, two, one, two, one)
    outs = (big, big, one, one, two, one, two, one, one, one, two, one, two, one, P())
    return ins, outs


MESH = pl.DeviceIdType.MESH
AHEAD = 2
ANY = pl.BlockSpec(memory_space=pl.ANY)
FSDP = 8


def multiple(value, by):
    return pl.multiple_of(value * by, by)


class Place:
    def __init__(self, copies):
        self.z, self.f = lax.axis_index("rep"), lax.axis_index("fsdp")
        self.core, self.chip = self.f & 1, self.f >> 1
        self.copies = copies

    def peer(self, mask):
        return (self.z, self.f ^ mask)

    def floor(self, offset):
        return (lax.rem(self.z + offset, self.copies), self.f)


def remote(src, dst, send, recv, device):
    return pltpu.make_async_remote_copy(
        src_ref=src, dst_ref=dst, send_sem=send, recv_sem=recv, device_id=device, device_id_type=MESH
    )


class Sum:
    def __init__(self, place, R):
        self.p, self.R = place, R
        self.rows = R.sum_done.shape[1] // place.copies

    def copy(self, step, t, src, dst, device):
        return remote(src, dst, self.R.sum_send.at[step], self.R.sum_recv.at[step, t], device)

    def wait(self, step, t):
        view = (self.R.sum_core, self.R.sum_chips, self.R.sum_floors, self.R.sum_floors)[step].at[t]
        self.copy(step, t, view, view, self.p.peer(1)).wait_recv()

    def piece(self, floor):
        return pl.ds(multiple(floor, self.rows), self.rows)

    def offsets(self):
        return range(1, self.p.copies)

    def start(self, t):
        other = 1 - self.p.core
        self.copy(0, t, self.R.sum_own.at[t, :, other], self.R.sum_core.at[t], self.p.peer(1)).start()

    def to_chips(self, t):
        R = self.R
        self.wait(0, t)
        for k in (3, 1, 2, 0):
            at = self.p.chip ^ k
            mine = R.sum_own[t, at, self.p.core].astype(F32) + R.sum_core[t, at].astype(F32)
            R.sum_own[t, at, self.p.core] = mine.astype(BF16)
            if k:
                self.copy(1, t, R.sum_own.at[t, at, self.p.core], R.sum_chips.at[t, k - 1], self.p.peer(2 * k)).start()

    def to_floors(self, t):
        R = self.R
        self.wait(1, t)
        total = R.sum_own[t, self.p.chip, self.p.core].astype(F32)
        for k in (1, 2, 3):
            total = total + R.sum_chips[t, k - 1].astype(F32)
        R.sum_total[t] = total.astype(BF16)
        for d in self.offsets():
            device = self.p.floor(d)
            self.copy(2, t, R.sum_total.at[t, self.piece(device[0])], R.sum_floors.at[t, d - 1], device).start()

    def to_all(self, t):
        R = self.R
        self.wait(2, t)
        mine = self.piece(self.p.z)
        total = R.sum_total[t, mine, :].astype(F32)
        for d in self.offsets():
            total = total + R.sum_floors[t, d - 1].astype(F32)
        R.sum_done[t, mine, :] = total.astype(BF16)
        for d in self.offsets():
            self.copy(3, t, R.sum_done.at[t, mine], R.sum_done.at[t, mine], self.p.floor(d)).start()

    def finish(self, t):
        self.wait(3, t)

    def sent(self):
        R = self.R
        for step, view in enumerate((R.sum_core, R.sum_chips, R.sum_floors, R.sum_floors)):
            self.copy(step, 0, view, view, self.p.peer(1)).wait_send()


class Gather:
    def __init__(self, R, place):
        self.R, self.p = R, place

    def bring(self):
        R = self.R
        deep, tall = R.we_in.shape[0], R.wc_in.shape[0]
        for m in range(R.we_in.shape[1] // CHUNK):
            self.local(R.we_in.at[:, pl.ds(m * CHUNK, CHUNK)], R.hidden.at[pl.ds(m * deep, deep), :]).start()
        for t in range(R.w.shape[0]):
            self.local(R.wc_in.at[pl.ds(t * deep, deep), :], R.w.at[t, self.p.f, :, pl.ds(CHUNK, CHUNK)]).start()

    def local(self, src, dst):
        return pltpu.make_async_copy(src, dst, self.R.keep_sems.at[0])

    def lay(self):
        R = self.R
        deep, tall = R.we_in.shape[0], R.wc_in.shape[0]
        all_of = R.hidden.at[pl.ds(0, 2 * R.wc_in.shape[0]), :]
        self.local(all_of, all_of).wait()
        for t in range(0, R.w.shape[0], 2):
            for m in range(R.we_in.shape[1] // CHUNK):
                held = R.hidden[pl.ds(m * deep, deep), :].astype(F32)
                even, odd = [held[:, at + t * BS : at + t * BS + 128] for at in (0, tall)]
                for side, part in enumerate(interleave(even, odd)):
                    R.w[t + side, self.p.f, :, 128 * m : 128 * m + 128] = part.astype(BF16)

    def copy(self, t, mask, target):
        R = self.R
        view = R.w.at[t, self.p.f ^ mask]
        recv = R.gather_core if target == 1 else R.gather_chips
        return remote(view, view, R.gather_send.at[0], recv.at[t], self.p.peer(target))

    def wait(self, t, sems, count):
        view = self.R.w.at[t, pl.ds(0, count)]
        remote(view, view, self.R.gather_send.at[0], sems.at[t], self.p.peer(1)).wait_recv()

    def start(self, t):
        for target in (6, 2, 4, 1):
            self.copy(t, 0, target).start()

    def pass_on(self, t):
        self.wait(t, self.R.gather_chips, 3)
        for mask in (2, 4, 6):
            self.copy(t, mask, 1).start()

    def finish(self, t):
        self.wait(t, self.R.gather_core, 4)

    def sent(self):
        view = self.R.w.at[:, pl.ds(0, 7)]
        remote(view, view, self.R.gather_send.at[0], self.R.gather_core.at[0], self.p.peer(1)).wait_send()


def pack_small(R):
    R.small[pl.ds(0, BS), :] = R.inner_in[...]
    R.small[pl.ds(BS, BS), :] = R.outer_in[...]

    def row(*refs):
        return jnp.concatenate([ref[...].astype(F32) for ref in refs], axis=1)

    none = jnp.zeros((1, BS), F32)
    rows = [
        row(R.fg_in, R.fs_in), R.ib_in[...].astype(F32), R.ob_in[...].astype(F32), row(R.gg_in, R.gs_in),
        jnp.concatenate([R.cb_in[...].astype(F32), none], axis=1),
        R.eb_in[...].astype(F32), jnp.zeros((9, 128), F32),
    ]
    R.small[pl.ds(2 * BS, 16), :] = jnp.concatenate(rows, axis=0).astype(BF16)


def unpack_small(R):
    for j in range(PAIRS):
        cols = slice(128 * j, 128 * j + 128)
        even = R.smalls[2 * j, pl.ds(2 * BS, 16), :].astype(F32)
        odd = R.smalls[2 * j + 1, pl.ds(2 * BS, 16), :].astype(F32)
        first, second = interleave(even, odd)
        for row, (part, at) in enumerate(
            [(first, 0), (second, 0), (first, 1), (second, 1), (first, 2), (second, 2), (first, 3), (second, 3), (first, 4)]
        ):
            R.vec[row : row + 1, cols] = part[at : at + 1] * (1.0 / SHRINK if at == 2 else 1.0)
        for t in range(R.be.shape[1] // CHUNK):
            R.be[0:1, t * CHUNK + 128 * j : t * CHUNK + 128 * j + 128] = (first, second)[t % 2][5 + t // 2 : 6 + t // 2]
    complex_pairs(R.smalls.at[:, pl.ds(0, BS), :], R.win)
    complex_pairs(R.smalls.at[:, pl.ds(BS, BS), :], R.wout, R.wout_up)


def pack_sums(R):
    slots = R.tok.shape[0] // PATCHES

    def total(ref, at):
        return jnp.sum(ref[pl.ds(at, 8), :], axis=0, keepdims=True)

    feed_gain, feed_shift, contract, gain, shift = [total(R.sums, 8 * i) for i in range(5)]
    outer, inner, expand = total(R.dbias, 0), total(R.dbias, 8), total(R.dbe, 0)
    lane = lax.broadcasted_iota(jnp.int32, (1, 128), 1)
    facts = jnp.zeros((1, 128), F32)
    for i in range(5):
        facts = jnp.where(lane == i, jnp.sum(total(R.stats, 8 * i), axis=1, keepdims=True), facts)
    valid = jnp.zeros((1, 128), F32)
    for slot in range(slots):
        kind = kind_of(R, slot, 128)
        valid = valid + jnp.where(kind == 0, 4, kind).astype(F32) * float(PATCHES // 4 * WIDTH)
    facts = jnp.where(lane == 5, valid, facts)
    none = jnp.zeros((1, 128), F32)
    for j in range(PAIRS):
        cols = slice(128 * j, 128 * j + 128)
        real, imag = slice(256 * j, 256 * j + 128), slice(256 * j + 128, 256 * j + 256)
        rows = [
            interleave(gain[:, cols], shift[:, cols]),
            interleave(inner[:, real], inner[:, imag]),
            interleave(outer[:, real], outer[:, imag]),
            interleave(feed_gain[:, cols], feed_shift[:, cols]),
            interleave(contract[:, cols], none),
        ]
        for t in range(0, R.be.shape[1] // CHUNK, 2):
            low, high = [expand[:, (t + s) * CHUNK + 128 * j : (t + s) * CHUNK + 128 * j + 128] for s in range(2)]
            rows.append(interleave(low, high))
        for side in range(2):
            R.vec_own[2 * j + side] = jnp.concatenate([row[side] for row in rows] + [facts], axis=0)


class Share:
    def __init__(self, place, own, arrived, floors, sems):
        self.p, self.own, self.arrived, self.floors, self.sems = place, own, arrived, floors, sems

    def copy(self, step, src, dst, device):
        return remote(src, dst, self.sems.at[2 * step], self.sems.at[2 * step + 1], device)

    def views(self):
        return self.arrived, self.floors.at[pl.ds(0, self.p.copies - 1)]

    def wait(self, step):
        view = self.views()[step]
        self.copy(step, view, view, self.p.peer(1)).wait_recv()

    def start(self):
        for k in (6, 7, 2, 4, 3, 5, 1):
            self.copy(0, self.own.at[self.p.f ^ k], self.arrived.at[k - 1], self.p.peer(k)).start()

    def to_floors(self):
        self.wait(0)
        total = self.own[self.p.f].astype(F32)
        for k in range(1, FSDP):
            total = total + self.arrived[k - 1].astype(F32)
        self.floors[self.p.z] = total.astype(self.floors.dtype)
        mine = self.floors.at[self.p.z]
        for d in range(1, self.p.copies):
            self.copy(1, mine, mine, self.p.floor(d)).start()

    def finish(self):
        self.wait(1)
        total = self.floors[0].astype(F32)
        for z in range(1, self.p.copies):
            total = total + self.floors[z].astype(F32)
        return total

    def sent(self):
        for step, view in enumerate(self.views()):
            self.copy(step, view, view, self.p.peer(1)).wait_send()


def layer(copies, R):
    p = Place(copies)
    n = R.tok.shape[0]
    slots = n // PATCHES
    chunks = R.w.shape[0]
    blocks = n // CHUNK
    last = chunks - 1

    def loads(i):
        rows = pl.ds(multiple(i, CHUNK), CHUNK)
        return [
            pltpu.make_async_copy(src.at[rows, :], dst.at[rows, :], R.load_sems.at[i])
            for src, dst in ((R.tok_in, R.tok), (R.cot_in, R.msk))
        ]

    def loaded(i):
        both = R.tok.at[pl.ds(0, 2 * CHUNK), :]
        pltpu.make_async_copy(both, both, R.load_sems.at[i]).wait()

    stores = ((R.feed, R.out_ref), (R.fg, R.grad_ref))

    def store(which, i):
        rows = pl.ds(multiple(i, CHUNK), CHUNK)
        src, dst = stores[which]
        pltpu.make_async_copy(src.at[rows, :], dst.at[rows, :], R.store_sems.at[which]).start()

    gather = Gather(R, p)
    gather.bring()
    barrier = pltpu.get_barrier_semaphore()
    for k in range(1, FSDP):
        pl.semaphore_signal(barrier, inc=1, device_id=p.peer(k), device_id_type=MESH)
    for d in range(1, copies):
        pl.semaphore_signal(barrier, inc=1, device_id=p.floor(d), device_id_type=MESH)
    for i in range(blocks):
        for load in loads(i):
            load.start()
    R.stats[...] = jnp.zeros_like(R.stats)
    R.sums[...] = jnp.zeros_like(R.sums)
    R.dbias[...] = jnp.zeros_like(R.dbias)
    R.dbe[...] = jnp.zeros_like(R.dbe)
    R.dmix[...] = jnp.zeros_like(R.dmix)
    pack_small(R)
    R.smalls[p.f] = R.small[...]
    gather.lay()

    def begin(i):
        loaded(i)
        for side in range(CHUNK // PATCHES):
            mixer_start(R, i * (CHUNK // PATCHES) + side)

    pl.semaphore_wait(barrier, FSDP - 1 + copies - 1)

    def small_copy(dst, k):
        return remote(R.small, dst, R.small_sems.at[0], R.small_sems.at[1], p.peer(k))

    for k in (6, 7, 2, 4, 3, 5, 1):
        small_copy(R.smalls.at[p.f], k).start()
    gather.start(0)
    pl.loop(0, blocks)(begin)
    seven = R.smalls.at[pl.ds(0, FSDP - 1)]
    remote(seven, seven, R.small_sems.at[0], R.small_sems.at[1], p.peer(1)).wait_recv()
    unpack_small(R)
    sums = Sum(p, R)

    def weights(t):
        return [R.w[t, :, :, pl.ds(at, CHUNK)].reshape(-1, CHUNK) for at in (0, CHUNK)]

    def weight_gradients(t):
        for at, (left, right) in ((0, (R.feed, R.hgrad)), (CHUNK, (R.hidden, R.msk))):
            piece = dot(left[...], right[...], TN).astype(BF16)
            for k in range(FSDP):
                R.sum_own[t, k // 2, k % 2, :, at : at + CHUNK] = piece[k * BS : (k + 1) * BS]
        sums.start(t)

    def chunk_cols(t):
        return slice(t * CHUNK, (t + 1) * CHUNK)

    def two(step, i):
        return step(R, 2 * i), step(R, 2 * i + 1)

    @pl.loop(0, AHEAD)
    def _(i):
        run(*two(mixer_forward, i))

        @pl.when(i == AHEAD - 1)
        def _():
            gather.start(1)
            gather.pass_on(0)

    gather.finish(0)

    @pl.loop(AHEAD, blocks)
    def _(i):
        weave(chain(*two(mixer_forward, i)), 5, mlp_chunk(R, i - AHEAD, chunk_cols(0), *weights(0), first=True))

        @pl.when(i == blocks - 2)
        def _():
            gather.start(2)

    @pl.loop(blocks - AHEAD, blocks)
    def _(i):
        run(mlp_chunk(R, i, chunk_cols(0), *weights(0), first=True))

        @pl.when(i == blocks - AHEAD)
        def _():
            gather.start(3)
            gather.pass_on(1)

    weight_gradients(0)
    gather.finish(1)

    @pl.loop(1, last)
    def _(t):
        cols = pl.ds(multiple(t, CHUNK), CHUNK)

        @pl.loop(0, blocks)
        def _(i):
            @pl.when(i == 1)
            def _():
                sums.to_chips(t - 1)

            @pl.when((t > 1) & (i == 1))
            def _():
                sums.to_floors(t - 2)

            run(mlp_chunk(R, i, cols, *weights(t)))

            @pl.when(i == 2)
            def _():
                gather.pass_on(t + 1)

        weight_gradients(t)
        gather.finish(t + 1)

    @pl.loop(0, blocks)
    def _(i):
        @pl.when(i == 1)
        def _():
            sums.to_all(last - 3)
            sums.to_chips(last - 1)
            sums.to_floors(last - 2)

        run(mlp_front(R, i, chunk_cols(last), *weights(last)))

    weight_gradients(last)

    run(mlp_back(R, 0, *weights(last)))

    @pl.loop(1, blocks)
    def _(i):
        weave(turns(*two(mixer_backward_first, i - 1)), 4, mlp_back(R, i, *weights(last)))

        @pl.when(i == 1)
        def _():
            sums.to_chips(last)
            sums.to_floors(last - 1)
            sums.to_all(last - 2)

        @pl.when(i == blocks - 1)
        def _():
            sums.to_all(last - 1)

    run(*two(mixer_backward_first, blocks - 1))
    sums.to_floors(last)

    def put(which, j, value):
        for side in range(2):
            R.mix_own[2 * j + side, pl.ds(which * BS, BS), :] = value[side * BS : (side + 1) * BS].astype(BF16)

    mixer_weight_gradients(R, put)
    mixing = Share(p, R.mix_own, R.mix_peers, R.mix_floors, R.mix_sems)
    mixing.start()

    @pl.loop(0, blocks)
    def _(i):
        run(*two(block_result, i), *two(mixer_backward_second, i))
        store(0, i)

        @pl.when(i == 1)
        def _():
            sums.to_all(last)

    pack_sums(R)
    vectors = Share(p, R.vec_own, R.vec_peers, R.vec_floors, R.vec_sems)
    vectors.start()
    mixing.to_floors()

    @pl.loop(0, blocks)
    def _(i):
        run(*two(norm_backward, i))
        store(1, i)

    vectors.to_floors()
    for t in range(chunks):
        sums.finish(t)
    done_out = pltpu.make_async_copy(R.sum_done, R.done_ref, R.store_sems.at[2])
    done_out.start()
    R.mix_ref[...] = mixing.finish()
    R.vec_ref[...] = vectors.finish()
    remote(seven, seven, R.small_sems.at[0], R.small_sems.at[1], p.peer(1)).wait_send()
    gather.sent()
    sums.sent()
    mixing.sent()
    vectors.sent()
    for which, (src, dst) in enumerate(stores):
        pltpu.make_async_copy(src, dst, R.store_sems.at[which]).wait()
    done_out.wait()


def body_in_one(
    copies, tokens, cotangent, slot_items, filter_gain, filter_shift, inner_weight, inner_bias, outer_weight, outer_bias,
    feed_gain, feed_shift, expand_weight, expand_bias, contract_weight, contract_bias,
):
    slots = tokens.shape[0]
    n = slots * PATCHES
    deep, hidden = expand_weight.shape
    tall = contract_weight.shape[0]
    chunks = hidden // CHUNK
    floors = copies - 1
    ins = dict(
        items=slot_items, tok_in=tokens.reshape(n, WIDTH), cot_in=cotangent.reshape(n, WIDTH), table=jnp.asarray(TABLES, BF16),
        inner_in=inner_weight, outer_in=outer_weight, we_in=expand_weight, wc_in=contract_weight,
        fg_in=filter_gain[None], fs_in=filter_shift[None], ib_in=inner_bias[None], ob_in=outer_bias[None],
        gg_in=feed_gain[None], gs_in=feed_shift[None], cb_in=contract_bias[None], eb_in=expand_bias.reshape(2, 128),
    )
    places = dict.fromkeys(("tok_in", "cot_in", "we_in", "wc_in", "out_ref", "grad_ref", "done_ref"), ANY)
    places["items"] = SMEM
    outs = dict(
        out_ref=((n, WIDTH), BF16), grad_ref=((n, WIDTH), F32), done_ref=((chunks, deep, 2 * CHUNK), BF16),
        mix_ref=((2 * BS, 2 * BS), F32), vec_ref=((8, 128), F32),
    )
    wide, flat, full = ((n, 2 * WIDTH), BF16), ((n, WIDTH), BF16), ((n, WIDTH), F32)
    pairs, sums = ((2 * WIDTH, 4 * BS), BF16), ((40, WIDTH), F32)
    both = 2 * CHUNK
    memory = dict(
        tok=flat, msk=flat, spec=wide, act=wide, slope=wide, bent=wide, mid=full, feed=flat, br=full, fg=full,
        hidden=((n, CHUNK), BF16), hgrad=((n, CHUNK), BF16), w=((chunks, FSDP, deep, both), BF16),
        win=pairs, wout=pairs, wout_up=pairs, vec=((16, WIDTH), F32), be=((8, hidden), F32), stats=sums, sums=sums,
        dbias=((16, 2 * WIDTH), F32), dbe=((8, hidden), F32),
        dmix=((2, PAIRS, 256, 256), F32), small=((144, 128), BF16), smalls=((FSDP, 144, 128), BF16),
        sum_own=((chunks, 4, 2, deep, both), BF16), sum_core=((chunks, 4, deep, both), BF16),
        sum_chips=((chunks, 3, deep, both), BF16), sum_total=((chunks, deep, both), BF16),
        sum_floors=((chunks, floors, deep // copies, both), BF16), sum_done=((chunks, deep, both), BF16),
        mix_own=((FSDP, 128, 128), BF16), mix_peers=((FSDP - 1, 128, 128), BF16), mix_floors=((copies, 128, 128), BF16),
        vec_own=((FSDP, 8, 128), F32), vec_peers=((FSDP - 1, 8, 128), F32), vec_floors=((copies, 8, 128), F32),
    )
    sems = dict(
        load_sems=(n // CHUNK,), store_sems=(3,), keep_sems=(1,), small_sems=(2,), gather_send=(1,), gather_chips=(chunks,),
        gather_core=(chunks,), sum_send=(4,), sum_recv=(4, chunks), mix_sems=(4,), vec_sems=(4,),
    )
    names = list(ins) + list(outs) + list(memory) + list(sems)

    def kernel(*refs):
        R = named(names, refs)
        R.mgrad, R.out, R.igrad, R.cot = R.fg, R.feed, R.slope, R.msk
        R.ngrad, R.igrad_out = R.mid, R.fg
        layer(copies, R)

    o = dict(
        zip(
            outs,
            pl.pallas_call(
                kernel,
                out_shape=[jax.ShapeDtypeStruct(*spec) for spec in outs.values()],
                in_specs=[places.get(key, VMEM) for key in ins],
                out_specs=[places.get(key, VMEM) for key in outs],
                scratch_shapes=[pltpu.VMEM(*spec) for spec in memory.values()]
                + [pltpu.SemaphoreType.DMA(shape) for shape in sems.values()],
                compiler_params=pltpu.CompilerParams(vmem_limit_bytes=ROOM, collective_id=0, has_side_effects=True),
                name="mega",
            )(*ins.values()),
        )
    )
    return finishing(tokens.shape, o, deep, hidden, tall)


PIECES = 2


def finishing(shape, o, deep, hidden, tall):
    ends = dict(
        out=(o["out_ref"].shape, BF16), grad=(o["grad_ref"].shape, F32), fg=((1, BS), F32), fs=((1, BS), F32),
        inner=((BS, 2 * BS), F32), ib=((1, 128), F32), outer=((BS, 2 * BS), F32), ob=((1, 128), F32), gg=((1, BS), F32),
        gs=((1, BS), F32), ew=((deep, hidden), F32), eb=((2, 128), F32), cw=((tall, WIDTH), F32), cb=((1, BS), F32),
        stat=((1, 5), F32),
    )
    names = list(o) + list(ends) + ["grad_held", "out_held", "done_held", "mix_held", "vec_held", "ew_held", "cw_held", "come_sems", "go_sems", "done_sems"]

    def kernel(*refs):
        R = named(names, refs)
        def way(which, i):
            src, held, dst = ((R.grad_ref, R.grad_held, R.grad), (R.out_ref, R.out_held, R.out))[which]
            size = src.shape[0] // PIECES
            rows = pl.ds(i * size, size)
            come = pltpu.make_async_copy(src.at[rows], held.at[rows], R.come_sems.at[which, i])
            return come, pltpu.make_async_copy(held.at[rows], dst.at[rows], R.go_sems.at[which])

        smalls = [
            pltpu.make_async_copy(src, held, R.done_sems.at[i])
            for i, (src, held) in enumerate(((R.done_ref, R.done_held), (R.mix_ref, R.mix_held), (R.vec_ref, R.vec_held)))
        ]
        ways = [way(which, i) for i in range(PIECES) for which in range(2)]
        for small in smalls:
            small.start()
        for come, _ in ways:
            come.start()
        for small in smalls:
            small.wait()
        chunks, deep = R.done_ref.shape[:2]
        for t in range(0, chunks, 2):
            for m in range(CHUNK // 128):
                low, high = [R.done_held[t + side, :, 128 * m : 128 * m + 128].astype(F32) for side in range(2)]
                at = 2 * m * tall + t * BS
                for side, part in enumerate(interleave(low, high)):
                    R.ew_held[:, at + side * tall : at + side * tall + 128] = part
        for t in range(chunks):
            R.cw_held[pl.ds(t * deep, deep), :] = R.done_held[t, :, CHUNK:].astype(F32)
        ends = [
            pltpu.make_async_copy(R.ew_held, R.ew, R.done_sems.at[3]),
            pltpu.make_async_copy(R.cw_held, R.cw, R.done_sems.at[4]),
        ]
        for end in ends:
            end.start()
        R.inner[...], R.outer[...] = R.mix_held[:BS], R.mix_held[BS:]
        vec = R.vec_held[...]
        R.fg[...], R.fs[...] = vec[0:1, :BS], vec[0:1, BS:]
        R.ib[...], R.ob[...] = vec[1:2], vec[2:3]
        R.gg[...], R.gs[...] = vec[3:4, :BS], vec[3:4, BS:]
        R.cb[...], R.eb[...] = vec[4:5, :BS], vec[5:7]
        lane = lax.broadcasted_iota(jnp.int32, (1, 128), 1)
        total = jnp.sum(jnp.where(lane == 5, vec[7:8], 0.0), axis=1, keepdims=True)
        R.stat[...] = jnp.sqrt(vec[7:8] / total)[:, :5]
        for come, go in ways:
            come.wait()
            go.start()
        for which, (held, dst) in enumerate(((R.grad_held, R.grad), (R.out_held, R.out))):
            pltpu.make_async_copy(held, dst, R.go_sems.at[which]).wait()
        for end in ends:
            end.wait()

    places = dict.fromkeys(("out_ref", "grad_ref", "done_ref", "mix_ref", "vec_ref", "out", "grad", "ew", "cw"), ANY)
    values = pl.pallas_call(
        kernel,
        out_shape=[jax.ShapeDtypeStruct(*spec) for spec in ends.values()],
        in_specs=[places.get(key, VMEM) for key in o],
        out_specs=[places.get(key, VMEM) for key in ends],
        scratch_shapes=[
            pltpu.VMEM(o["grad_ref"].shape, F32), pltpu.VMEM(o["out_ref"].shape, BF16), pltpu.VMEM(o["done_ref"].shape, BF16),
            pltpu.VMEM(o["mix_ref"].shape, F32), pltpu.VMEM(o["vec_ref"].shape, F32),
            pltpu.VMEM((deep, hidden), F32), pltpu.VMEM((tall, WIDTH), F32), pltpu.SemaphoreType.DMA((2, PIECES)),
            pltpu.SemaphoreType.DMA((2,)), pltpu.SemaphoreType.DMA((5,)),
        ],
        compiler_params=pltpu.CompilerParams(vmem_limit_bytes=ROOM),
        name="finishing",
    )(*o.values())
    e = dict(zip(ends, values))
    for key in ("out", "grad"):
        e[key] = e[key].reshape(shape)
    for key in ("fg", "fs", "ib", "ob", "gg", "gs", "eb", "cb", "stat"):
        e[key] = e[key].reshape(-1)
    return tuple(e.values())


def solution(mesh):
    ins, outs = specs()
    whole = body_by_collectives
    if mesh.shape["fsdp"] == FSDP and mesh.shape["rep"] in (2, 4):
        whole = functools.partial(body_in_one, mesh.shape["rep"])
    return jax.shard_map(whole, mesh=mesh, in_specs=ins, out_specs=outs, check_vma=False)
```

```python
import functools
import math

import jax
import jax.numpy as jnp
import numpy as np
from jax import lax
from jax.experimental import pallas as pl
from jax.experimental.pallas import tpu as pltpu
from jax.sharding import PartitionSpec as P

BS = 64
NB = 8
SIDE = 16
PATCHES = SIDE * SIDE
WIDTH = NB * BS
HALF = PATCHES // 2
TAIL = 16
PAIRS = NB // 2
CHUNK = 512
EPSILON = 1e-05
SHRINK = 0.25
F32 = jnp.float32
BF16 = jnp.bfloat16
NT = (((1,), (1,)), ((), ()))
TN = (((0,), (0,)), ((), ()))
TABLE_SCALE = 1.132805


def frequency_order(side):
    pairs, selfs = [], []
    for a in range(side):
        for b in range(side):
            other = ((-a) % side, (-b) % side)
            if other == (a, b):
                selfs.append((a, b))
            elif (a, b) < other:
                pairs.append((a, b))
    return pairs, selfs


def spectrum_table(side):
    tiles = SIDE // side
    pairs, selfs = frequency_order(side)
    row = np.arange(PATCHES) // SIDE
    col = np.arange(PATCHES) % SIDE
    top, bottom = [], []
    for kind in ("pair", "self"):
        for qr in range(tiles):
            for qc in range(tiles):
                inside = (row // side == qr) & (col // side == qc)
                listed = pairs if kind == "pair" else selfs
                for at, (a, b) in enumerate(listed):
                    angle = 2.0 * math.pi / side * ((a * row + b * col) % side)
                    if kind == "pair":
                        top.append(np.where(inside, np.cos(angle), 0.0) / side)
                        bottom.append(np.where(inside, -np.sin(angle), 0.0) / side)
    extra = []
    for at in range(len(selfs)):
        for qr in range(tiles):
            for qc in range(tiles):
                inside = (row // side == qr) & (col // side == qc)
                a, b = selfs[at]
                angle = 2.0 * math.pi / side * ((a * row + b * col) % side)
                extra.append(np.where(inside, np.cos(angle), 0.0) / side)
    half = len(extra) // 2
    return np.array(top + extra[:half] + bottom + extra[half:]), len(top), tiles * tiles


WHOLE_TABLE, WHOLE_PAIRS, WHOLE_ZEROS = spectrum_table(SIDE)
PART_TABLE, PART_PAIRS, PART_ZEROS = spectrum_table(SIDE // 2)
TABLES = np.concatenate([WHOLE_TABLE * TABLE_SCALE, PART_TABLE], axis=0)


def dot(a, b, dims=(((1,), (0,)), ((), ()))):
    return lax.dot_general(a, b, dims, preferred_element_type=F32)


def sum8(values):
    return jnp.sum(values.reshape(-1, 8, values.shape[-1]), axis=0)


def gelu_and_slope(v):
    phi = 0.5 * lax.erf(v * 0.7071067811865476) + 0.5
    bell = jnp.exp2(v * v * (-0.5 / math.log(2.0))) * (1.0 / math.sqrt(2.0 * math.pi))
    return v * phi, phi + v * bell


def row_stats(values):
    mean = jnp.mean(values, axis=-1, keepdims=True)
    centre = values - mean
    spread = jnp.mean(centre * centre, axis=-1, keepdims=True)
    scale = lax.rsqrt(spread + EPSILON)
    return centre * scale, scale, spread + mean * mean


def turns(*steps):
    left = list(steps)
    while left:
        for step in list(left):
            if next(step, None) is None:
                left.remove(step)
        yield True


def run(*steps):
    for _ in turns(*steps):
        pass


def chain(*steps):
    for step in steps:
        yield from step


def weave(first, count, second):
    ended = False
    while not ended:
        for _ in range(count):
            if next(first, None) is None:
                ended = True
        next(second, None)
    for _ in second:
        pass


def kind_of(R, slot, lanes=WIDTH):
    return jnp.full((1, lanes), R.items[slot], jnp.int32)


def slot_facts(kind):
    whole = kind == 0
    pairs = jnp.where(whole, WHOLE_PAIRS, PART_PAIRS)
    scale = jnp.where(whole, 1.0 / TABLE_SCALE, 1.0).astype(F32)
    return whole, pairs, scale


def table_of(R, kind):
    whole = jnp.where(kind[:, :PATCHES] == 0, 1.0, 0.0).astype(F32)
    first, second = whole.astype(BF16), (1.0 - whole).astype(BF16)
    return R.table[pl.ds(0, PATCHES), :] * first + R.table[pl.ds(PATCHES, PATCHES), :] * second


def tail_pairs(pairs, lanes):
    row = lax.broadcasted_iota(jnp.int32, (TAIL, lanes), 0) + (HALF - TAIL)
    return row < pairs[:, :lanes]


def spread(halves, pairs):
    head = HALF - TAIL
    is_pair = tail_pairs(pairs, halves.shape[1])
    top, bottom = halves[:HALF], halves[HALF:]
    low_imag = jnp.where(is_pair, bottom[head:], 0.0)
    low_real = jnp.where(is_pair, top[head:], bottom[head:])
    imag = jnp.concatenate([bottom[:head], low_imag], axis=0)
    return top, imag, jnp.concatenate([top[:head], low_real], axis=0)


def fold(block, pairs):
    head = HALF - TAIL
    is_pair = tail_pairs(pairs, 128)
    ra, ia = block[:HALF, :128], block[:HALF, 128:]
    rb, ib = block[HALF:, :128], block[HALF:, 128:]
    top = [ra[:head] + rb[:head], ra[head:] + jnp.where(is_pair, rb[head:], 0.0)]
    bottom = [ia[:head] - ib[:head], jnp.where(is_pair, ia[head:] - ib[head:], rb[head:])]
    return jnp.concatenate(top, axis=0), jnp.concatenate(bottom, axis=0)


def interleave(first, second):
    low = lax.broadcasted_iota(jnp.int32, first.shape, 1) < BS
    return (
        jnp.where(low, first, pltpu.roll(second, BS, 1)),
        jnp.where(low, pltpu.roll(first, BS, 1), second),
    )


def complex_pairs(weight_ref, out_ref, up_ref=None):
    low = lax.broadcasted_iota(jnp.int32, (BS, 128), 1) < BS
    for j in range(PAIRS):
        first, second = weight_ref[j, 0].astype(F32), weight_ref[j, 1].astype(F32)
        real = jnp.concatenate([jnp.where(low, first, 0.0), jnp.where(low, 0.0, pltpu.roll(second, BS, 1))], axis=0)
        imag = jnp.concatenate([jnp.where(low, pltpu.roll(first, BS, 1), 0.0), jnp.where(low, 0.0, second)], axis=0)
        matrix = jnp.concatenate(
            [jnp.concatenate([real, imag], axis=1), jnp.concatenate([-imag, real], axis=1)], axis=0
        )
        out_ref[pl.ds(256 * j, 256), :] = matrix.astype(BF16)
        if up_ref is not None:
            up_ref[pl.ds(256 * j, 256), :] = (matrix * (1.0 / SHRINK)).astype(BF16)


def pair_gradient(product):
    real = product[:128, :128] + product[128:, 128:]
    imag = product[:128, 128:] - product[128:, :128]
    low = lax.broadcasted_iota(jnp.int32, (BS, 128), 1) < BS
    first = jnp.where(low, real[:BS], pltpu.roll(imag[:BS], BS, 1))
    second = jnp.where(low, pltpu.roll(real[BS:], BS, 1), imag[BS:])
    return jnp.concatenate([first, second], axis=0)


def masked_squares(values, kind):
    squares = values * values
    parts = jnp.sum(squares.reshape(2, 8, 2, 8, squares.shape[-1]), axis=1)
    total = parts[0, 0]
    for q in range(1, 4):
        valid = jnp.where((kind == 0) | (q < kind), 1.0, 0.0).astype(F32)
        total = total + valid * parts[q // 2, q % 2]
    return total


def quadrant_of(shape):
    position = lax.broadcasted_iota(jnp.int32, shape, 0)
    return (position >> 7) * 2 + ((position >> 3) & 1)


def masked(values, kind):
    kind = kind[:, : values.shape[1]]
    return jnp.where((kind == 0) | (quadrant_of(values.shape) < kind), values, 0.0)


def add_mean_squares(R, at, means, kind):
    R.stats[pl.ds(at, 8), 0:1] += sum8(masked(means, kind)) * float(WIDTH)


def mixer_start(R, slot):
    kind = kind_of(R, slot)
    whole, pairs, scale = slot_facts(kind)
    rows = pl.ds(pl.multiple_of(slot * PATCHES, PATCHES), PATCHES)
    x = R.tok[rows, :].astype(F32)
    xhat, _, means = row_stats(x)
    add_mean_squares(R, 0, means, kind)
    R.mid[rows, :] = dot(table_of(R, kind), xhat.astype(BF16))
    grad = masked(R.cot[rows, :].astype(F32), kind)
    R.sums[pl.ds(16, 8), :] += sum8(grad)
    R.msk[rows, :] = grad.astype(BF16)


def mixer_forward(R, slot):
    kind = kind_of(R, slot)
    whole, pairs, scale = slot_facts(kind)
    rows = pl.ds(pl.multiple_of(slot * PATCHES, PATCHES), PATCHES)
    spec = R.mid[rows, :] * (R.vec[0:1, :] * scale)
    row = lax.broadcasted_iota(jnp.int32, (TAIL, WIDTH), 0) + (HALF - TAIL)
    at_zero = (row >= pairs) & (row < pairs + jnp.where(whole, WHOLE_ZEROS, PART_ZEROS))
    shift = R.vec[1:2, :] * jnp.where(whole, float(SIDE), float(SIDE // 2)).astype(F32)
    zeros = spec[HALF - TAIL : HALF] + jnp.where(at_zero, shift, 0.0)
    spec = jnp.concatenate([spec[: HALF - TAIL], zeros, spec[HALF:]], axis=0)
    ra, ia, rb = [part.astype(BF16) for part in spread(spec, pairs)]
    tops, bottoms = [], []
    for j in range(PAIRS):
        lanes = slice(256 * j, 256 * j + 256)
        cols = slice(128 * j, 128 * j + 128)
        low = jnp.concatenate(
            [
                jnp.concatenate([ra[:, cols], ia[:, cols]], axis=1),
                jnp.concatenate([rb[:, cols], -ia[:, cols]], axis=1),
            ],
            axis=0,
        )
        R.spec[rows, lanes] = low
        yield True
        pre = dot(low, R.win[pl.ds(256 * j, 256), :]) + jnp.concatenate([R.vec[2:3, cols], R.vec[3:4, cols]], axis=1)
        act, slope = gelu_and_slope(pre)
        act = act.astype(BF16)
        R.act[rows, lanes] = act
        R.slope[rows, lanes] = slope.astype(BF16)
        yield True
        post = dot(act, R.wout_up[pl.ds(256 * j, 256), :]) + jnp.concatenate(
            [R.vec[4:5, cols], R.vec[5:6, cols]], axis=1
        )
        bent = jnp.tanh(post)
        R.bent[rows, lanes] = (bent * bent).astype(BF16)
        u, v = fold(post - bent, pairs)
        tops.append(u.astype(BF16))
        bottoms.append(v.astype(BF16))
    yield True
    folded = jnp.concatenate([jnp.concatenate(tops, axis=1), jnp.concatenate(bottoms, axis=1)], axis=0)
    mixer_out = dot(table_of(R, kind), folded, TN) * (scale * SHRINK)
    R.stats[pl.ds(8, 8), :] += masked_squares(mixer_out, kind)
    middle = R.tok[rows, :].astype(F32) + mixer_out
    R.mid[rows, :] = middle
    yield True
    yhat, _, means = row_stats(middle)
    add_mean_squares(R, 16, means, kind)
    R.feed[rows, :] = (yhat * R.vec[6:7, :] + R.vec[7:8, :]).astype(BF16)
    yield True


def mlp_front(R, i, cols, we, wc):
    rows = pl.ds(pl.multiple_of(i * CHUNK, CHUNK), CHUNK)
    hidden, slope = gelu_and_slope(dot(R.feed[rows, :], we) + R.be[0:1, cols])
    hidden = hidden.astype(BF16)
    R.hidden[rows, :] = hidden
    yield True
    back = dot(R.msk[rows, :], wc, NT) * slope
    R.dbe[:, cols] += sum8(back)
    back = back.astype(BF16)
    R.hgrad[rows, :] = back
    yield True


def mlp_back(R, i, we, wc, first=False):
    rows = pl.ds(pl.multiple_of(i * CHUNK, CHUNK), CHUNK)
    branch = dot(R.hidden[rows, :], wc)
    R.br[rows, :] = branch if first else R.br[rows, :] + branch
    yield True
    grad = dot(R.hgrad[rows, :], we, NT)
    R.fg[rows, :] = grad if first else R.fg[rows, :] + grad
    yield True


def mlp_chunk(R, i, cols, we, wc, first=False):
    return chain(mlp_front(R, i, cols, we, wc), mlp_back(R, i, we, wc, first))


def mixer_backward_first(R, slot):
    kind = kind_of(R, slot)
    whole, pairs, scale = slot_facts(kind)
    rows = pl.ds(pl.multiple_of(slot * PATCHES, PATCHES), PATCHES)
    feed_grad = R.fg[rows, :]
    yhat, yscale, _ = row_stats(R.mid[rows, :])
    R.sums[pl.ds(0, 8), :] += sum8(feed_grad * yhat)
    R.sums[pl.ds(8, 8), :] += sum8(feed_grad)
    scaled = feed_grad * R.vec[6:7, :]
    yield True
    inner = scaled - jnp.mean(scaled, axis=-1, keepdims=True) - yhat * jnp.mean(scaled * yhat, axis=-1, keepdims=True)
    mgrad = R.msk[rows, :].astype(F32) + inner * yscale
    R.mgrad[rows, :] = mgrad
    yield True
    ra_all, ia_all, rb_all = spread(dot(table_of(R, kind), mgrad.astype(BF16)) * scale, pairs)
    for j in range(PAIRS):
        lanes = slice(256 * j, 256 * j + 256)
        cols = slice(128 * j, 128 * j + 128)
        ra, ia, rb = ra_all[:, cols], ia_all[:, cols], rb_all[:, cols]
        grad = jnp.concatenate([jnp.concatenate([ra, ia], axis=1), jnp.concatenate([rb, -ia], axis=1)], axis=0)
        grad = grad * R.bent[rows, lanes].astype(F32)
        R.dbias[pl.ds(0, 8), lanes] += sum8(grad)
        grad = grad.astype(BF16)
        R.ograd[rows, lanes] = grad
        yield True
        grad = dot(grad, R.wout[pl.ds(256 * j, 256), :], NT) * R.slope[rows, lanes].astype(F32)
        R.dbias[pl.ds(8, 8), lanes] += sum8(grad)
        grad = grad.astype(BF16)
        R.igrad[rows, lanes] = grad
        yield True


def mixer_products(R, i, first=False):
    rows = pl.ds(pl.multiple_of(i * CHUNK, CHUNK), CHUNK)
    for j in range(PAIRS):
        lanes = slice(256 * j, 256 * j + 256)
        for which, (left, right) in enumerate(((R.spec, R.igrad), (R.act, R.ograd))):
            product = dot(left[rows, lanes], right[rows, lanes], TN)
            R.dmix[which, j] = product if first else R.dmix[which, j] + product
            yield True


def block_result(R, slot):
    kind = kind_of(R, slot)
    rows = pl.ds(pl.multiple_of(slot * PATCHES, PATCHES), PATCHES)
    branch = R.br[rows, :] + R.vec[8:9, :]
    result = R.mid[rows, :] + branch
    R.stats[pl.ds(24, 8), :] += masked_squares(branch, kind)
    R.stats[pl.ds(32, 8), :] += masked_squares(result, kind)
    R.out[rows, :] = result.astype(BF16)
    yield True


def mixer_weight_gradients(R, put):
    for j in range(PAIRS):
        for which in range(2):
            put(which, j, pair_gradient(R.dmix[which, j]))


def mixer_backward_second(R, slot):
    kind = kind_of(R, slot)
    whole, pairs, scale = slot_facts(kind)
    rows = pl.ds(pl.multiple_of(slot * PATCHES, PATCHES), PATCHES)
    tops, bottoms = [], []
    for j in range(PAIRS):
        lanes = slice(256 * j, 256 * j + 256)
        u, v = fold(dot(R.igrad[rows, lanes], R.win[pl.ds(256 * j, 256), :], NT), pairs)
        tops.append(u.astype(BF16))
        bottoms.append(v.astype(BF16))
        yield True
    folded = jnp.concatenate([jnp.concatenate(tops, axis=1), jnp.concatenate(bottoms, axis=1)], axis=0)
    ngrad = dot(table_of(R, kind), folded, TN) * scale
    R.ngrad[rows, :] = ngrad
    xhat, _, _ = row_stats(R.tok[rows, :].astype(F32))
    yield True
    R.sums[pl.ds(24, 8), :] += sum8(ngrad * xhat)
    R.sums[pl.ds(32, 8), :] += sum8(ngrad)
    yield True


def norm_backward(R, slot):
    rows = pl.ds(pl.multiple_of(slot * PATCHES, PATCHES), PATCHES)
    xhat, xscale, _ = row_stats(R.tok[rows, :].astype(F32))
    scaled = R.ngrad[rows, :] * R.vec[0:1, :]
    yield True
    inner = scaled - jnp.mean(scaled, axis=-1, keepdims=True) - xhat * jnp.mean(scaled * xhat, axis=-1, keepdims=True)
    R.igrad_out[rows, :] = R.mgrad[rows, :] + inner * xscale
    yield True

class Refs:
    pass


VMEM = pl.BlockSpec(memory_space=pltpu.VMEM)
SMEM = pl.BlockSpec(memory_space=pltpu.SMEM)
ROOM = 127 * 2**19


def named(names, refs):
    R = Refs()
    for name, ref in zip(names, refs):
        setattr(R, name, ref)
    return R


def plain_call(body, ins, outs, scratch, name):
    names = list(ins) + list(outs) + list(scratch)

    def kernel(*refs):
        body(named(names, refs))

    values = pl.pallas_call(
        kernel,
        out_shape=[jax.ShapeDtypeStruct(*spec) for spec in outs.values()],
        in_specs=[SMEM if key == "items" else VMEM for key in ins],
        out_specs=[VMEM for _ in outs],
        scratch_shapes=[pltpu.VMEM(*spec) for spec in scratch.values()],
        compiler_params=pltpu.CompilerParams(vmem_limit_bytes=ROOM),
        name=name,
    )(*ins.values())
    return dict(zip(outs, values))


def forward_body(R):
    complex_pairs(R.inner, R.win)
    complex_pairs(R.outer, R.wout, R.wout_up)
    R.stats[...] = jnp.zeros_like(R.stats)
    R.sums[...] = jnp.zeros_like(R.sums)

    @pl.loop(0, R.tok.shape[0] // PATCHES)
    def _(slot):
        mixer_start(R, slot)
        run(mixer_forward(R, slot))


def mlp_body(R):
    R.dbe[...] = jnp.zeros_like(R.dbe)
    R.br[...] = jnp.zeros_like(R.br)
    R.fg[...] = jnp.zeros_like(R.fg)

    @pl.loop(0, R.we.shape[1] // CHUNK)
    def _(t):
        cols = pl.ds(pl.multiple_of(t * CHUNK, CHUNK), CHUNK)

        @pl.loop(0, R.feed.shape[0] // CHUNK)
        def _(i):
            run(mlp_chunk(R, i, cols, R.we[:, cols], R.wc[cols, :]))

        R.dwe[:, cols] = dot(R.feed[...], R.hgrad[...], TN).astype(BF16)
        R.dwc[:, cols] = dot(R.msk[...], R.hidden[...], TN).astype(BF16)


def backward_body(R):
    R.stats[...] = jnp.zeros_like(R.stats)
    R.sums[...] = jnp.zeros_like(R.sums)
    R.dbias[...] = jnp.zeros_like(R.dbias)
    R.dmix[...] = jnp.zeros_like(R.dmix)
    slots = R.tok.shape[0] // PATCHES

    @pl.loop(0, slots)
    def _(slot):
        run(block_result(R, slot), mixer_backward_first(R, slot))

    @pl.loop(0, slots * PATCHES // CHUNK)
    def _(i):
        run(mixer_products(R, i))

    def put_mix(which, j, value):
        (R.dinner, R.douter)[which][pl.ds(128 * j, 128), :] = value

    mixer_weight_gradients(R, put_mix)

    @pl.loop(0, slots)
    def _(slot):
        run(chain(mixer_backward_second(R, slot), norm_backward(R, slot)))


def pair_order(vector):
    parts = vector.reshape(NB, 2, BS)
    return parts[:, 0].reshape(1, WIDTH), parts[:, 1].reshape(1, WIDTH)


def body_by_collectives(
    tokens, cotangent, slot_items, filter_gain, filter_shift, inner_weight, inner_bias, outer_weight, outer_bias,
    feed_gain, feed_shift, expand_weight, expand_bias, contract_weight, contract_bias,
):
    def gather(x):
        return lax.all_gather(x, "fsdp", axis=0, tiled=True)

    vectors = (filter_gain, filter_shift, inner_bias, outer_bias, feed_gain, feed_shift, contract_bias, expand_bias)
    sizes = [v.shape[0] for v in vectors]
    packed = lax.all_gather(jnp.concatenate(vectors), "fsdp", axis=0)
    ends = np.cumsum([0] + sizes)
    g1, s1, bi, bo, g2, s2, bc, be = [packed[:, a:b].reshape(-1).astype(F32) for a, b in zip(ends, ends[1:])]
    vec = jnp.concatenate(
        [g1[None], s1[None], *pair_order(bi), *pair_order(bo / SHRINK), g2[None], s2[None], bc[None], jnp.zeros((7, WIDTH), F32)]
    )
    inner, outer, we, wc = gather(inner_weight), gather(outer_weight), gather(expand_weight), gather(contract_weight)
    n = tokens.shape[0] * PATCHES
    hidden = we.shape[1]
    tok, cot = tokens.reshape(n, WIDTH), cotangent.reshape(n, WIDTH)
    table = jnp.asarray(TABLES, BF16)
    wide = ((n, 2 * WIDTH), BF16)
    flat = ((n, WIDTH), BF16)
    full = ((n, WIDTH), F32)
    pairs = ((2 * WIDTH, 2 * 2 * BS), BF16)
    sums = ((40, WIDTH), F32)
    a = plain_call(
        forward_body,
        dict(items=slot_items, tok=tok, cot=cot, table=table, vec=vec, inner=inner.reshape(PAIRS, 2, BS, 2 * BS), outer=outer.reshape(PAIRS, 2, BS, 2 * BS)),
        dict(spec=wide, act=wide, slope=wide, bent=wide, mid=full, feed=flat, msk=flat, win=pairs, wout=pairs, stats=sums, sums=sums),
        dict(wout_up=pairs),
        "mixer_forward",
    )
    b = plain_call(
        mlp_body,
        dict(feed=a["feed"], msk=a["msk"], we=we, wc=wc, be=be.reshape(1, hidden)),
        dict(br=full, fg=full, dwe=((WIDTH, hidden), BF16), dwc=((WIDTH, hidden), BF16), dbe=((8, hidden), F32)),
        dict(hidden=((n, CHUNK), BF16), hgrad=((n, CHUNK), BF16)),
        "mlp",
    )
    c = plain_call(
        backward_body,
        dict(
            items=slot_items, tok=tok, table=table, vec=vec, spec=a["spec"], act=a["act"], slope=a["slope"], bent=a["bent"],
            mid=a["mid"], msk=a["msk"], br=b["br"], fg=b["fg"], win=a["win"], wout=a["wout"],
        ),
        dict(
            out=flat, igrad_out=full, dinner=((WIDTH, 2 * BS), F32), douter=((WIDTH, 2 * BS), F32),
            dbias=((16, 2 * WIDTH), F32), sums=sums, stats=sums,
        ),
        dict(mgrad=full, ograd=wide, igrad=wide, ngrad=full, dmix=((2, PAIRS, 256, 256), F32)),
        "mixer_backward",
    )

    def scatter(x):
        return lax.psum_scatter(x, "fsdp", scatter_dimension=0, tiled=True)

    def rows_of(x, at):
        return jnp.sum(x[at : at + 8], axis=0)

    def bias_of(at):
        parts = rows_of(c["dbias"], at).reshape(PAIRS, 2, 2, BS)
        return jnp.swapaxes(parts, 1, 2).reshape(2 * WIDTH)

    sums_ = a["sums"] + c["sums"]
    stats_ = a["stats"] + c["stats"]
    small = [
        rows_of(sums_, 24), rows_of(sums_, 32), bias_of(8), bias_of(0), rows_of(sums_, 0), rows_of(sums_, 8),
        rows_of(sums_, 16), jnp.sum(b["dbe"], axis=0),
    ]
    fsdp = lax.axis_size("fsdp")
    small = jnp.concatenate([v.reshape(fsdp, -1) for v in small], axis=1)
    weights = jnp.concatenate([c["dinner"].reshape(fsdp, -1), c["douter"].reshape(fsdp, -1)], axis=1)
    weights = jnp.concatenate([weights, small], axis=1).astype(BF16)
    own_small = scatter(weights.reshape(-1))
    own_we = scatter(b["dwe"])
    own_wc = scatter(b["dwc"].T)
    own_small, own_we, own_wc = lax.psum((own_small, own_we, own_wc), "rep")
    own_small = own_small.astype(F32)
    cut = inner_weight.size
    own_iw, own_ow = own_small[:cut].reshape(inner_weight.shape), own_small[cut : 2 * cut].reshape(inner_weight.shape)
    own = [own_small[2 * cut + x : 2 * cut + y] for x, y in zip(ends, ends[1:])]
    kinds = slot_items[:, None]
    valid = jnp.where((kinds == 0) | (jnp.arange(4)[None] < kinds), 1.0, 0.0)
    local = jnp.concatenate([jnp.sum(stats_.reshape(5, -1), axis=1), jnp.sum(valid)[None] * (PATCHES // 4 * WIDTH)])
    total = lax.psum(local, ("rep", "fsdp"))
    statistics = jnp.sqrt(total[:5] / total[5])
    return (
        c["out"].reshape(tokens.shape), c["igrad_out"].reshape(tokens.shape), own[0], own[1], own_iw, own[2], own_ow, own[3],
        own[4], own[5], own_we.astype(F32), own[7], own_wc.astype(F32), own[6], statistics,
    )


def specs():
    items = P(("rep", "fsdp"))
    big = P(("rep", "fsdp"), None, None)
    one, two = P("fsdp"), P("fsdp", None)
    ins = (big, big, items, one, one, two, one, two, one, one, one, two, one, two, one)
    outs = (big, big, one, one, two, one, two, one, one, one, two, one, two, one, P())
    return ins, outs


MESH = pl.DeviceIdType.MESH
AHEAD = 2
ANY = pl.BlockSpec(memory_space=pl.ANY)
FSDP = 8


def multiple(value, by):
    return pl.multiple_of(value * by, by)


class Place:
    def __init__(self, copies):
        self.z, self.f = lax.axis_index("rep"), lax.axis_index("fsdp")
        self.core, self.chip = self.f & 1, self.f >> 1
        self.copies = copies

    def peer(self, mask):
        return (self.z, self.f ^ mask)

    def floor(self, offset):
        return (lax.rem(self.z + offset, self.copies), self.f)


def remote(src, dst, send, recv, device):
    return pltpu.make_async_remote_copy(
        src_ref=src, dst_ref=dst, send_sem=send, recv_sem=recv, device_id=device, device_id_type=MESH
    )


class Sum:
    def __init__(self, place, R):
        self.p, self.R = place, R
        self.rows = R.sum_done.shape[1] // place.copies

    def copy(self, step, t, src, dst, device):
        return remote(src, dst, self.R.sum_send.at[step], self.R.sum_recv.at[step, t], device)

    def wait(self, step, t):
        view = (self.R.sum_core, self.R.sum_chips, self.R.sum_floors, self.R.sum_floors)[step].at[t]
        self.copy(step, t, view, view, self.p.peer(1)).wait_recv()

    def piece(self, floor):
        return pl.ds(multiple(floor, self.rows), self.rows)

    def offsets(self):
        return range(1, self.p.copies)

    def start(self, t):
        other = 1 - self.p.core
        self.copy(0, t, self.R.sum_own.at[t, :, other], self.R.sum_core.at[t], self.p.peer(1)).start()

    def to_chips(self, t):
        R = self.R
        self.wait(0, t)
        for k in (3, 1, 2, 0):
            at = self.p.chip ^ k
            R.sum_own[t, at, self.p.core] = R.sum_own[t, at, self.p.core] + R.sum_core[t, at]
            if k:
                self.copy(1, t, R.sum_own.at[t, at, self.p.core], R.sum_chips.at[t, k - 1], self.p.peer(2 * k)).start()

    def to_floors(self, t):
        R = self.R
        self.wait(1, t)
        total = R.sum_own[t, self.p.chip, self.p.core].astype(F32)
        for k in (1, 2, 3):
            total = total + R.sum_chips[t, k - 1].astype(F32)
        R.sum_total[t] = total.astype(BF16)
        for d in self.offsets():
            device = self.p.floor(d)
            self.copy(2, t, R.sum_total.at[t, self.piece(device[0])], R.sum_floors.at[t, d - 1], device).start()

    def to_all(self, t):
        R = self.R
        self.wait(2, t)
        mine = self.piece(self.p.z)
        total = R.sum_total[t, mine, :].astype(F32)
        for d in self.offsets():
            total = total + R.sum_floors[t, d - 1].astype(F32)
        R.sum_done[t, mine, :] = total.astype(BF16)
        for d in self.offsets():
            self.copy(3, t, R.sum_done.at[t, mine], R.sum_done.at[t, mine], self.p.floor(d)).start()

    def finish(self, t):
        self.wait(3, t)

    def sent(self):
        R = self.R
        for step, view in enumerate((R.sum_core, R.sum_chips, R.sum_floors, R.sum_floors)):
            self.copy(step, 0, view, view, self.p.peer(1)).wait_send()


class Gather:
    def __init__(self, R, place):
        self.R, self.p = R, place

    def bring(self):
        R = self.R
        deep, tall = R.we_in.shape[0], R.wc_in.shape[0]
        for m in range(R.we_in.shape[1] // CHUNK):
            self.local(R.we_in.at[:, pl.ds(m * CHUNK, CHUNK)], R.hidden.at[pl.ds(m * deep, deep), :]).start()
        for t in range(R.w.shape[0]):
            self.local(R.wc_in.at[pl.ds(t * deep, deep), :], R.w.at[t, self.p.chip, self.p.core, :, pl.ds(CHUNK, CHUNK)]).start()

    def local(self, src, dst):
        return pltpu.make_async_copy(src, dst, self.R.keep_sems.at[0])

    def lay(self):
        R = self.R
        deep, tall = R.we_in.shape[0], R.wc_in.shape[0]
        all_of = R.hidden.at[pl.ds(0, 2 * R.wc_in.shape[0]), :]
        self.local(all_of, all_of).wait()
        for t in range(0, R.w.shape[0], 2):
            for m in range(R.we_in.shape[1] // CHUNK):
                held = R.hidden[pl.ds(m * deep, deep), :].astype(F32)
                even, odd = [held[:, at + t * BS : at + t * BS + 128] for at in (0, tall)]
                for side, part in enumerate(interleave(even, odd)):
                    R.w[t + side, self.p.chip, self.p.core, :, 128 * m : 128 * m + 128] = part.astype(BF16)

    def start(self, t):
        R, p = self.R, self.p
        view = R.w.at[t, p.chip, p.core]
        for k in (1, 2, 3):
            remote(view, view, R.gather_send.at[0], R.gather_chips.at[t], p.peer(2 * k)).start()

    def pass_on(self, t):
        R, p = self.R, self.p
        three, view = R.w.at[t, pl.ds(0, 3), 0], R.w.at[t, :, p.core]
        remote(three, three, R.gather_send.at[0], R.gather_chips.at[t], p.peer(1)).wait_recv()
        remote(view, view, R.gather_send.at[1], R.gather_core.at[t], p.peer(1)).start()

    def finish(self, t):
        R, p = self.R, self.p
        view = R.w.at[t, :, 1 - p.core]
        remote(view, view, R.gather_send.at[1], R.gather_core.at[t], p.peer(1)).wait_recv()

    def sent(self):
        R, p = self.R, self.p
        for at, view in enumerate((R.w.at[pl.ds(0, 3), :, 0], R.w.at[:, :, 0])):
            remote(view, view, R.gather_send.at[at], R.gather_core.at[0], p.peer(1)).wait_send()


class SmallGather:
    def __init__(self, R, place):
        self.R, self.p = R, place

    def way(self, view, step, device):
        return remote(view, view, self.R.small_sems.at[2 * step], self.R.small_sems.at[2 * step + 1], device)

    def start(self):
        for k in (1, 2, 3):
            self.way(self.R.smalls.at[self.p.chip, self.p.core], 0, self.p.peer(2 * k)).start()

    def pass_on(self):
        self.way(self.R.smalls.at[pl.ds(0, 3), 0], 0, self.p.peer(1)).wait_recv()
        self.way(self.R.smalls.at[:, self.p.core], 1, self.p.peer(1)).start()

    def finish(self):
        self.way(self.R.smalls.at[:, 1 - self.p.core], 1, self.p.peer(1)).wait_recv()

    def sent(self):
        self.way(self.R.smalls.at[pl.ds(0, 3), 0], 0, self.p.peer(1)).wait_send()
        self.way(self.R.smalls.at[:, 0], 1, self.p.peer(1)).wait_send()


def pack_small(R):
    R.small[pl.ds(0, BS), :] = R.inner_in[...]
    R.small[pl.ds(BS, BS), :] = R.outer_in[...]

    def row(*refs):
        return jnp.concatenate([ref[...].astype(F32) for ref in refs], axis=1)

    none = jnp.zeros((1, BS), F32)
    rows = [
        row(R.fg_in, R.fs_in), R.ib_in[...].astype(F32), R.ob_in[...].astype(F32), row(R.gg_in, R.gs_in),
        jnp.concatenate([R.cb_in[...].astype(F32), none], axis=1),
        R.eb_in[...].astype(F32), jnp.zeros((9, 128), F32),
    ]
    R.small[pl.ds(2 * BS, 16), :] = jnp.concatenate(rows, axis=0).astype(BF16)


def unpack_small(R):
    for j in range(PAIRS):
        cols = slice(128 * j, 128 * j + 128)
        even = R.smalls[j, 0, pl.ds(2 * BS, 16), :].astype(F32)
        odd = R.smalls[j, 1, pl.ds(2 * BS, 16), :].astype(F32)
        first, second = interleave(even, odd)
        for row, (part, at) in enumerate(
            [(first, 0), (second, 0), (first, 1), (second, 1), (first, 2), (second, 2), (first, 3), (second, 3), (first, 4)]
        ):
            R.vec[row : row + 1, cols] = part[at : at + 1] * (1.0 / SHRINK if at == 2 else 1.0)
        for t in range(R.be.shape[1] // CHUNK):
            R.be[0:1, t * CHUNK + 128 * j : t * CHUNK + 128 * j + 128] = (first, second)[t % 2][5 + t // 2 : 6 + t // 2]
    complex_pairs(R.smalls.at[:, :, pl.ds(0, BS), :], R.win)
    complex_pairs(R.smalls.at[:, :, pl.ds(BS, BS), :], R.wout, R.wout_up)


def pack_sums(R):
    slots = R.tok.shape[0] // PATCHES

    def total(ref, at):
        return jnp.sum(ref[pl.ds(at, 8), :], axis=0, keepdims=True)

    feed_gain, feed_shift, contract, gain, shift = [total(R.sums, 8 * i) for i in range(5)]
    outer, inner, expand = total(R.dbias, 0), total(R.dbias, 8), total(R.dbe, 0)
    lane = lax.broadcasted_iota(jnp.int32, (1, 128), 1)
    facts = jnp.zeros((1, 128), F32)
    for i in range(5):
        facts = jnp.where(lane == i, jnp.sum(total(R.stats, 8 * i), axis=1, keepdims=True), facts)
    valid = jnp.zeros((1, 128), F32)
    for slot in range(slots):
        kind = kind_of(R, slot, 128)
        valid = valid + jnp.where(kind == 0, 4, kind).astype(F32) * float(PATCHES // 4 * WIDTH)
    facts = jnp.where(lane == 5, valid, facts)
    none = jnp.zeros((1, 128), F32)
    for j in range(PAIRS):
        cols = slice(128 * j, 128 * j + 128)
        real, imag = slice(256 * j, 256 * j + 128), slice(256 * j + 128, 256 * j + 256)
        rows = [
            interleave(gain[:, cols], shift[:, cols]),
            interleave(inner[:, real], inner[:, imag]),
            interleave(outer[:, real], outer[:, imag]),
            interleave(feed_gain[:, cols], feed_shift[:, cols]),
            interleave(contract[:, cols], none),
        ]
        for t in range(0, R.be.shape[1] // CHUNK, 2):
            low, high = [expand[:, (t + s) * CHUNK + 128 * j : (t + s) * CHUNK + 128 * j + 128] for s in range(2)]
            rows.append(interleave(low, high))
        for side in range(2):
            R.vec_own[2 * j + side] = jnp.concatenate([row[side] for row in rows] + [facts], axis=0)


class Share:
    def __init__(self, place, own, arrived, floors, sems):
        self.p, self.own, self.arrived, self.floors, self.sems = place, own, arrived, floors, sems

    def copy(self, step, src, dst, device):
        return remote(src, dst, self.sems.at[2 * step], self.sems.at[2 * step + 1], device)

    def views(self):
        return self.arrived, self.floors.at[pl.ds(0, self.p.copies - 1)]

    def wait(self, step):
        view = self.views()[step]
        self.copy(step, view, view, self.p.peer(1)).wait_recv()

    def start(self):
        for k in (6, 7, 2, 4, 3, 5, 1):
            self.copy(0, self.own.at[self.p.f ^ k], self.arrived.at[k - 1], self.p.peer(k)).start()

    def to_floors(self):
        self.wait(0)
        total = self.own[self.p.f].astype(F32)
        for k in range(1, FSDP):
            total = total + self.arrived[k - 1].astype(F32)
        self.floors[self.p.z] = total.astype(self.floors.dtype)
        mine = self.floors.at[self.p.z]
        for d in range(1, self.p.copies):
            self.copy(1, mine, mine, self.p.floor(d)).start()

    def finish(self):
        self.wait(1)
        total = self.floors[0].astype(F32)
        for z in range(1, self.p.copies):
            total = total + self.floors[z].astype(F32)
        return total

    def sent(self):
        for step, view in enumerate(self.views()):
            self.copy(step, view, view, self.p.peer(1)).wait_send()


def layer(copies, R):
    p = Place(copies)
    n = R.tok.shape[0]
    slots = n // PATCHES
    chunks = R.w.shape[0]
    blocks = n // CHUNK
    last = chunks - 1

    def loads(i):
        rows = pl.ds(multiple(i, CHUNK), CHUNK)
        return [
            pltpu.make_async_copy(src.at[rows, :], dst.at[rows, :], R.load_sems.at[i])
            for src, dst in ((R.tok_in, R.tok), (R.cot_in, R.msk))
        ]

    def loaded(i):
        both = R.tok.at[pl.ds(0, 2 * CHUNK), :]
        pltpu.make_async_copy(both, both, R.load_sems.at[i]).wait()

    stores = ((R.feed, R.out_ref), (R.fg, R.grad_ref))

    def store(which, i):
        rows = pl.ds(multiple(i, CHUNK), CHUNK)
        src, dst = stores[which]
        pltpu.make_async_copy(src.at[rows, :], dst.at[rows, :], R.store_sems.at[which]).start()

    gather = Gather(R, p)
    gather.bring()
    barrier = pltpu.get_barrier_semaphore()
    for k in range(1, FSDP):
        pl.semaphore_signal(barrier, inc=1, device_id=p.peer(k), device_id_type=MESH)
    for d in range(1, copies):
        pl.semaphore_signal(barrier, inc=1, device_id=p.floor(d), device_id_type=MESH)
    for i in range(blocks):
        for load in loads(i):
            load.start()
    R.stats[...] = jnp.zeros_like(R.stats)
    R.sums[...] = jnp.zeros_like(R.sums)
    R.dbias[...] = jnp.zeros_like(R.dbias)
    R.dbe[...] = jnp.zeros_like(R.dbe)
    pack_small(R)
    R.smalls[p.chip, p.core] = R.small[...]
    gather.lay()

    def begin(i):
        loaded(i)
        for side in range(CHUNK // PATCHES):
            mixer_start(R, i * (CHUNK // PATCHES) + side)

    pl.semaphore_wait(barrier, FSDP - 1 + copies - 1)

    small = SmallGather(R, p)
    small.start()
    gather.start(0)
    pl.loop(0, blocks)(begin)
    small.pass_on()
    small.finish()
    unpack_small(R)
    sums = Sum(p, R)

    def weights(t):
        return [R.w[t, :, :, :, pl.ds(at, CHUNK)].reshape(-1, CHUNK) for at in (0, CHUNK)]

    def weight_gradients(t):
        for at, (left, right) in ((0, (R.feed, R.hgrad)), (CHUNK, (R.hidden, R.msk))):
            piece = dot(left[...], right[...], TN).astype(BF16)
            for k in range(FSDP):
                R.sum_own[t, k // 2, k % 2, :, at : at + CHUNK] = piece[k * BS : (k + 1) * BS]
        sums.start(t)

    def chunk_cols(t):
        return slice(t * CHUNK, (t + 1) * CHUNK)

    def two(step, i):
        return step(R, 2 * i), step(R, 2 * i + 1)

    @pl.loop(0, AHEAD)
    def _(i):
        run(*two(mixer_forward, i))

        @pl.when(i == AHEAD - 1)
        def _():
            gather.start(1)
            gather.pass_on(0)

    gather.finish(0)

    @pl.loop(AHEAD, blocks)
    def _(i):
        weave(chain(*two(mixer_forward, i)), 5, mlp_chunk(R, i - AHEAD, chunk_cols(0), *weights(0), first=True))

        @pl.when(i == blocks - 2)
        def _():
            gather.start(2)

    @pl.loop(blocks - AHEAD, blocks)
    def _(i):
        run(mlp_chunk(R, i, chunk_cols(0), *weights(0), first=True))

        @pl.when(i == blocks - AHEAD)
        def _():
            gather.start(3)
            gather.pass_on(1)

    weight_gradients(0)
    gather.finish(1)

    @pl.loop(1, last)
    def _(t):
        cols = pl.ds(multiple(t, CHUNK), CHUNK)

        @pl.loop(0, blocks)
        def _(i):
            @pl.when(i == 1)
            def _():
                sums.to_chips(t - 1)

            @pl.when((t > 1) & (i == 1))
            def _():
                sums.to_floors(t - 2)

            run(mlp_chunk(R, i, cols, *weights(t)))

            @pl.when(i == 2)
            def _():
                gather.pass_on(t + 1)

        weight_gradients(t)
        gather.finish(t + 1)

    @pl.loop(0, blocks)
    def _(i):
        @pl.when(i == 1)
        def _():
            sums.to_all(last - 3)
            sums.to_chips(last - 1)
            sums.to_floors(last - 2)

        run(mlp_front(R, i, chunk_cols(last), *weights(last)))

    weight_gradients(last)

    def first_back(i, *beside):
        weave(turns(*two(mixer_backward_first, i)), 1, turns(*beside))

    run(mlp_back(R, 0, *weights(last)))
    first_back(0, mlp_back(R, 1, *weights(last)))
    sums.to_chips(last)
    sums.to_floors(last - 1)
    sums.to_all(last - 2)
    first_back(1, mlp_back(R, 2, *weights(last)), mixer_products(R, 0, first=True))

    @pl.loop(3, blocks)
    def _(i):
        first_back(i - 1, mlp_back(R, i, *weights(last)), mixer_products(R, i - 2))

    sums.to_all(last - 1)
    first_back(blocks - 1, mixer_products(R, blocks - 2))
    sums.to_floors(last)
    run(mixer_products(R, blocks - 1))

    def put(which, j, value):
        for side in range(2):
            R.mix_own[2 * j + side, pl.ds(which * BS, BS), :] = value[side * BS : (side + 1) * BS].astype(BF16)

    mixer_weight_gradients(R, put)
    mixing = Share(p, R.mix_own, R.mix_peers, R.mix_floors, R.mix_sems)
    mixing.start()

    @pl.loop(0, blocks)
    def _(i):
        run(*two(block_result, i), *two(mixer_backward_second, i))
        store(0, i)

        @pl.when(i == 1)
        def _():
            sums.to_all(last)

    pack_sums(R)
    vectors = Share(p, R.vec_own, R.vec_peers, R.vec_floors, R.vec_sems)
    vectors.start()
    mixing.to_floors()

    @pl.loop(0, blocks)
    def _(i):
        run(*two(norm_backward, i))
        store(1, i)

    vectors.to_floors()
    for t in range(chunks):
        sums.finish(t)
    done_out = pltpu.make_async_copy(R.sum_done, R.done_ref, R.store_sems.at[2])
    done_out.start()
    R.mix_ref[...] = mixing.finish()
    R.vec_ref[...] = vectors.finish()
    small.sent()
    gather.sent()
    sums.sent()
    mixing.sent()
    vectors.sent()
    for which, (src, dst) in enumerate(stores):
        pltpu.make_async_copy(src, dst, R.store_sems.at[which]).wait()
    done_out.wait()


def body_in_one(
    copies, tokens, cotangent, slot_items, filter_gain, filter_shift, inner_weight, inner_bias, outer_weight, outer_bias,
    feed_gain, feed_shift, expand_weight, expand_bias, contract_weight, contract_bias,
):
    slots = tokens.shape[0]
    n = slots * PATCHES
    deep, hidden = expand_weight.shape
    tall = contract_weight.shape[0]
    chunks = hidden // CHUNK
    floors = copies - 1
    ins = dict(
        items=slot_items, tok_in=tokens.reshape(n, WIDTH), cot_in=cotangent.reshape(n, WIDTH), table=jnp.asarray(TABLES, BF16),
        inner_in=inner_weight, outer_in=outer_weight, we_in=expand_weight, wc_in=contract_weight,
        fg_in=filter_gain[None], fs_in=filter_shift[None], ib_in=inner_bias[None], ob_in=outer_bias[None],
        gg_in=feed_gain[None], gs_in=feed_shift[None], cb_in=contract_bias[None], eb_in=expand_bias.reshape(2, 128),
    )
    places = dict.fromkeys(("tok_in", "cot_in", "we_in", "wc_in", "out_ref", "grad_ref", "done_ref"), ANY)
    places["items"] = SMEM
    outs = dict(
        out_ref=((n, WIDTH), BF16), grad_ref=((n, WIDTH), F32), done_ref=((chunks, deep, 2 * CHUNK), BF16),
        mix_ref=((2 * BS, 2 * BS), F32), vec_ref=((8, 128), F32),
    )
    wide, flat, full = ((n, 2 * WIDTH), BF16), ((n, WIDTH), BF16), ((n, WIDTH), F32)
    pairs, sums = ((2 * WIDTH, 4 * BS), BF16), ((40, WIDTH), F32)
    both = 2 * CHUNK
    memory = dict(
        tok=flat, msk=flat, spec=wide, act=wide, slope=wide, bent=wide, mid=full, feed=flat, br=full, fg=full,
        hidden=((n, CHUNK), BF16), hgrad=((n, CHUNK), BF16), w=((chunks, FSDP // 2, 2, deep, both), BF16),
        win=pairs, wout=pairs, wout_up=pairs, vec=((16, WIDTH), F32), be=((8, hidden), F32), stats=sums, sums=sums,
        dbias=((16, 2 * WIDTH), F32), dbe=((8, hidden), F32),
        dmix=((2, PAIRS, 256, 256), F32), small=((144, 128), BF16), smalls=((FSDP // 2, 2, 144, 128), BF16),
        sum_own=((chunks, 4, 2, deep, both), BF16), sum_core=((chunks, 4, deep, both), BF16),
        sum_chips=((chunks, 3, deep, both), BF16), sum_total=((chunks, deep, both), BF16),
        sum_floors=((chunks, floors, deep // copies, both), BF16), sum_done=((chunks, deep, both), BF16),
        mix_own=((FSDP, 128, 128), BF16), mix_peers=((FSDP - 1, 128, 128), BF16), mix_floors=((copies, 128, 128), BF16),
        vec_own=((FSDP, 8, 128), F32), vec_peers=((FSDP - 1, 8, 128), F32), vec_floors=((copies, 8, 128), F32),
    )
    sems = dict(
        load_sems=(n // CHUNK,), store_sems=(3,), keep_sems=(1,), small_sems=(4,), gather_send=(2,), gather_chips=(chunks,),
        gather_core=(chunks,), sum_send=(4,), sum_recv=(4, chunks), mix_sems=(4,), vec_sems=(4,),
    )
    names = list(ins) + list(outs) + list(memory) + list(sems)

    def kernel(*refs):
        R = named(names, refs)
        R.mgrad, R.out, R.ograd, R.igrad, R.cot = R.fg, R.feed, R.bent, R.slope, R.msk
        R.ngrad, R.igrad_out = R.mid, R.fg
        layer(copies, R)

    o = dict(
        zip(
            outs,
            pl.pallas_call(
                kernel,
                out_shape=[jax.ShapeDtypeStruct(*spec) for spec in outs.values()],
                in_specs=[places.get(key, VMEM) for key in ins],
                out_specs=[places.get(key, VMEM) for key in outs],
                scratch_shapes=[pltpu.VMEM(*spec) for spec in memory.values()]
                + [pltpu.SemaphoreType.DMA(shape) for shape in sems.values()],
                compiler_params=pltpu.CompilerParams(vmem_limit_bytes=ROOM, collective_id=0, has_side_effects=True),
                name="mega",
            )(*ins.values()),
        )
    )
    return finishing(tokens.shape, o, deep, hidden, tall)


PIECES = 2


def finishing(shape, o, deep, hidden, tall):
    ends = dict(
        out=(o["out_ref"].shape, BF16), grad=(o["grad_ref"].shape, F32), fg=((1, BS), F32), fs=((1, BS), F32),
        inner=((BS, 2 * BS), F32), ib=((1, 128), F32), outer=((BS, 2 * BS), F32), ob=((1, 128), F32), gg=((1, BS), F32),
        gs=((1, BS), F32), ew=((deep, hidden), F32), eb=((2, 128), F32), cw=((tall, WIDTH), F32), cb=((1, BS), F32),
        stat=((1, 5), F32),
    )
    names = list(o) + list(ends) + ["grad_held", "out_held", "done_held", "mix_held", "vec_held", "ew_held", "cw_held", "come_sems", "go_sems", "done_sems"]

    def kernel(*refs):
        R = named(names, refs)
        def way(which, i):
            src, held, dst = ((R.grad_ref, R.grad_held, R.grad), (R.out_ref, R.out_held, R.out))[which]
            size = src.shape[0] // PIECES
            rows = pl.ds(i * size, size)
            come = pltpu.make_async_copy(src.at[rows], held.at[rows], R.come_sems.at[which, i])
            return come, pltpu.make_async_copy(held.at[rows], dst.at[rows], R.go_sems.at[which])

        smalls = [
            pltpu.make_async_copy(src, held, R.done_sems.at[i])
            for i, (src, held) in enumerate(((R.done_ref, R.done_held), (R.mix_ref, R.mix_held), (R.vec_ref, R.vec_held)))
        ]
        ways = [way(which, i) for i in range(PIECES) for which in range(2)]
        for small in smalls:
            small.start()
        for come, _ in ways:
            come.start()
        for small in smalls:
            small.wait()
        chunks, deep = R.done_ref.shape[:2]
        for t in range(0, chunks, 2):
            for m in range(CHUNK // 128):
                low, high = [R.done_held[t + side, :, 128 * m : 128 * m + 128].astype(F32) for side in range(2)]
                at = 2 * m * tall + t * BS
                for side, part in enumerate(interleave(low, high)):
                    R.ew_held[:, at + side * tall : at + side * tall + 128] = part
        for t in range(chunks):
            R.cw_held[pl.ds(t * deep, deep), :] = R.done_held[t, :, CHUNK:].astype(F32)
        ends = [
            pltpu.make_async_copy(R.ew_held, R.ew, R.done_sems.at[3]),
            pltpu.make_async_copy(R.cw_held, R.cw, R.done_sems.at[4]),
        ]
        for end in ends:
            end.start()
        R.inner[...], R.outer[...] = R.mix_held[:BS], R.mix_held[BS:]
        vec = R.vec_held[...]
        R.fg[...], R.fs[...] = vec[0:1, :BS], vec[0:1, BS:]
        R.ib[...], R.ob[...] = vec[1:2], vec[2:3]
        R.gg[...], R.gs[...] = vec[3:4, :BS], vec[3:4, BS:]
        R.cb[...], R.eb[...] = vec[4:5, :BS], vec[5:7]
        lane = lax.broadcasted_iota(jnp.int32, (1, 128), 1)
        total = jnp.sum(jnp.where(lane == 5, vec[7:8], 0.0), axis=1, keepdims=True)
        R.stat[...] = jnp.sqrt(vec[7:8] / total)[:, :5]
        for come, go in ways:
            come.wait()
            go.start()
        for which, (held, dst) in enumerate(((R.grad_held, R.grad), (R.out_held, R.out))):
            pltpu.make_async_copy(held, dst, R.go_sems.at[which]).wait()
        for end in ends:
            end.wait()

    places = dict.fromkeys(("out_ref", "grad_ref", "done_ref", "mix_ref", "vec_ref", "out", "grad", "ew", "cw"), ANY)
    values = pl.pallas_call(
        kernel,
        out_shape=[jax.ShapeDtypeStruct(*spec) for spec in ends.values()],
        in_specs=[places.get(key, VMEM) for key in o],
        out_specs=[places.get(key, VMEM) for key in ends],
        scratch_shapes=[
            pltpu.VMEM(o["grad_ref"].shape, F32), pltpu.VMEM(o["out_ref"].shape, BF16), pltpu.VMEM(o["done_ref"].shape, BF16),
            pltpu.VMEM(o["mix_ref"].shape, F32), pltpu.VMEM(o["vec_ref"].shape, F32),
            pltpu.VMEM((deep, hidden), F32), pltpu.VMEM((tall, WIDTH), F32), pltpu.SemaphoreType.DMA((2, PIECES)),
            pltpu.SemaphoreType.DMA((2,)), pltpu.SemaphoreType.DMA((5,)),
        ],
        compiler_params=pltpu.CompilerParams(vmem_limit_bytes=ROOM),
        name="finishing",
    )(*o.values())
    e = dict(zip(ends, values))
    for key in ("out", "grad"):
        e[key] = e[key].reshape(shape)
    for key in ("fg", "fs", "ib", "ob", "gg", "gs", "eb", "cb", "stat"):
        e[key] = e[key].reshape(-1)
    return tuple(e.values())


def solution(mesh):
    ins, outs = specs()
    whole = body_by_collectives
    if mesh.shape["fsdp"] == FSDP and mesh.shape["rep"] in (2, 4):
        whole = functools.partial(body_in_one, mesh.shape["rep"])
    return jax.shard_map(whole, mesh=mesh, in_specs=ins, out_specs=outs, check_vma=False)
```

```python
import functools
import math

import jax
import jax.numpy as jnp
import numpy as np
from jax import lax
from jax.experimental import pallas as pl
from jax.experimental.pallas import tpu as pltpu
from jax.sharding import PartitionSpec as P

BS = 64
NB = 8
SIDE = 16
PATCHES = SIDE * SIDE
WIDTH = NB * BS
HALF = PATCHES // 2
TAIL = 16
PAIRS = NB // 2
CHUNK = 512
EPSILON = 1e-05
SHRINK = 0.25
F32 = jnp.float32
BF16 = jnp.bfloat16
NT = (((1,), (1,)), ((), ()))
TN = (((0,), (0,)), ((), ()))
TABLE_SCALE = 1.132805


def frequency_order(side):
    pairs, selfs = [], []
    for a in range(side):
        for b in range(side):
            other = ((-a) % side, (-b) % side)
            if other == (a, b):
                selfs.append((a, b))
            elif (a, b) < other:
                pairs.append((a, b))
    return pairs, selfs


def spectrum_table(side):
    tiles = SIDE // side
    pairs, selfs = frequency_order(side)
    row = np.arange(PATCHES) // SIDE
    col = np.arange(PATCHES) % SIDE
    top, bottom = [], []
    for kind in ("pair", "self"):
        for qr in range(tiles):
            for qc in range(tiles):
                inside = (row // side == qr) & (col // side == qc)
                listed = pairs if kind == "pair" else selfs
                for at, (a, b) in enumerate(listed):
                    angle = 2.0 * math.pi / side * ((a * row + b * col) % side)
                    if kind == "pair":
                        top.append(np.where(inside, np.cos(angle), 0.0) / side)
                        bottom.append(np.where(inside, -np.sin(angle), 0.0) / side)
    extra = []
    for at in range(len(selfs)):
        for qr in range(tiles):
            for qc in range(tiles):
                inside = (row // side == qr) & (col // side == qc)
                a, b = selfs[at]
                angle = 2.0 * math.pi / side * ((a * row + b * col) % side)
                extra.append(np.where(inside, np.cos(angle), 0.0) / side)
    half = len(extra) // 2
    return np.array(top + extra[:half] + bottom + extra[half:]), len(top), tiles * tiles


WHOLE_TABLE, WHOLE_PAIRS, WHOLE_ZEROS = spectrum_table(SIDE)
PART_TABLE, PART_PAIRS, PART_ZEROS = spectrum_table(SIDE // 2)
TABLES = np.concatenate([WHOLE_TABLE * TABLE_SCALE, PART_TABLE], axis=0)


def dot(a, b, dims=(((1,), (0,)), ((), ()))):
    return lax.dot_general(a, b, dims, preferred_element_type=F32)


def sum8(values):
    return jnp.sum(values.reshape(-1, 8, values.shape[-1]), axis=0)


def gelu_and_slope(v):
    phi = 0.5 * lax.erf(v * 0.7071067811865476) + 0.5
    bell = jnp.exp2(v * v * (-0.5 / math.log(2.0))) * (1.0 / math.sqrt(2.0 * math.pi))
    return v * phi, phi + v * bell


def row_stats(values):
    mean = jnp.mean(values, axis=-1, keepdims=True)
    centre = values - mean
    spread = jnp.mean(centre * centre, axis=-1, keepdims=True)
    scale = lax.rsqrt(spread + EPSILON)
    return centre * scale, scale, spread + mean * mean


def turns(*steps):
    left = list(steps)
    while left:
        for step in list(left):
            if next(step, None) is None:
                left.remove(step)
        yield True


def run(*steps):
    for _ in turns(*steps):
        pass


def chain(*steps):
    for step in steps:
        yield from step


def weave(first, count, second):
    ended = False
    while not ended:
        for _ in range(count):
            if next(first, None) is None:
                ended = True
        next(second, None)
    for _ in second:
        pass


def kind_of(R, slot, lanes=WIDTH):
    return jnp.full((1, lanes), R.items[slot], jnp.int32)


def slot_facts(kind):
    whole = kind == 0
    pairs = jnp.where(whole, WHOLE_PAIRS, PART_PAIRS)
    scale = jnp.where(whole, 1.0 / TABLE_SCALE, 1.0).astype(F32)
    return whole, pairs, scale


def table_of(R, kind):
    whole = jnp.where(kind[:, :PATCHES] == 0, 1.0, 0.0).astype(F32)
    first, second = whole.astype(BF16), (1.0 - whole).astype(BF16)
    return R.table[pl.ds(0, PATCHES), :] * first + R.table[pl.ds(PATCHES, PATCHES), :] * second


def tail_pairs(pairs, lanes):
    row = lax.broadcasted_iota(jnp.int32, (TAIL, lanes), 0) + (HALF - TAIL)
    return row < pairs[:, :lanes]


def spread(halves, pairs):
    head = HALF - TAIL
    is_pair = tail_pairs(pairs, halves.shape[1])
    top, bottom = halves[:HALF], halves[HALF:]
    low_imag = jnp.where(is_pair, bottom[head:], 0.0)
    low_real = jnp.where(is_pair, top[head:], bottom[head:])
    imag = jnp.concatenate([bottom[:head], low_imag], axis=0)
    return top, imag, jnp.concatenate([top[:head], low_real], axis=0)


def fold(block, pairs):
    head = HALF - TAIL
    is_pair = tail_pairs(pairs, 128)
    ra, ia = block[:HALF, :128], block[:HALF, 128:]
    rb, ib = block[HALF:, :128], block[HALF:, 128:]
    top = [ra[:head] + rb[:head], ra[head:] + jnp.where(is_pair, rb[head:], 0.0)]
    bottom = [ia[:head] - ib[:head], jnp.where(is_pair, ia[head:] - ib[head:], rb[head:])]
    return jnp.concatenate(top, axis=0), jnp.concatenate(bottom, axis=0)


def interleave(first, second):
    low = lax.broadcasted_iota(jnp.int32, first.shape, 1) < BS
    return (
        jnp.where(low, first, pltpu.roll(second, BS, 1)),
        jnp.where(low, pltpu.roll(first, BS, 1), second),
    )


def complex_pairs(weight_ref, out_ref, up_ref=None):
    low = lax.broadcasted_iota(jnp.int32, (BS, 128), 1) < BS
    for j in range(PAIRS):
        first, second = weight_ref[j, 0].astype(F32), weight_ref[j, 1].astype(F32)
        real = jnp.concatenate([jnp.where(low, first, 0.0), jnp.where(low, 0.0, pltpu.roll(second, BS, 1))], axis=0)
        imag = jnp.concatenate([jnp.where(low, pltpu.roll(first, BS, 1), 0.0), jnp.where(low, 0.0, second)], axis=0)
        matrix = jnp.concatenate(
            [jnp.concatenate([real, imag], axis=1), jnp.concatenate([-imag, real], axis=1)], axis=0
        )
        out_ref[pl.ds(256 * j, 256), :] = matrix.astype(BF16)
        if up_ref is not None:
            up_ref[pl.ds(256 * j, 256), :] = (matrix * (1.0 / SHRINK)).astype(BF16)


def pair_gradient(product):
    real = product[:128, :128] + product[128:, 128:]
    imag = product[:128, 128:] - product[128:, :128]
    low = lax.broadcasted_iota(jnp.int32, (BS, 128), 1) < BS
    first = jnp.where(low, real[:BS], pltpu.roll(imag[:BS], BS, 1))
    second = jnp.where(low, pltpu.roll(real[BS:], BS, 1), imag[BS:])
    return jnp.concatenate([first, second], axis=0)


def masked_squares(values, kind):
    squares = values * values
    parts = jnp.sum(squares.reshape(2, 8, 2, 8, squares.shape[-1]), axis=1)
    total = parts[0, 0]
    for q in range(1, 4):
        valid = jnp.where((kind == 0) | (q < kind), 1.0, 0.0).astype(F32)
        total = total + valid * parts[q // 2, q % 2]
    return total


def quadrant_of(shape):
    position = lax.broadcasted_iota(jnp.int32, shape, 0)
    return (position >> 7) * 2 + ((position >> 3) & 1)


def masked(values, kind):
    kind = kind[:, : values.shape[1]]
    return jnp.where((kind == 0) | (quadrant_of(values.shape) < kind), values, 0.0)


def add_mean_squares(R, at, means, kind):
    R.stats[pl.ds(at, 8), 0:1] += sum8(masked(means, kind)) * float(WIDTH)


def mixer_start(R, slot):
    kind = kind_of(R, slot)
    whole, pairs, scale = slot_facts(kind)
    rows = pl.ds(pl.multiple_of(slot * PATCHES, PATCHES), PATCHES)
    x = R.tok[rows, :].astype(F32)
    xhat, _, means = row_stats(x)
    add_mean_squares(R, 0, means, kind)
    R.mid[rows, :] = dot(table_of(R, kind), xhat.astype(BF16))
    grad = masked(R.cot[rows, :].astype(F32), kind)
    R.sums[pl.ds(16, 8), :] += sum8(grad)
    R.msk[rows, :] = grad.astype(BF16)


def mixer_forward(R, slot):
    kind = kind_of(R, slot)
    whole, pairs, scale = slot_facts(kind)
    rows = pl.ds(pl.multiple_of(slot * PATCHES, PATCHES), PATCHES)
    spec = R.mid[rows, :] * (R.vec[0:1, :] * scale)
    row = lax.broadcasted_iota(jnp.int32, (TAIL, WIDTH), 0) + (HALF - TAIL)
    at_zero = (row >= pairs) & (row < pairs + jnp.where(whole, WHOLE_ZEROS, PART_ZEROS))
    shift = R.vec[1:2, :] * jnp.where(whole, float(SIDE), float(SIDE // 2)).astype(F32)
    zeros = spec[HALF - TAIL : HALF] + jnp.where(at_zero, shift, 0.0)
    spec = jnp.concatenate([spec[: HALF - TAIL], zeros, spec[HALF:]], axis=0)
    ra, ia, rb = [part.astype(BF16) for part in spread(spec, pairs)]
    tops, bottoms = [], []
    for j in range(PAIRS):
        lanes = slice(256 * j, 256 * j + 256)
        cols = slice(128 * j, 128 * j + 128)
        low = jnp.concatenate(
            [
                jnp.concatenate([ra[:, cols], ia[:, cols]], axis=1),
                jnp.concatenate([rb[:, cols], -ia[:, cols]], axis=1),
            ],
            axis=0,
        )
        R.spec[rows, lanes] = low
        yield True
        pre = dot(low, R.win[pl.ds(256 * j, 256), :]) + jnp.concatenate([R.vec[2:3, cols], R.vec[3:4, cols]], axis=1)
        act, slope = gelu_and_slope(pre)
        act = act.astype(BF16)
        R.act[rows, lanes] = act
        R.slope[rows, lanes] = slope.astype(BF16)
        yield True
        post = dot(act, R.wout_up[pl.ds(256 * j, 256), :]) + jnp.concatenate(
            [R.vec[4:5, cols], R.vec[5:6, cols]], axis=1
        )
        bent = jnp.tanh(post)
        R.bent[rows, lanes] = (bent * bent).astype(BF16)
        u, v = fold(post - bent, pairs)
        tops.append(u.astype(BF16))
        bottoms.append(v.astype(BF16))
    yield True
    folded = jnp.concatenate([jnp.concatenate(tops, axis=1), jnp.concatenate(bottoms, axis=1)], axis=0)
    mixer_out = dot(table_of(R, kind), folded, TN) * (scale * SHRINK)
    R.stats[pl.ds(8, 8), :] += masked_squares(mixer_out, kind)
    middle = R.tok[rows, :].astype(F32) + mixer_out
    R.mid[rows, :] = middle
    yield True
    yhat, _, means = row_stats(middle)
    add_mean_squares(R, 16, means, kind)
    R.feed[rows, :] = (yhat * R.vec[6:7, :] + R.vec[7:8, :]).astype(BF16)
    yield True


def mlp_front(R, i, cols, we, wc):
    rows = pl.ds(pl.multiple_of(i * CHUNK, CHUNK), CHUNK)
    hidden, slope = gelu_and_slope(dot(R.feed[rows, :], we) + R.be[0:1, cols])
    hidden = hidden.astype(BF16)
    R.hidden[rows, :] = hidden
    yield True
    back = dot(R.msk[rows, :], wc, NT) * slope
    R.dbe[:, cols] += sum8(back)
    back = back.astype(BF16)
    R.hgrad[rows, :] = back
    yield True


def mlp_back(R, i, we, wc, first=False):
    rows = pl.ds(pl.multiple_of(i * CHUNK, CHUNK), CHUNK)
    branch = dot(R.hidden[rows, :], wc)
    R.br[rows, :] = branch if first else R.br[rows, :] + branch
    yield True
    grad = dot(R.hgrad[rows, :], we, NT)
    R.fg[rows, :] = grad if first else R.fg[rows, :] + grad
    yield True


def mlp_chunk(R, i, cols, we, wc, first=False):
    return chain(mlp_front(R, i, cols, we, wc), mlp_back(R, i, we, wc, first))


def mixer_backward_first(R, slot):
    kind = kind_of(R, slot)
    whole, pairs, scale = slot_facts(kind)
    rows = pl.ds(pl.multiple_of(slot * PATCHES, PATCHES), PATCHES)
    feed_grad = R.fg[rows, :]
    yhat, yscale, _ = row_stats(R.mid[rows, :])
    R.sums[pl.ds(0, 8), :] += sum8(feed_grad * yhat)
    R.sums[pl.ds(8, 8), :] += sum8(feed_grad)
    scaled = feed_grad * R.vec[6:7, :]
    yield True
    inner = scaled - jnp.mean(scaled, axis=-1, keepdims=True) - yhat * jnp.mean(scaled * yhat, axis=-1, keepdims=True)
    mgrad = R.msk[rows, :].astype(F32) + inner * yscale
    R.mgrad[rows, :] = mgrad
    yield True
    ra_all, ia_all, rb_all = spread(dot(table_of(R, kind), mgrad.astype(BF16)) * scale, pairs)
    for j in range(PAIRS):
        lanes = slice(256 * j, 256 * j + 256)
        cols = slice(128 * j, 128 * j + 128)
        ra, ia, rb = ra_all[:, cols], ia_all[:, cols], rb_all[:, cols]
        grad = jnp.concatenate([jnp.concatenate([ra, ia], axis=1), jnp.concatenate([rb, -ia], axis=1)], axis=0)
        grad = grad * R.bent[rows, lanes].astype(F32)
        R.dbias[pl.ds(0, 8), lanes] += sum8(grad)
        grad = grad.astype(BF16)
        R.ograd[rows, lanes] = grad
        yield True
        grad = dot(grad, R.wout[pl.ds(256 * j, 256), :], NT) * R.slope[rows, lanes].astype(F32)
        R.dbias[pl.ds(8, 8), lanes] += sum8(grad)
        grad = grad.astype(BF16)
        R.igrad[rows, lanes] = grad
        yield True


def mixer_products(R, i, first=False):
    rows = pl.ds(pl.multiple_of(i * CHUNK, CHUNK), CHUNK)
    for j in range(PAIRS):
        lanes = slice(256 * j, 256 * j + 256)
        for which, (left, right) in enumerate(((R.spec, R.igrad), (R.act, R.ograd))):
            product = dot(left[rows, lanes], right[rows, lanes], TN)
            R.dmix[which, j] = product if first else R.dmix[which, j] + product
            yield True


def block_result(R, slot):
    kind = kind_of(R, slot)
    rows = pl.ds(pl.multiple_of(slot * PATCHES, PATCHES), PATCHES)
    branch = R.br[rows, :] + R.vec[8:9, :]
    result = R.mid[rows, :] + branch
    R.stats[pl.ds(24, 8), :] += masked_squares(branch, kind)
    R.stats[pl.ds(32, 8), :] += masked_squares(result, kind)
    R.out[rows, :] = result.astype(BF16)
    yield True


def mixer_weight_gradients(R, put):
    for j in range(PAIRS):
        for which in range(2):
            put(which, j, pair_gradient(R.dmix[which, j]))


def mixer_backward_second(R, slot):
    kind = kind_of(R, slot)
    whole, pairs, scale = slot_facts(kind)
    rows = pl.ds(pl.multiple_of(slot * PATCHES, PATCHES), PATCHES)
    tops, bottoms = [], []
    for j in range(PAIRS):
        lanes = slice(256 * j, 256 * j + 256)
        u, v = fold(dot(R.igrad[rows, lanes], R.win[pl.ds(256 * j, 256), :], NT), pairs)
        tops.append(u.astype(BF16))
        bottoms.append(v.astype(BF16))
        yield True
    folded = jnp.concatenate([jnp.concatenate(tops, axis=1), jnp.concatenate(bottoms, axis=1)], axis=0)
    ngrad = dot(table_of(R, kind), folded, TN) * scale
    R.ngrad[rows, :] = ngrad
    xhat, _, _ = row_stats(R.tok[rows, :].astype(F32))
    yield True
    R.sums[pl.ds(24, 8), :] += sum8(ngrad * xhat)
    R.sums[pl.ds(32, 8), :] += sum8(ngrad)
    yield True


def norm_backward(R, slot):
    rows = pl.ds(pl.multiple_of(slot * PATCHES, PATCHES), PATCHES)
    xhat, xscale, _ = row_stats(R.tok[rows, :].astype(F32))
    scaled = R.ngrad[rows, :] * R.vec[0:1, :]
    yield True
    inner = scaled - jnp.mean(scaled, axis=-1, keepdims=True) - xhat * jnp.mean(scaled * xhat, axis=-1, keepdims=True)
    R.igrad_out[rows, :] = R.mgrad[rows, :] + inner * xscale
    yield True

class Refs:
    pass


VMEM = pl.BlockSpec(memory_space=pltpu.VMEM)
SMEM = pl.BlockSpec(memory_space=pltpu.SMEM)
ROOM = 127 * 2**19


def named(names, refs):
    R = Refs()
    for name, ref in zip(names, refs):
        setattr(R, name, ref)
    return R


def plain_call(body, ins, outs, scratch, name):
    names = list(ins) + list(outs) + list(scratch)

    def kernel(*refs):
        body(named(names, refs))

    values = pl.pallas_call(
        kernel,
        out_shape=[jax.ShapeDtypeStruct(*spec) for spec in outs.values()],
        in_specs=[SMEM if key == "items" else VMEM for key in ins],
        out_specs=[VMEM for _ in outs],
        scratch_shapes=[pltpu.VMEM(*spec) for spec in scratch.values()],
        compiler_params=pltpu.CompilerParams(vmem_limit_bytes=ROOM),
        name=name,
    )(*ins.values())
    return dict(zip(outs, values))


def forward_body(R):
    complex_pairs(R.inner, R.win)
    complex_pairs(R.outer, R.wout, R.wout_up)
    R.stats[...] = jnp.zeros_like(R.stats)
    R.sums[...] = jnp.zeros_like(R.sums)

    @pl.loop(0, R.tok.shape[0] // PATCHES)
    def _(slot):
        mixer_start(R, slot)
        run(mixer_forward(R, slot))


def mlp_body(R):
    R.dbe[...] = jnp.zeros_like(R.dbe)
    R.br[...] = jnp.zeros_like(R.br)
    R.fg[...] = jnp.zeros_like(R.fg)

    @pl.loop(0, R.we.shape[1] // CHUNK)
    def _(t):
        cols = pl.ds(pl.multiple_of(t * CHUNK, CHUNK), CHUNK)

        @pl.loop(0, R.feed.shape[0] // CHUNK)
        def _(i):
            run(mlp_chunk(R, i, cols, R.we[:, cols], R.wc[cols, :]))

        R.dwe[:, cols] = dot(R.feed[...], R.hgrad[...], TN).astype(BF16)
        R.dwc[:, cols] = dot(R.msk[...], R.hidden[...], TN).astype(BF16)


def backward_body(R):
    R.stats[...] = jnp.zeros_like(R.stats)
    R.sums[...] = jnp.zeros_like(R.sums)
    R.dbias[...] = jnp.zeros_like(R.dbias)
    R.dmix[...] = jnp.zeros_like(R.dmix)
    slots = R.tok.shape[0] // PATCHES

    @pl.loop(0, slots)
    def _(slot):
        run(block_result(R, slot), mixer_backward_first(R, slot))

    @pl.loop(0, slots * PATCHES // CHUNK)
    def _(i):
        run(mixer_products(R, i))

    def put_mix(which, j, value):
        (R.dinner, R.douter)[which][pl.ds(128 * j, 128), :] = value

    mixer_weight_gradients(R, put_mix)

    @pl.loop(0, slots)
    def _(slot):
        run(chain(mixer_backward_second(R, slot), norm_backward(R, slot)))


def pair_order(vector):
    parts = vector.reshape(NB, 2, BS)
    return parts[:, 0].reshape(1, WIDTH), parts[:, 1].reshape(1, WIDTH)


def body_by_collectives(
    tokens, cotangent, slot_items, filter_gain, filter_shift, inner_weight, inner_bias, outer_weight, outer_bias,
    feed_gain, feed_shift, expand_weight, expand_bias, contract_weight, contract_bias,
):
    def gather(x):
        return lax.all_gather(x, "fsdp", axis=0, tiled=True)

    vectors = (filter_gain, filter_shift, inner_bias, outer_bias, feed_gain, feed_shift, contract_bias, expand_bias)
    sizes = [v.shape[0] for v in vectors]
    packed = lax.all_gather(jnp.concatenate(vectors), "fsdp", axis=0)
    ends = np.cumsum([0] + sizes)
    g1, s1, bi, bo, g2, s2, bc, be = [packed[:, a:b].reshape(-1).astype(F32) for a, b in zip(ends, ends[1:])]
    vec = jnp.concatenate(
        [g1[None], s1[None], *pair_order(bi), *pair_order(bo / SHRINK), g2[None], s2[None], bc[None], jnp.zeros((7, WIDTH), F32)]
    )
    inner, outer, we, wc = gather(inner_weight), gather(outer_weight), gather(expand_weight), gather(contract_weight)
    n = tokens.shape[0] * PATCHES
    hidden = we.shape[1]
    tok, cot = tokens.reshape(n, WIDTH), cotangent.reshape(n, WIDTH)
    table = jnp.asarray(TABLES, BF16)
    wide = ((n, 2 * WIDTH), BF16)
    flat = ((n, WIDTH), BF16)
    full = ((n, WIDTH), F32)
    pairs = ((2 * WIDTH, 2 * 2 * BS), BF16)
    sums = ((40, WIDTH), F32)
    a = plain_call(
        forward_body,
        dict(items=slot_items, tok=tok, cot=cot, table=table, vec=vec, inner=inner.reshape(PAIRS, 2, BS, 2 * BS), outer=outer.reshape(PAIRS, 2, BS, 2 * BS)),
        dict(spec=wide, act=wide, slope=wide, bent=wide, mid=full, feed=flat, msk=flat, win=pairs, wout=pairs, stats=sums, sums=sums),
        dict(wout_up=pairs),
        "mixer_forward",
    )
    b = plain_call(
        mlp_body,
        dict(feed=a["feed"], msk=a["msk"], we=we, wc=wc, be=be.reshape(1, hidden)),
        dict(br=full, fg=full, dwe=((WIDTH, hidden), BF16), dwc=((WIDTH, hidden), BF16), dbe=((8, hidden), F32)),
        dict(hidden=((n, CHUNK), BF16), hgrad=((n, CHUNK), BF16)),
        "mlp",
    )
    c = plain_call(
        backward_body,
        dict(
            items=slot_items, tok=tok, table=table, vec=vec, spec=a["spec"], act=a["act"], slope=a["slope"], bent=a["bent"],
            mid=a["mid"], msk=a["msk"], br=b["br"], fg=b["fg"], win=a["win"], wout=a["wout"],
        ),
        dict(
            out=flat, igrad_out=full, dinner=((WIDTH, 2 * BS), F32), douter=((WIDTH, 2 * BS), F32),
            dbias=((16, 2 * WIDTH), F32), sums=sums, stats=sums,
        ),
        dict(mgrad=full, ograd=wide, igrad=wide, ngrad=full, dmix=((2, PAIRS, 256, 256), F32)),
        "mixer_backward",
    )

    def scatter(x):
        return lax.psum_scatter(x, "fsdp", scatter_dimension=0, tiled=True)

    def rows_of(x, at):
        return jnp.sum(x[at : at + 8], axis=0)

    def bias_of(at):
        parts = rows_of(c["dbias"], at).reshape(PAIRS, 2, 2, BS)
        return jnp.swapaxes(parts, 1, 2).reshape(2 * WIDTH)

    sums_ = a["sums"] + c["sums"]
    stats_ = a["stats"] + c["stats"]
    small = [
        rows_of(sums_, 24), rows_of(sums_, 32), bias_of(8), bias_of(0), rows_of(sums_, 0), rows_of(sums_, 8),
        rows_of(sums_, 16), jnp.sum(b["dbe"], axis=0),
    ]
    fsdp = lax.axis_size("fsdp")
    small = jnp.concatenate([v.reshape(fsdp, -1) for v in small], axis=1)
    weights = jnp.concatenate([c["dinner"].reshape(fsdp, -1), c["douter"].reshape(fsdp, -1)], axis=1)
    weights = jnp.concatenate([weights, small], axis=1).astype(BF16)
    own_small = scatter(weights.reshape(-1))
    own_we = scatter(b["dwe"])
    own_wc = scatter(b["dwc"].T)
    own_small, own_we, own_wc = lax.psum((own_small, own_we, own_wc), "rep")
    own_small = own_small.astype(F32)
    cut = inner_weight.size
    own_iw, own_ow = own_small[:cut].reshape(inner_weight.shape), own_small[cut : 2 * cut].reshape(inner_weight.shape)
    own = [own_small[2 * cut + x : 2 * cut + y] for x, y in zip(ends, ends[1:])]
    kinds = slot_items[:, None]
    valid = jnp.where((kinds == 0) | (jnp.arange(4)[None] < kinds), 1.0, 0.0)
    local = jnp.concatenate([jnp.sum(stats_.reshape(5, -1), axis=1), jnp.sum(valid)[None] * (PATCHES // 4 * WIDTH)])
    total = lax.psum(local, ("rep", "fsdp"))
    statistics = jnp.sqrt(total[:5] / total[5])
    return (
        c["out"].reshape(tokens.shape), c["igrad_out"].reshape(tokens.shape), own[0], own[1], own_iw, own[2], own_ow, own[3],
        own[4], own[5], own_we.astype(F32), own[7], own_wc.astype(F32), own[6], statistics,
    )


def specs():
    items = P(("rep", "fsdp"))
    big = P(("rep", "fsdp"), None, None)
    one, two = P("fsdp"), P("fsdp", None)
    ins = (big, big, items, one, one, two, one, two, one, one, one, two, one, two, one)
    outs = (big, big, one, one, two, one, two, one, one, one, two, one, two, one, P())
    return ins, outs


MESH = pl.DeviceIdType.MESH
AHEAD = 2
ANY = pl.BlockSpec(memory_space=pl.ANY)
FSDP = 8


def multiple(value, by):
    return pl.multiple_of(value * by, by)


class Place:
    def __init__(self, copies):
        self.z, self.f = lax.axis_index("rep"), lax.axis_index("fsdp")
        self.core, self.chip = self.f & 1, self.f >> 1
        self.copies = copies

    def peer(self, mask):
        return (self.z, self.f ^ mask)

    def floor(self, offset):
        return (lax.rem(self.z + offset, self.copies), self.f)


def remote(src, dst, send, recv, device):
    return pltpu.make_async_remote_copy(
        src_ref=src, dst_ref=dst, send_sem=send, recv_sem=recv, device_id=device, device_id_type=MESH
    )


class Sum:
    def __init__(self, place, R):
        self.p, self.R = place, R
        self.rows = R.sum_done.shape[1] // place.copies

    def copy(self, step, t, src, dst, device):
        return remote(src, dst, self.R.sum_send.at[step], self.R.sum_recv.at[step, t], device)

    def wait(self, step, t):
        view = (self.R.sum_core, self.R.sum_chips, self.R.sum_floors, self.R.sum_floors)[step].at[t]
        self.copy(step, t, view, view, self.p.peer(1)).wait_recv()

    def piece(self, floor):
        return pl.ds(multiple(floor, self.rows), self.rows)

    def offsets(self):
        return range(1, self.p.copies)

    def start(self, t):
        other = 1 - self.p.core
        self.copy(0, t, self.R.sum_own.at[t, :, other], self.R.sum_core.at[t], self.p.peer(1)).start()

    def to_chips(self, t):
        R = self.R
        self.wait(0, t)
        for k in (3, 1, 2, 0):
            at = self.p.chip ^ k
            R.sum_own[t, at, self.p.core] = R.sum_own[t, at, self.p.core] + R.sum_core[t, at]
            if k:
                self.copy(1, t, R.sum_own.at[t, at, self.p.core], R.sum_chips.at[t, k - 1], self.p.peer(2 * k)).start()

    def to_floors(self, t):
        R = self.R
        self.wait(1, t)
        total = R.sum_own[t, self.p.chip, self.p.core].astype(F32)
        for k in (1, 2, 3):
            total = total + R.sum_chips[t, k - 1].astype(F32)
        R.sum_total[t] = total.astype(BF16)
        for d in self.offsets():
            device = self.p.floor(d)
            self.copy(2, t, R.sum_total.at[t, self.piece(device[0])], R.sum_floors.at[t, d - 1], device).start()

    def to_all(self, t):
        R = self.R
        self.wait(2, t)
        mine = self.piece(self.p.z)
        total = R.sum_total[t, mine, :].astype(F32)
        for d in self.offsets():
            total = total + R.sum_floors[t, d - 1].astype(F32)
        R.sum_done[t, mine, :] = total.astype(BF16)
        for d in self.offsets():
            self.copy(3, t, R.sum_done.at[t, mine], R.sum_done.at[t, mine], self.p.floor(d)).start()

    def finish(self, t):
        self.wait(3, t)

    def sent(self):
        R = self.R
        for step, view in enumerate((R.sum_core, R.sum_chips, R.sum_floors, R.sum_floors)):
            self.copy(step, 0, view, view, self.p.peer(1)).wait_send()


class Gather:
    def __init__(self, R, place):
        self.R, self.p = R, place

    def bring(self):
        R = self.R
        deep, tall = R.we_in.shape[0], R.wc_in.shape[0]
        for m in range(R.we_in.shape[1] // CHUNK):
            self.local(R.we_in.at[:, pl.ds(m * CHUNK, CHUNK)], R.hidden.at[pl.ds(m * deep, deep), :]).start()
        for t in range(R.w.shape[0]):
            self.local(R.wc_in.at[pl.ds(t * deep, deep), :], R.w.at[t, self.p.chip, self.p.core, :, pl.ds(CHUNK, CHUNK)]).start()

    def local(self, src, dst):
        return pltpu.make_async_copy(src, dst, self.R.keep_sems.at[0])

    def lay(self):
        R = self.R
        deep, tall = R.we_in.shape[0], R.wc_in.shape[0]
        all_of = R.hidden.at[pl.ds(0, 2 * R.wc_in.shape[0]), :]
        self.local(all_of, all_of).wait()
        for t in range(0, R.w.shape[0], 2):
            for m in range(R.we_in.shape[1] // CHUNK):
                held = R.hidden[pl.ds(m * deep, deep), :].astype(F32)
                even, odd = [held[:, at + t * BS : at + t * BS + 128] for at in (0, tall)]
                for side, part in enumerate(interleave(even, odd)):
                    R.w[t + side, self.p.chip, self.p.core, :, 128 * m : 128 * m + 128] = part.astype(BF16)

    def start(self, t):
        R, p = self.R, self.p
        view = R.w.at[t, p.chip, p.core]
        for k in (1, 2, 3):
            remote(view, view, R.gather_send.at[0], R.gather_chips.at[t], p.peer(2 * k)).start()

    def pass_on(self, t):
        R, p = self.R, self.p
        three, view = R.w.at[t, pl.ds(0, 3), 0], R.w.at[t, :, p.core]
        remote(three, three, R.gather_send.at[0], R.gather_chips.at[t], p.peer(1)).wait_recv()
        remote(view, view, R.gather_send.at[1], R.gather_core.at[t], p.peer(1)).start()

    def finish(self, t):
        R, p = self.R, self.p
        view = R.w.at[t, :, 1 - p.core]
        remote(view, view, R.gather_send.at[1], R.gather_core.at[t], p.peer(1)).wait_recv()

    def sent(self):
        R, p = self.R, self.p
        for at, view in enumerate((R.w.at[pl.ds(0, 3), :, 0], R.w.at[:, :, 0])):
            remote(view, view, R.gather_send.at[at], R.gather_core.at[0], p.peer(1)).wait_send()


class SmallGather:
    def __init__(self, R, place):
        self.R, self.p = R, place

    def way(self, view, step, device):
        return remote(view, view, self.R.small_sems.at[2 * step], self.R.small_sems.at[2 * step + 1], device)

    def start(self):
        for k in (1, 2, 3):
            self.way(self.R.smalls.at[self.p.chip, self.p.core], 0, self.p.peer(2 * k)).start()

    def pass_on(self):
        self.way(self.R.smalls.at[pl.ds(0, 3), 0], 0, self.p.peer(1)).wait_recv()
        self.way(self.R.smalls.at[:, self.p.core], 1, self.p.peer(1)).start()

    def finish(self):
        self.way(self.R.smalls.at[:, 1 - self.p.core], 1, self.p.peer(1)).wait_recv()

    def sent(self):
        self.way(self.R.smalls.at[pl.ds(0, 3), 0], 0, self.p.peer(1)).wait_send()
        self.way(self.R.smalls.at[:, 0], 1, self.p.peer(1)).wait_send()


def pack_small(R):
    R.small[pl.ds(0, BS), :] = R.inner_in[...]
    R.small[pl.ds(BS, BS), :] = R.outer_in[...]

    def row(*refs):
        return jnp.concatenate([ref[...].astype(F32) for ref in refs], axis=1)

    none = jnp.zeros((1, BS), F32)
    rows = [
        row(R.fg_in, R.fs_in), R.ib_in[...].astype(F32), R.ob_in[...].astype(F32), row(R.gg_in, R.gs_in),
        jnp.concatenate([R.cb_in[...].astype(F32), none], axis=1),
        R.eb_in[...].astype(F32), jnp.zeros((9, 128), F32),
    ]
    R.small[pl.ds(2 * BS, 16), :] = jnp.concatenate(rows, axis=0).astype(BF16)


def unpack_small(R):
    for j in range(PAIRS):
        cols = slice(128 * j, 128 * j + 128)
        even = R.smalls[j, 0, pl.ds(2 * BS, 16), :].astype(F32)
        odd = R.smalls[j, 1, pl.ds(2 * BS, 16), :].astype(F32)
        first, second = interleave(even, odd)
        for row, (part, at) in enumerate(
            [(first, 0), (second, 0), (first, 1), (second, 1), (first, 2), (second, 2), (first, 3), (second, 3), (first, 4)]
        ):
            R.vec[row : row + 1, cols] = part[at : at + 1] * (1.0 / SHRINK if at == 2 else 1.0)
        for t in range(R.be.shape[1] // CHUNK):
            R.be[0:1, t * CHUNK + 128 * j : t * CHUNK + 128 * j + 128] = (first, second)[t % 2][5 + t // 2 : 6 + t // 2]
    complex_pairs(R.smalls.at[:, :, pl.ds(0, BS), :], R.win)
    complex_pairs(R.smalls.at[:, :, pl.ds(BS, BS), :], R.wout, R.wout_up)


def pack_sums(R):
    slots = R.tok.shape[0] // PATCHES

    def total(ref, at):
        return jnp.sum(ref[pl.ds(at, 8), :], axis=0, keepdims=True)

    feed_gain, feed_shift, contract, gain, shift = [total(R.sums, 8 * i) for i in range(5)]
    outer, inner, expand = total(R.dbias, 0), total(R.dbias, 8), total(R.dbe, 0)
    lane = lax.broadcasted_iota(jnp.int32, (1, 128), 1)
    facts = jnp.zeros((1, 128), F32)
    for i in range(5):
        facts = jnp.where(lane == i, jnp.sum(total(R.stats, 8 * i), axis=1, keepdims=True), facts)
    valid = jnp.zeros((1, 128), F32)
    for slot in range(slots):
        kind = kind_of(R, slot, 128)
        valid = valid + jnp.where(kind == 0, 4, kind).astype(F32) * float(PATCHES // 4 * WIDTH)
    facts = jnp.where(lane == 5, valid, facts)
    none = jnp.zeros((1, 128), F32)
    for j in range(PAIRS):
        cols = slice(128 * j, 128 * j + 128)
        real, imag = slice(256 * j, 256 * j + 128), slice(256 * j + 128, 256 * j + 256)
        rows = [
            interleave(gain[:, cols], shift[:, cols]),
            interleave(inner[:, real], inner[:, imag]),
            interleave(outer[:, real], outer[:, imag]),
            interleave(feed_gain[:, cols], feed_shift[:, cols]),
            interleave(contract[:, cols], none),
        ]
        for t in range(0, R.be.shape[1] // CHUNK, 2):
            low, high = [expand[:, (t + s) * CHUNK + 128 * j : (t + s) * CHUNK + 128 * j + 128] for s in range(2)]
            rows.append(interleave(low, high))
        for side in range(2):
            R.vec_own[2 * j + side] = jnp.concatenate([row[side] for row in rows] + [facts], axis=0)


class Share:
    def __init__(self, place, own, arrived, floors, sems):
        self.p, self.own, self.arrived, self.floors, self.sems = place, own, arrived, floors, sems

    def copy(self, step, src, dst, device):
        return remote(src, dst, self.sems.at[2 * step], self.sems.at[2 * step + 1], device)

    def views(self):
        return self.arrived, self.floors.at[pl.ds(0, self.p.copies - 1)]

    def wait(self, step):
        view = self.views()[step]
        self.copy(step, view, view, self.p.peer(1)).wait_recv()

    def start(self):
        for k in (6, 7, 2, 4, 3, 5, 1):
            self.copy(0, self.own.at[self.p.f ^ k], self.arrived.at[k - 1], self.p.peer(k)).start()

    def to_floors(self):
        self.wait(0)
        total = self.own[self.p.f].astype(F32)
        for k in range(1, FSDP):
            total = total + self.arrived[k - 1].astype(F32)
        self.floors[self.p.z] = total.astype(self.floors.dtype)
        mine = self.floors.at[self.p.z]
        for d in range(1, self.p.copies):
            self.copy(1, mine, mine, self.p.floor(d)).start()

    def finish(self):
        self.wait(1)
        total = self.floors[0].astype(F32)
        for z in range(1, self.p.copies):
            total = total + self.floors[z].astype(F32)
        return total

    def sent(self):
        for step, view in enumerate(self.views()):
            self.copy(step, view, view, self.p.peer(1)).wait_send()


def layer(copies, R):
    p = Place(copies)
    n = R.tok.shape[0]
    slots = n // PATCHES
    chunks = R.w.shape[0]
    blocks = n // CHUNK
    last = chunks - 1

    def loads(i):
        rows = pl.ds(multiple(i, CHUNK), CHUNK)
        return [
            pltpu.make_async_copy(src.at[rows, :], dst.at[rows, :], R.load_sems.at[i])
            for src, dst in ((R.tok_in, R.tok), (R.cot_in, R.msk))
        ]

    def loaded(i):
        both = R.tok.at[pl.ds(0, 2 * CHUNK), :]
        pltpu.make_async_copy(both, both, R.load_sems.at[i]).wait()

    stores = ((R.feed, R.out_ref), (R.fg, R.grad_ref))

    def store(which, i):
        rows = pl.ds(multiple(i, CHUNK), CHUNK)
        src, dst = stores[which]
        pltpu.make_async_copy(src.at[rows, :], dst.at[rows, :], R.store_sems.at[which]).start()

    gather = Gather(R, p)
    gather.bring()
    barrier = pltpu.get_barrier_semaphore()
    for k in range(1, FSDP):
        pl.semaphore_signal(barrier, inc=1, device_id=p.peer(k), device_id_type=MESH)
    for d in range(1, copies):
        pl.semaphore_signal(barrier, inc=1, device_id=p.floor(d), device_id_type=MESH)
    for i in range(blocks):
        for load in loads(i):
            load.start()
    R.stats[...] = jnp.zeros_like(R.stats)
    R.sums[...] = jnp.zeros_like(R.sums)
    R.dbias[...] = jnp.zeros_like(R.dbias)
    R.dbe[...] = jnp.zeros_like(R.dbe)
    pack_small(R)
    R.smalls[p.chip, p.core] = R.small[...]
    gather.lay()

    def begin(i):
        loaded(i)
        for side in range(CHUNK // PATCHES):
            mixer_start(R, i * (CHUNK // PATCHES) + side)

    pl.semaphore_wait(barrier, FSDP - 1 + copies - 1)

    small = SmallGather(R, p)
    small.start()
    gather.start(0)
    pl.loop(0, blocks)(begin)
    small.pass_on()
    small.finish()
    unpack_small(R)
    sums = Sum(p, R)

    def weights(t):
        return [R.w[t, :, :, :, pl.ds(at, CHUNK)].reshape(-1, CHUNK) for at in (0, CHUNK)]

    def weight_gradients(t):
        for at, (left, right) in ((0, (R.feed, R.hgrad)), (CHUNK, (R.hidden, R.msk))):
            piece = dot(left[...], right[...], TN).astype(BF16)
            for k in range(FSDP):
                R.sum_own[t, k // 2, k % 2, :, at : at + CHUNK] = piece[k * BS : (k + 1) * BS]
        sums.start(t)

    def chunk_cols(t):
        return slice(t * CHUNK, (t + 1) * CHUNK)

    def two(step, i):
        return step(R, 2 * i), step(R, 2 * i + 1)

    @pl.loop(0, AHEAD)
    def _(i):
        run(*two(mixer_forward, i))

        @pl.when(i == AHEAD - 1)
        def _():
            gather.start(1)
            gather.pass_on(0)

    gather.finish(0)

    @pl.loop(AHEAD, blocks)
    def _(i):
        weave(chain(*two(mixer_forward, i)), 5, mlp_chunk(R, i - AHEAD, chunk_cols(0), *weights(0), first=True))

        @pl.when(i == blocks - 2)
        def _():
            gather.start(2)

    @pl.loop(blocks - AHEAD, blocks)
    def _(i):
        run(mlp_chunk(R, i, chunk_cols(0), *weights(0), first=True))

        @pl.when(i == blocks - AHEAD)
        def _():
            gather.start(3)
            gather.pass_on(1)

    weight_gradients(0)
    gather.finish(1)

    @pl.loop(1, last)
    def _(t):
        cols = pl.ds(multiple(t, CHUNK), CHUNK)

        @pl.loop(0, blocks)
        def _(i):
            @pl.when(i == 1)
            def _():
                sums.to_chips(t - 1)

            @pl.when((t > 1) & (i == 3))
            def _():
                sums.to_floors(t - 2)

            run(mlp_chunk(R, i, cols, *weights(t)))

            @pl.when(i == 2)
            def _():
                gather.pass_on(t + 1)

        weight_gradients(t)
        gather.finish(t + 1)

    @pl.loop(0, blocks)
    def _(i):
        @pl.when(i == 1)
        def _():
            sums.to_chips(last - 1)

        @pl.when(i == 2)
        def _():
            sums.to_all(last - 3)

        @pl.when(i == 3)
        def _():
            sums.to_floors(last - 2)

        run(mlp_front(R, i, chunk_cols(last), *weights(last)))

    weight_gradients(last)

    def first_back(i, *beside):
        weave(turns(*two(mixer_backward_first, i)), 1, turns(*beside))

    run(mlp_back(R, 0, *weights(last)))
    first_back(0, mlp_back(R, 1, *weights(last)))
    sums.to_chips(last)
    sums.to_floors(last - 1)
    first_back(1, mlp_back(R, 2, *weights(last)), mixer_products(R, 0, first=True))

    sums.to_all(last - 2)

    @pl.loop(3, blocks)
    def _(i):
        first_back(i - 1, mlp_back(R, i, *weights(last)), mixer_products(R, i - 2))

    sums.to_all(last - 1)
    first_back(blocks - 1, mixer_products(R, blocks - 2))
    sums.to_floors(last)
    run(mixer_products(R, blocks - 1))

    def put(which, j, value):
        for side in range(2):
            R.mix_own[2 * j + side, pl.ds(which * BS, BS), :] = value[side * BS : (side + 1) * BS].astype(BF16)

    mixer_weight_gradients(R, put)
    mixing = Share(p, R.mix_own, R.mix_peers, R.mix_floors, R.mix_sems)
    mixing.start()

    @pl.loop(0, blocks)
    def _(i):
        run(*two(block_result, i), *two(mixer_backward_second, i))
        store(0, i)

        @pl.when(i == 1)
        def _():
            sums.to_all(last)

    pack_sums(R)
    vectors = Share(p, R.vec_own, R.vec_peers, R.vec_floors, R.vec_sems)
    vectors.start()
    mixing.to_floors()

    @pl.loop(0, blocks)
    def _(i):
        run(*two(norm_backward, i))
        store(1, i)

    vectors.to_floors()
    for t in range(chunks):
        sums.finish(t)
    done_out = pltpu.make_async_copy(R.sum_done, R.done_ref, R.store_sems.at[2])
    done_out.start()
    R.mix_ref[...] = mixing.finish()
    R.vec_ref[...] = vectors.finish()
    small.sent()
    gather.sent()
    sums.sent()
    mixing.sent()
    vectors.sent()
    for which, (src, dst) in enumerate(stores):
        pltpu.make_async_copy(src, dst, R.store_sems.at[which]).wait()
    done_out.wait()


def body_in_one(
    copies, tokens, cotangent, slot_items, filter_gain, filter_shift, inner_weight, inner_bias, outer_weight, outer_bias,
    feed_gain, feed_shift, expand_weight, expand_bias, contract_weight, contract_bias,
):
    slots = tokens.shape[0]
    n = slots * PATCHES
    deep, hidden = expand_weight.shape
    tall = contract_weight.shape[0]
    chunks = hidden // CHUNK
    floors = copies - 1
    ins = dict(
        items=slot_items, tok_in=tokens.reshape(n, WIDTH), cot_in=cotangent.reshape(n, WIDTH), table=jnp.asarray(TABLES, BF16),
        inner_in=inner_weight, outer_in=outer_weight, we_in=expand_weight, wc_in=contract_weight,
        fg_in=filter_gain[None], fs_in=filter_shift[None], ib_in=inner_bias[None], ob_in=outer_bias[None],
        gg_in=feed_gain[None], gs_in=feed_shift[None], cb_in=contract_bias[None], eb_in=expand_bias.reshape(2, 128),
    )
    places = dict.fromkeys(("tok_in", "cot_in", "we_in", "wc_in", "out_ref", "grad_ref", "done_ref"), ANY)
    places["items"] = SMEM
    outs = dict(
        out_ref=((n, WIDTH), BF16), grad_ref=((n, WIDTH), F32), done_ref=((chunks, deep, 2 * CHUNK), BF16),
        mix_ref=((2 * BS, 2 * BS), F32), vec_ref=((8, 128), F32),
    )
    wide, flat, full = ((n, 2 * WIDTH), BF16), ((n, WIDTH), BF16), ((n, WIDTH), F32)
    pairs, sums = ((2 * WIDTH, 4 * BS), BF16), ((40, WIDTH), F32)
    both = 2 * CHUNK
    memory = dict(
        tok=flat, msk=flat, spec=wide, act=wide, slope=wide, bent=wide, mid=full, feed=flat, br=full, fg=full,
        hidden=((n, CHUNK), BF16), hgrad=((n, CHUNK), BF16), w=((chunks, FSDP // 2, 2, deep, both), BF16),
        win=pairs, wout=pairs, wout_up=pairs, vec=((16, WIDTH), F32), be=((8, hidden), F32), stats=sums, sums=sums,
        dbias=((16, 2 * WIDTH), F32), dbe=((8, hidden), F32),
        dmix=((2, PAIRS, 256, 256), F32), small=((144, 128), BF16), smalls=((FSDP // 2, 2, 144, 128), BF16),
        sum_own=((chunks, 4, 2, deep, both), BF16), sum_core=((chunks, 4, deep, both), BF16),
        sum_chips=((chunks, 3, deep, both), BF16), sum_total=((chunks, deep, both), BF16),
        sum_floors=((chunks, floors, deep // copies, both), BF16), sum_done=((chunks, deep, both), BF16),
        mix_own=((FSDP, 128, 128), BF16), mix_peers=((FSDP - 1, 128, 128), BF16), mix_floors=((copies, 128, 128), BF16),
        vec_own=((FSDP, 8, 128), F32), vec_peers=((FSDP - 1, 8, 128), F32), vec_floors=((copies, 8, 128), F32),
    )
    sems = dict(
        load_sems=(n // CHUNK,), store_sems=(3,), keep_sems=(1,), small_sems=(4,), gather_send=(2,), gather_chips=(chunks,),
        gather_core=(chunks,), sum_send=(4,), sum_recv=(4, chunks), mix_sems=(4,), vec_sems=(4,),
    )
    names = list(ins) + list(outs) + list(memory) + list(sems)

    def kernel(*refs):
        R = named(names, refs)
        R.mgrad, R.out, R.ograd, R.igrad, R.cot = R.fg, R.feed, R.bent, R.slope, R.msk
        R.ngrad, R.igrad_out = R.mid, R.fg
        layer(copies, R)

    o = dict(
        zip(
            outs,
            pl.pallas_call(
                kernel,
                out_shape=[jax.ShapeDtypeStruct(*spec) for spec in outs.values()],
                in_specs=[places.get(key, VMEM) for key in ins],
                out_specs=[places.get(key, VMEM) for key in outs],
                scratch_shapes=[pltpu.VMEM(*spec) for spec in memory.values()]
                + [pltpu.SemaphoreType.DMA(shape) for shape in sems.values()],
                compiler_params=pltpu.CompilerParams(vmem_limit_bytes=ROOM, collective_id=0, has_side_effects=True),
                name="mega",
            )(*ins.values()),
        )
    )
    return finishing(tokens.shape, o, deep, hidden, tall)


PIECES = 1


def finishing(shape, o, deep, hidden, tall):
    ends = dict(
        out=(o["out_ref"].shape, BF16), grad=(o["grad_ref"].shape, F32), fg=((1, BS), F32), fs=((1, BS), F32),
        inner=((BS, 2 * BS), F32), ib=((1, 128), F32), outer=((BS, 2 * BS), F32), ob=((1, 128), F32), gg=((1, BS), F32),
        gs=((1, BS), F32), ew=((deep, hidden), F32), eb=((2, 128), F32), cw=((tall, WIDTH), F32), cb=((1, BS), F32),
        stat=((1, 5), F32),
    )
    names = list(o) + list(ends) + ["grad_held", "out_held", "done_held", "mix_held", "vec_held", "ew_held", "cw_held", "come_sems", "go_sems", "done_sems"]

    def kernel(*refs):
        R = named(names, refs)
        def way(which, i):
            src, held, dst = ((R.grad_ref, R.grad_held, R.grad), (R.out_ref, R.out_held, R.out))[which]
            size = src.shape[0] // PIECES
            rows = pl.ds(i * size, size)
            come = pltpu.make_async_copy(src.at[rows], held.at[rows], R.come_sems.at[which, i])
            return come, pltpu.make_async_copy(held.at[rows], dst.at[rows], R.go_sems.at[which])

        smalls = [
            pltpu.make_async_copy(src, held, R.done_sems.at[i])
            for i, (src, held) in enumerate(((R.done_ref, R.done_held), (R.mix_ref, R.mix_held), (R.vec_ref, R.vec_held)))
        ]
        ways = [way(which, i) for i in range(PIECES) for which in range(2)]
        for small in smalls:
            small.start()
        for come, _ in ways:
            come.start()
        for small in smalls:
            small.wait()
        chunks, deep = R.done_ref.shape[:2]
        for t in range(0, chunks, 2):
            for m in range(CHUNK // 128):
                low, high = [R.done_held[t + side, :, 128 * m : 128 * m + 128].astype(F32) for side in range(2)]
                at = 2 * m * tall + t * BS
                for side, part in enumerate(interleave(low, high)):
                    R.ew_held[:, at + side * tall : at + side * tall + 128] = part
        for t in range(chunks):
            R.cw_held[pl.ds(t * deep, deep), :] = R.done_held[t, :, CHUNK:].astype(F32)
        ends = [
            pltpu.make_async_copy(R.ew_held, R.ew, R.done_sems.at[3]),
            pltpu.make_async_copy(R.cw_held, R.cw, R.done_sems.at[4]),
        ]
        for end in ends:
            end.start()
        R.inner[...], R.outer[...] = R.mix_held[:BS], R.mix_held[BS:]
        vec = R.vec_held[...]
        R.fg[...], R.fs[...] = vec[0:1, :BS], vec[0:1, BS:]
        R.ib[...], R.ob[...] = vec[1:2], vec[2:3]
        R.gg[...], R.gs[...] = vec[3:4, :BS], vec[3:4, BS:]
        R.cb[...], R.eb[...] = vec[4:5, :BS], vec[5:7]
        lane = lax.broadcasted_iota(jnp.int32, (1, 128), 1)
        total = jnp.sum(jnp.where(lane == 5, vec[7:8], 0.0), axis=1, keepdims=True)
        R.stat[...] = jnp.sqrt(vec[7:8] / total)[:, :5]
        for come, go in ways:
            come.wait()
            go.start()
        for which, (held, dst) in enumerate(((R.grad_held, R.grad), (R.out_held, R.out))):
            pltpu.make_async_copy(held, dst, R.go_sems.at[which]).wait()
        for end in ends:
            end.wait()

    places = dict.fromkeys(("out_ref", "grad_ref", "done_ref", "mix_ref", "vec_ref", "out", "grad", "ew", "cw"), ANY)
    values = pl.pallas_call(
        kernel,
        out_shape=[jax.ShapeDtypeStruct(*spec) for spec in ends.values()],
        in_specs=[places.get(key, VMEM) for key in o],
        out_specs=[places.get(key, VMEM) for key in ends],
        scratch_shapes=[
            pltpu.VMEM(o["grad_ref"].shape, F32), pltpu.VMEM(o["out_ref"].shape, BF16), pltpu.VMEM(o["done_ref"].shape, BF16),
            pltpu.VMEM(o["mix_ref"].shape, F32), pltpu.VMEM(o["vec_ref"].shape, F32),
            pltpu.VMEM((deep, hidden), F32), pltpu.VMEM((tall, WIDTH), F32), pltpu.SemaphoreType.DMA((2, PIECES)),
            pltpu.SemaphoreType.DMA((2,)), pltpu.SemaphoreType.DMA((5,)),
        ],
        compiler_params=pltpu.CompilerParams(vmem_limit_bytes=ROOM),
        name="finishing",
    )(*o.values())
    e = dict(zip(ends, values))
    for key in ("out", "grad"):
        e[key] = e[key].reshape(shape)
    for key in ("fg", "fs", "ib", "ob", "gg", "gs", "eb", "cb", "stat"):
        e[key] = e[key].reshape(-1)
    return tuple(e.values())


def solution(mesh):
    ins, outs = specs()
    whole = body_by_collectives
    if mesh.shape["fsdp"] == FSDP and mesh.shape["rep"] in (2, 4):
        whole = functools.partial(body_in_one, mesh.shape["rep"])
    return jax.shard_map(whole, mesh=mesh, in_specs=ins, out_specs=outs, check_vma=False)
```

```python
import functools
import math

import jax
import jax.numpy as jnp
import numpy as np
from jax import lax
from jax.experimental import pallas as pl
from jax.experimental.pallas import tpu as pltpu
from jax.sharding import PartitionSpec as P

BS = 64
NB = 8
SIDE = 16
PATCHES = SIDE * SIDE
WIDTH = NB * BS
HALF = PATCHES // 2
TAIL = 16
PAIRS = NB // 2
CHUNK = 512
EPSILON = 1e-05
SHRINK = 0.25
F32 = jnp.float32
BF16 = jnp.bfloat16
NT = (((1,), (1,)), ((), ()))
TN = (((0,), (0,)), ((), ()))
TABLE_SCALE = 1.132805


def frequency_order(side):
    pairs, selfs = [], []
    for a in range(side):
        for b in range(side):
            other = ((-a) % side, (-b) % side)
            if other == (a, b):
                selfs.append((a, b))
            elif (a, b) < other:
                pairs.append((a, b))
    return pairs, selfs


def spectrum_table(side):
    tiles = SIDE // side
    pairs, selfs = frequency_order(side)
    row = np.arange(PATCHES) // SIDE
    col = np.arange(PATCHES) % SIDE
    top, bottom = [], []
    for kind in ("pair", "self"):
        for qr in range(tiles):
            for qc in range(tiles):
                inside = (row // side == qr) & (col // side == qc)
                listed = pairs if kind == "pair" else selfs
                for at, (a, b) in enumerate(listed):
                    angle = 2.0 * math.pi / side * ((a * row + b * col) % side)
                    if kind == "pair":
                        top.append(np.where(inside, np.cos(angle), 0.0) / side)
                        bottom.append(np.where(inside, -np.sin(angle), 0.0) / side)
    extra = []
    for at in range(len(selfs)):
        for qr in range(tiles):
            for qc in range(tiles):
                inside = (row // side == qr) & (col // side == qc)
                a, b = selfs[at]
                angle = 2.0 * math.pi / side * ((a * row + b * col) % side)
                extra.append(np.where(inside, np.cos(angle), 0.0) / side)
    half = len(extra) // 2
    return np.array(top + extra[:half] + bottom + extra[half:]), len(top), tiles * tiles


WHOLE_TABLE, WHOLE_PAIRS, WHOLE_ZEROS = spectrum_table(SIDE)
PART_TABLE, PART_PAIRS, PART_ZEROS = spectrum_table(SIDE // 2)
TABLES = np.concatenate([WHOLE_TABLE * TABLE_SCALE, PART_TABLE], axis=0)


def dot(a, b, dims=(((1,), (0,)), ((), ()))):
    return lax.dot_general(a, b, dims, preferred_element_type=F32)


def sum8(values):
    return jnp.sum(values.reshape(-1, 8, values.shape[-1]), axis=0)


def gelu_and_slope(v):
    phi = 0.5 * lax.erf(v * 0.7071067811865476) + 0.5
    bell = jnp.exp2(v * v * (-0.5 / math.log(2.0))) * (1.0 / math.sqrt(2.0 * math.pi))
    return v * phi, phi + v * bell


def row_stats(values):
    mean = jnp.mean(values, axis=-1, keepdims=True)
    centre = values - mean
    spread = jnp.mean(centre * centre, axis=-1, keepdims=True)
    scale = lax.rsqrt(spread + EPSILON)
    return centre * scale, scale, spread + mean * mean


def turns(*steps):
    left = list(steps)
    while left:
        for step in list(left):
            if next(step, None) is None:
                left.remove(step)
        yield True


def run(*steps):
    for _ in turns(*steps):
        pass


def chain(*steps):
    for step in steps:
        yield from step


def weave(first, count, second):
    ended = False
    while not ended:
        for _ in range(count):
            if next(first, None) is None:
                ended = True
        next(second, None)
    for _ in second:
        pass


def kind_of(R, slot, lanes=WIDTH):
    return jnp.full((1, lanes), R.items[slot], jnp.int32)


def slot_facts(kind):
    whole = kind == 0
    pairs = jnp.where(whole, WHOLE_PAIRS, PART_PAIRS)
    scale = jnp.where(whole, 1.0 / TABLE_SCALE, 1.0).astype(F32)
    return whole, pairs, scale


def table_of(R, kind):
    whole = jnp.where(kind[:, :PATCHES] == 0, 1.0, 0.0).astype(F32)
    first, second = whole.astype(BF16), (1.0 - whole).astype(BF16)
    return R.table[pl.ds(0, PATCHES), :] * first + R.table[pl.ds(PATCHES, PATCHES), :] * second


def tail_pairs(pairs, lanes):
    row = lax.broadcasted_iota(jnp.int32, (TAIL, lanes), 0) + (HALF - TAIL)
    return row < pairs[:, :lanes]


def spread(halves, pairs):
    head = HALF - TAIL
    is_pair = tail_pairs(pairs, halves.shape[1])
    top, bottom = halves[:HALF], halves[HALF:]
    low_imag = jnp.where(is_pair, bottom[head:], 0.0)
    low_real = jnp.where(is_pair, top[head:], bottom[head:])
    imag = jnp.concatenate([bottom[:head], low_imag], axis=0)
    return top, imag, jnp.concatenate([top[:head], low_real], axis=0)


def fold(block, pairs):
    head = HALF - TAIL
    is_pair = tail_pairs(pairs, 128)
    ra, ia = block[:HALF, :128], block[:HALF, 128:]
    rb, ib = block[HALF:, :128], block[HALF:, 128:]
    top = [ra[:head] + rb[:head], ra[head:] + jnp.where(is_pair, rb[head:], 0.0)]
    bottom = [ia[:head] - ib[:head], jnp.where(is_pair, ia[head:] - ib[head:], rb[head:])]
    return jnp.concatenate(top, axis=0), jnp.concatenate(bottom, axis=0)


def interleave(first, second):
    low = lax.broadcasted_iota(jnp.int32, first.shape, 1) < BS
    return (
        jnp.where(low, first, pltpu.roll(second, BS, 1)),
        jnp.where(low, pltpu.roll(first, BS, 1), second),
    )


def complex_pairs(weight_ref, out_ref, up_ref=None):
    low = lax.broadcasted_iota(jnp.int32, (BS, 128), 1) < BS
    for j in range(PAIRS):
        first, second = weight_ref[j, 0].astype(F32), weight_ref[j, 1].astype(F32)
        real = jnp.concatenate([jnp.where(low, first, 0.0), jnp.where(low, 0.0, pltpu.roll(second, BS, 1))], axis=0)
        imag = jnp.concatenate([jnp.where(low, pltpu.roll(first, BS, 1), 0.0), jnp.where(low, 0.0, second)], axis=0)
        matrix = jnp.concatenate(
            [jnp.concatenate([real, imag], axis=1), jnp.concatenate([-imag, real], axis=1)], axis=0
        )
        out_ref[pl.ds(256 * j, 256), :] = matrix.astype(BF16)
        if up_ref is not None:
            up_ref[pl.ds(256 * j, 256), :] = (matrix * (1.0 / SHRINK)).astype(BF16)


def pair_gradient(product):
    real = product[:128, :128] + product[128:, 128:]
    imag = product[:128, 128:] - product[128:, :128]
    low = lax.broadcasted_iota(jnp.int32, (BS, 128), 1) < BS
    first = jnp.where(low, real[:BS], pltpu.roll(imag[:BS], BS, 1))
    second = jnp.where(low, pltpu.roll(real[BS:], BS, 1), imag[BS:])
    return jnp.concatenate([first, second], axis=0)


def masked_squares(values, kind):
    squares = values * values
    parts = jnp.sum(squares.reshape(2, 8, 2, 8, squares.shape[-1]), axis=1)
    total = parts[0, 0]
    for q in range(1, 4):
        valid = jnp.where((kind == 0) | (q < kind), 1.0, 0.0).astype(F32)
        total = total + valid * parts[q // 2, q % 2]
    return total


def quadrant_of(shape):
    position = lax.broadcasted_iota(jnp.int32, shape, 0)
    return (position >> 7) * 2 + ((position >> 3) & 1)


def masked(values, kind):
    kind = kind[:, : values.shape[1]]
    return jnp.where((kind == 0) | (quadrant_of(values.shape) < kind), values, 0.0)


def add_mean_squares(R, at, means, kind):
    R.stats[pl.ds(at, 8), 0:1] += sum8(masked(means, kind)) * float(WIDTH)


def mixer_start(R, slot):
    kind = kind_of(R, slot)
    whole, pairs, scale = slot_facts(kind)
    rows = pl.ds(pl.multiple_of(slot * PATCHES, PATCHES), PATCHES)
    x = R.tok[rows, :].astype(F32)
    xhat, _, means = row_stats(x)
    add_mean_squares(R, 0, means, kind)
    R.mid[rows, :] = dot(table_of(R, kind), xhat.astype(BF16))
    grad = masked(R.cot[rows, :].astype(F32), kind)
    R.sums[pl.ds(16, 8), :] += sum8(grad)
    R.msk[rows, :] = grad.astype(BF16)


def mixer_forward(R, slot):
    kind = kind_of(R, slot)
    whole, pairs, scale = slot_facts(kind)
    rows = pl.ds(pl.multiple_of(slot * PATCHES, PATCHES), PATCHES)
    spec = R.mid[rows, :] * (R.vec[0:1, :] * scale)
    row = lax.broadcasted_iota(jnp.int32, (TAIL, WIDTH), 0) + (HALF - TAIL)
    at_zero = (row >= pairs) & (row < pairs + jnp.where(whole, WHOLE_ZEROS, PART_ZEROS))
    shift = R.vec[1:2, :] * jnp.where(whole, float(SIDE), float(SIDE // 2)).astype(F32)
    zeros = spec[HALF - TAIL : HALF] + jnp.where(at_zero, shift, 0.0)
    spec = jnp.concatenate([spec[: HALF - TAIL], zeros, spec[HALF:]], axis=0)
    ra, ia, rb = [part.astype(BF16) for part in spread(spec, pairs)]
    tops, bottoms = [], []
    for j in range(PAIRS):
        lanes = slice(256 * j, 256 * j + 256)
        cols = slice(128 * j, 128 * j + 128)
        low = jnp.concatenate(
            [
                jnp.concatenate([ra[:, cols], ia[:, cols]], axis=1),
                jnp.concatenate([rb[:, cols], -ia[:, cols]], axis=1),
            ],
            axis=0,
        )
        R.spec[rows, lanes] = low
        yield True
        pre = dot(low, R.win[pl.ds(256 * j, 256), :]) + jnp.concatenate([R.vec[2:3, cols], R.vec[3:4, cols]], axis=1)
        act, slope = gelu_and_slope(pre)
        act = act.astype(BF16)
        R.act[rows, lanes] = act
        R.slope[rows, lanes] = slope.astype(BF16)
        yield True
        post = dot(act, R.wout_up[pl.ds(256 * j, 256), :]) + jnp.concatenate(
            [R.vec[4:5, cols], R.vec[5:6, cols]], axis=1
        )
        bent = jnp.tanh(post)
        R.bent[rows, lanes] = (bent * bent).astype(BF16)
        u, v = fold(post - bent, pairs)
        tops.append(u.astype(BF16))
        bottoms.append(v.astype(BF16))
    yield True
    folded = jnp.concatenate([jnp.concatenate(tops, axis=1), jnp.concatenate(bottoms, axis=1)], axis=0)
    mixer_out = dot(table_of(R, kind), folded, TN) * (scale * SHRINK)
    R.stats[pl.ds(8, 8), :] += masked_squares(mixer_out, kind)
    middle = R.tok[rows, :].astype(F32) + mixer_out
    R.mid[rows, :] = middle
    yield True
    yhat, _, means = row_stats(middle)
    add_mean_squares(R, 16, means, kind)
    R.feed[rows, :] = (yhat * R.vec[6:7, :] + R.vec[7:8, :]).astype(BF16)
    yield True


def mlp_front(R, i, cols, we, wc):
    rows = pl.ds(pl.multiple_of(i * CHUNK, CHUNK), CHUNK)
    hidden, slope = gelu_and_slope(dot(R.feed[rows, :], we) + R.be[0:1, cols])
    hidden = hidden.astype(BF16)
    R.hidden[rows, :] = hidden
    yield True
    back = dot(R.msk[rows, :], wc, NT) * slope
    R.dbe[:, cols] += sum8(back)
    back = back.astype(BF16)
    R.hgrad[rows, :] = back
    yield True


def mlp_back(R, i, we, wc, first=False):
    rows = pl.ds(pl.multiple_of(i * CHUNK, CHUNK), CHUNK)
    branch = dot(R.hidden[rows, :], wc)
    R.br[rows, :] = branch if first else R.br[rows, :] + branch
    yield True
    grad = dot(R.hgrad[rows, :], we, NT)
    R.fg[rows, :] = grad if first else R.fg[rows, :] + grad
    yield True


def mlp_chunk(R, i, cols, we, wc, first=False):
    return chain(mlp_front(R, i, cols, we, wc), mlp_back(R, i, we, wc, first))


def mixer_backward_first(R, slot):
    kind = kind_of(R, slot)
    whole, pairs, scale = slot_facts(kind)
    rows = pl.ds(pl.multiple_of(slot * PATCHES, PATCHES), PATCHES)
    feed_grad = R.fg[rows, :]
    yhat, yscale, _ = row_stats(R.mid[rows, :])
    R.sums[pl.ds(0, 8), :] += sum8(feed_grad * yhat)
    R.sums[pl.ds(8, 8), :] += sum8(feed_grad)
    scaled = feed_grad * R.vec[6:7, :]
    yield True
    inner = scaled - jnp.mean(scaled, axis=-1, keepdims=True) - yhat * jnp.mean(scaled * yhat, axis=-1, keepdims=True)
    mgrad = R.msk[rows, :].astype(F32) + inner * yscale
    R.mgrad[rows, :] = mgrad
    yield True
    ra_all, ia_all, rb_all = spread(dot(table_of(R, kind), mgrad.astype(BF16)) * scale, pairs)
    for j in range(PAIRS):
        lanes = slice(256 * j, 256 * j + 256)
        cols = slice(128 * j, 128 * j + 128)
        ra, ia, rb = ra_all[:, cols], ia_all[:, cols], rb_all[:, cols]
        grad = jnp.concatenate([jnp.concatenate([ra, ia], axis=1), jnp.concatenate([rb, -ia], axis=1)], axis=0)
        grad = grad * R.bent[rows, lanes].astype(F32)
        R.dbias[pl.ds(0, 8), lanes] += sum8(grad)
        grad = grad.astype(BF16)
        R.ograd[rows, lanes] = grad
        yield True
        grad = dot(grad, R.wout[pl.ds(256 * j, 256), :], NT) * R.slope[rows, lanes].astype(F32)
        R.dbias[pl.ds(8, 8), lanes] += sum8(grad)
        grad = grad.astype(BF16)
        R.igrad[rows, lanes] = grad
        yield True


def mixer_products(R, i, first=False):
    rows = pl.ds(pl.multiple_of(i * CHUNK, CHUNK), CHUNK)
    for j in range(PAIRS):
        lanes = slice(256 * j, 256 * j + 256)
        for which, (left, right) in enumerate(((R.spec, R.igrad), (R.act, R.ograd))):
            product = dot(left[rows, lanes], right[rows, lanes], TN)
            R.dmix[which, j] = product if first else R.dmix[which, j] + product
            yield True


def block_result(R, slot):
    kind = kind_of(R, slot)
    rows = pl.ds(pl.multiple_of(slot * PATCHES, PATCHES), PATCHES)
    branch = R.br[rows, :] + R.vec[8:9, :]
    result = R.mid[rows, :] + branch
    R.stats[pl.ds(24, 8), :] += masked_squares(branch, kind)
    R.stats[pl.ds(32, 8), :] += masked_squares(result, kind)
    R.out[rows, :] = result.astype(BF16)
    yield True


def mixer_weight_gradients(R, put):
    for j in range(PAIRS):
        for which in range(2):
            put(which, j, pair_gradient(R.dmix[which, j]))


def mixer_backward_second(R, slot):
    kind = kind_of(R, slot)
    whole, pairs, scale = slot_facts(kind)
    rows = pl.ds(pl.multiple_of(slot * PATCHES, PATCHES), PATCHES)
    tops, bottoms = [], []
    for j in range(PAIRS):
        lanes = slice(256 * j, 256 * j + 256)
        u, v = fold(dot(R.igrad[rows, lanes], R.win[pl.ds(256 * j, 256), :], NT), pairs)
        tops.append(u.astype(BF16))
        bottoms.append(v.astype(BF16))
        yield True
    folded = jnp.concatenate([jnp.concatenate(tops, axis=1), jnp.concatenate(bottoms, axis=1)], axis=0)
    ngrad = dot(table_of(R, kind), folded, TN) * scale
    R.ngrad[rows, :] = ngrad
    xhat, _, _ = row_stats(R.tok[rows, :].astype(F32))
    yield True
    R.sums[pl.ds(24, 8), :] += sum8(ngrad * xhat)
    R.sums[pl.ds(32, 8), :] += sum8(ngrad)
    yield True


def norm_backward(R, slot):
    rows = pl.ds(pl.multiple_of(slot * PATCHES, PATCHES), PATCHES)
    xhat, xscale, _ = row_stats(R.tok[rows, :].astype(F32))
    scaled = R.ngrad[rows, :] * R.vec[0:1, :]
    yield True
    inner = scaled - jnp.mean(scaled, axis=-1, keepdims=True) - xhat * jnp.mean(scaled * xhat, axis=-1, keepdims=True)
    R.igrad_out[rows, :] = R.mgrad[rows, :] + inner * xscale
    yield True

class Refs:
    pass


VMEM = pl.BlockSpec(memory_space=pltpu.VMEM)
SMEM = pl.BlockSpec(memory_space=pltpu.SMEM)
ROOM = 127 * 2**19


def named(names, refs):
    R = Refs()
    for name, ref in zip(names, refs):
        setattr(R, name, ref)
    return R


def plain_call(body, ins, outs, scratch, name):
    names = list(ins) + list(outs) + list(scratch)

    def kernel(*refs):
        body(named(names, refs))

    values = pl.pallas_call(
        kernel,
        out_shape=[jax.ShapeDtypeStruct(*spec) for spec in outs.values()],
        in_specs=[SMEM if key == "items" else VMEM for key in ins],
        out_specs=[VMEM for _ in outs],
        scratch_shapes=[pltpu.VMEM(*spec) for spec in scratch.values()],
        compiler_params=pltpu.CompilerParams(vmem_limit_bytes=ROOM),
        name=name,
    )(*ins.values())
    return dict(zip(outs, values))


def forward_body(R):
    complex_pairs(R.inner, R.win)
    complex_pairs(R.outer, R.wout, R.wout_up)
    R.stats[...] = jnp.zeros_like(R.stats)
    R.sums[...] = jnp.zeros_like(R.sums)

    @pl.loop(0, R.tok.shape[0] // PATCHES)
    def _(slot):
        mixer_start(R, slot)
        run(mixer_forward(R, slot))


def mlp_body(R):
    R.dbe[...] = jnp.zeros_like(R.dbe)
    R.br[...] = jnp.zeros_like(R.br)
    R.fg[...] = jnp.zeros_like(R.fg)

    @pl.loop(0, R.we.shape[1] // CHUNK)
    def _(t):
        cols = pl.ds(pl.multiple_of(t * CHUNK, CHUNK), CHUNK)

        @pl.loop(0, R.feed.shape[0] // CHUNK)
        def _(i):
            run(mlp_chunk(R, i, cols, R.we[:, cols], R.wc[cols, :]))

        R.dwe[:, cols] = dot(R.feed[...], R.hgrad[...], TN).astype(BF16)
        R.dwc[:, cols] = dot(R.msk[...], R.hidden[...], TN).astype(BF16)


def backward_body(R):
    R.stats[...] = jnp.zeros_like(R.stats)
    R.sums[...] = jnp.zeros_like(R.sums)
    R.dbias[...] = jnp.zeros_like(R.dbias)
    R.dmix[...] = jnp.zeros_like(R.dmix)
    slots = R.tok.shape[0] // PATCHES

    @pl.loop(0, slots)
    def _(slot):
        run(block_result(R, slot), mixer_backward_first(R, slot))

    @pl.loop(0, slots * PATCHES // CHUNK)
    def _(i):
        run(mixer_products(R, i))

    def put_mix(which, j, value):
        (R.dinner, R.douter)[which][pl.ds(128 * j, 128), :] = value

    mixer_weight_gradients(R, put_mix)

    @pl.loop(0, slots)
    def _(slot):
        run(chain(mixer_backward_second(R, slot), norm_backward(R, slot)))


def pair_order(vector):
    parts = vector.reshape(NB, 2, BS)
    return parts[:, 0].reshape(1, WIDTH), parts[:, 1].reshape(1, WIDTH)


def body_by_collectives(
    tokens, cotangent, slot_items, filter_gain, filter_shift, inner_weight, inner_bias, outer_weight, outer_bias,
    feed_gain, feed_shift, expand_weight, expand_bias, contract_weight, contract_bias,
):
    def gather(x):
        return lax.all_gather(x, "fsdp", axis=0, tiled=True)

    vectors = (filter_gain, filter_shift, inner_bias, outer_bias, feed_gain, feed_shift, contract_bias, expand_bias)
    sizes = [v.shape[0] for v in vectors]
    packed = lax.all_gather(jnp.concatenate(vectors), "fsdp", axis=0)
    ends = np.cumsum([0] + sizes)
    g1, s1, bi, bo, g2, s2, bc, be = [packed[:, a:b].reshape(-1).astype(F32) for a, b in zip(ends, ends[1:])]
    vec = jnp.concatenate(
        [g1[None], s1[None], *pair_order(bi), *pair_order(bo / SHRINK), g2[None], s2[None], bc[None], jnp.zeros((7, WIDTH), F32)]
    )
    inner, outer, we, wc = gather(inner_weight), gather(outer_weight), gather(expand_weight), gather(contract_weight)
    n = tokens.shape[0] * PATCHES
    hidden = we.shape[1]
    tok, cot = tokens.reshape(n, WIDTH), cotangent.reshape(n, WIDTH)
    table = jnp.asarray(TABLES, BF16)
    wide = ((n, 2 * WIDTH), BF16)
    flat = ((n, WIDTH), BF16)
    full = ((n, WIDTH), F32)
    pairs = ((2 * WIDTH, 2 * 2 * BS), BF16)
    sums = ((40, WIDTH), F32)
    a = plain_call(
        forward_body,
        dict(items=slot_items, tok=tok, cot=cot, table=table, vec=vec, inner=inner.reshape(PAIRS, 2, BS, 2 * BS), outer=outer.reshape(PAIRS, 2, BS, 2 * BS)),
        dict(spec=wide, act=wide, slope=wide, bent=wide, mid=full, feed=flat, msk=flat, win=pairs, wout=pairs, stats=sums, sums=sums),
        dict(wout_up=pairs),
        "mixer_forward",
    )
    b = plain_call(
        mlp_body,
        dict(feed=a["feed"], msk=a["msk"], we=we, wc=wc, be=be.reshape(1, hidden)),
        dict(br=full, fg=full, dwe=((WIDTH, hidden), BF16), dwc=((WIDTH, hidden), BF16), dbe=((8, hidden), F32)),
        dict(hidden=((n, CHUNK), BF16), hgrad=((n, CHUNK), BF16)),
        "mlp",
    )
    c = plain_call(
        backward_body,
        dict(
            items=slot_items, tok=tok, table=table, vec=vec, spec=a["spec"], act=a["act"], slope=a["slope"], bent=a["bent"],
            mid=a["mid"], msk=a["msk"], br=b["br"], fg=b["fg"], win=a["win"], wout=a["wout"],
        ),
        dict(
            out=flat, igrad_out=full, dinner=((WIDTH, 2 * BS), F32), douter=((WIDTH, 2 * BS), F32),
            dbias=((16, 2 * WIDTH), F32), sums=sums, stats=sums,
        ),
        dict(mgrad=full, ograd=wide, igrad=wide, ngrad=full, dmix=((2, PAIRS, 256, 256), F32)),
        "mixer_backward",
    )

    def scatter(x):
        return lax.psum_scatter(x, "fsdp", scatter_dimension=0, tiled=True)

    def rows_of(x, at):
        return jnp.sum(x[at : at + 8], axis=0)

    def bias_of(at):
        parts = rows_of(c["dbias"], at).reshape(PAIRS, 2, 2, BS)
        return jnp.swapaxes(parts, 1, 2).reshape(2 * WIDTH)

    sums_ = a["sums"] + c["sums"]
    stats_ = a["stats"] + c["stats"]
    small = [
        rows_of(sums_, 24), rows_of(sums_, 32), bias_of(8), bias_of(0), rows_of(sums_, 0), rows_of(sums_, 8),
        rows_of(sums_, 16), jnp.sum(b["dbe"], axis=0),
    ]
    fsdp = lax.axis_size("fsdp")
    small = jnp.concatenate([v.reshape(fsdp, -1) for v in small], axis=1)
    weights = jnp.concatenate([c["dinner"].reshape(fsdp, -1), c["douter"].reshape(fsdp, -1)], axis=1)
    weights = jnp.concatenate([weights, small], axis=1).astype(BF16)
    own_small = scatter(weights.reshape(-1))
    own_we = scatter(b["dwe"])
    own_wc = scatter(b["dwc"].T)
    own_small, own_we, own_wc = lax.psum((own_small, own_we, own_wc), "rep")
    own_small = own_small.astype(F32)
    cut = inner_weight.size
    own_iw, own_ow = own_small[:cut].reshape(inner_weight.shape), own_small[cut : 2 * cut].reshape(inner_weight.shape)
    own = [own_small[2 * cut + x : 2 * cut + y] for x, y in zip(ends, ends[1:])]
    kinds = slot_items[:, None]
    valid = jnp.where((kinds == 0) | (jnp.arange(4)[None] < kinds), 1.0, 0.0)
    local = jnp.concatenate([jnp.sum(stats_.reshape(5, -1), axis=1), jnp.sum(valid)[None] * (PATCHES // 4 * WIDTH)])
    total = lax.psum(local, ("rep", "fsdp"))
    statistics = jnp.sqrt(total[:5] / total[5])
    return (
        c["out"].reshape(tokens.shape), c["igrad_out"].reshape(tokens.shape), own[0], own[1], own_iw, own[2], own_ow, own[3],
        own[4], own[5], own_we.astype(F32), own[7], own_wc.astype(F32), own[6], statistics,
    )


def specs():
    items = P(("rep", "fsdp"))
    big = P(("rep", "fsdp"), None, None)
    one, two = P("fsdp"), P("fsdp", None)
    ins = (big, big, items, one, one, two, one, two, one, one, one, two, one, two, one)
    outs = (big, big, one, one, two, one, two, one, one, one, two, one, two, one, P())
    return ins, outs


MESH = pl.DeviceIdType.MESH
AHEAD = 2
ANY = pl.BlockSpec(memory_space=pl.ANY)
FSDP = 8


def multiple(value, by):
    return pl.multiple_of(value * by, by)


class Place:
    def __init__(self, copies):
        self.z, self.f = lax.axis_index("rep"), lax.axis_index("fsdp")
        self.core, self.chip = self.f & 1, self.f >> 1
        self.copies = copies

    def peer(self, mask):
        return (self.z, self.f ^ mask)

    def floor(self, offset):
        return (lax.rem(self.z + offset, self.copies), self.f)


def remote(src, dst, send, recv, device):
    return pltpu.make_async_remote_copy(
        src_ref=src, dst_ref=dst, send_sem=send, recv_sem=recv, device_id=device, device_id_type=MESH
    )


class Sum:
    def __init__(self, place, R):
        self.p, self.R = place, R
        self.rows = R.sum_done.shape[1] // place.copies

    def copy(self, step, t, src, dst, device):
        return remote(src, dst, self.R.sum_send.at[step], self.R.sum_recv.at[step, t], device)

    def wait(self, step, t):
        view = (self.R.sum_core, self.R.sum_chips, self.R.sum_floors, self.R.sum_floors)[step].at[t]
        self.copy(step, t, view, view, self.p.peer(1)).wait_recv()

    def piece(self, floor):
        return pl.ds(multiple(floor, self.rows), self.rows)

    def offsets(self):
        return range(1, self.p.copies)

    def start(self, t):
        other = 1 - self.p.core
        self.copy(0, t, self.R.sum_own.at[t, :, other], self.R.sum_core.at[t], self.p.peer(1)).start()

    def to_chips(self, t):
        R = self.R
        self.wait(0, t)
        for k in (3, 1, 2, 0):
            at = self.p.chip ^ k
            R.sum_own[t, at, self.p.core] = R.sum_own[t, at, self.p.core] + R.sum_core[t, at]
            if k:
                self.copy(1, t, R.sum_own.at[t, at, self.p.core], R.sum_chips.at[t, k - 1], self.p.peer(2 * k)).start()

    def to_floors(self, t):
        R = self.R
        self.wait(1, t)
        total = R.sum_own[t, self.p.chip, self.p.core].astype(F32)
        for k in (1, 2, 3):
            total = total + R.sum_chips[t, k - 1].astype(F32)
        R.sum_total[t] = total.astype(BF16)
        for d in self.offsets():
            device = self.p.floor(d)
            self.copy(2, t, R.sum_total.at[t, self.piece(device[0])], R.sum_floors.at[t, d - 1], device).start()

    def to_all(self, t):
        R = self.R
        self.wait(2, t)
        mine = self.piece(self.p.z)
        total = R.sum_total[t, mine, :].astype(F32)
        for d in self.offsets():
            total = total + R.sum_floors[t, d - 1].astype(F32)
        R.sum_done[t, mine, :] = total.astype(BF16)
        for d in self.offsets():
            self.copy(3, t, R.sum_done.at[t, mine], R.sum_done.at[t, mine], self.p.floor(d)).start()

    def finish(self, t):
        self.wait(3, t)

    def sent(self):
        R = self.R
        for step, view in enumerate((R.sum_core, R.sum_chips, R.sum_floors, R.sum_floors)):
            self.copy(step, 0, view, view, self.p.peer(1)).wait_send()


class Gather:
    def __init__(self, R, place):
        self.R, self.p = R, place

    def bring(self):
        R = self.R
        deep, tall = R.we_in.shape[0], R.wc_in.shape[0]
        for m in range(R.we_in.shape[1] // CHUNK):
            self.local(R.we_in.at[:, pl.ds(m * CHUNK, CHUNK)], R.hidden.at[pl.ds(m * deep, deep), :]).start()
        for t in range(R.w.shape[0]):
            self.local(R.wc_in.at[pl.ds(t * deep, deep), :], R.w.at[t, self.p.chip, self.p.core, :, pl.ds(CHUNK, CHUNK)]).start()

    def local(self, src, dst):
        return pltpu.make_async_copy(src, dst, self.R.keep_sems.at[0])

    def lay(self):
        R = self.R
        deep, tall = R.we_in.shape[0], R.wc_in.shape[0]
        all_of = R.hidden.at[pl.ds(0, 2 * R.wc_in.shape[0]), :]
        self.local(all_of, all_of).wait()
        for t in range(0, R.w.shape[0], 2):
            for m in range(R.we_in.shape[1] // CHUNK):
                held = R.hidden[pl.ds(m * deep, deep), :].astype(F32)
                even, odd = [held[:, at + t * BS : at + t * BS + 128] for at in (0, tall)]
                for side, part in enumerate(interleave(even, odd)):
                    R.w[t + side, self.p.chip, self.p.core, :, 128 * m : 128 * m + 128] = part.astype(BF16)

    def start(self, t):
        R, p = self.R, self.p
        view = R.w.at[t, p.chip, p.core]
        for k in (1, 2, 3):
            remote(view, view, R.gather_send.at[0], R.gather_chips.at[t], p.peer(2 * k)).start()

    def pass_on(self, t):
        R, p = self.R, self.p
        three, view = R.w.at[t, pl.ds(0, 3), 0], R.w.at[t, :, p.core]
        remote(three, three, R.gather_send.at[0], R.gather_chips.at[t], p.peer(1)).wait_recv()
        remote(view, view, R.gather_send.at[1], R.gather_core.at[t], p.peer(1)).start()

    def finish(self, t):
        R, p = self.R, self.p
        view = R.w.at[t, :, 1 - p.core]
        remote(view, view, R.gather_send.at[1], R.gather_core.at[t], p.peer(1)).wait_recv()

    def sent(self):
        R, p = self.R, self.p
        for at, view in enumerate((R.w.at[pl.ds(0, 3), :, 0], R.w.at[:, :, 0])):
            remote(view, view, R.gather_send.at[at], R.gather_core.at[0], p.peer(1)).wait_send()


class SmallGather:
    def __init__(self, R, place):
        self.R, self.p = R, place

    def way(self, view, step, device):
        return remote(view, view, self.R.small_sems.at[2 * step], self.R.small_sems.at[2 * step + 1], device)

    def start(self):
        for k in (1, 2, 3):
            self.way(self.R.smalls.at[self.p.chip, self.p.core], 0, self.p.peer(2 * k)).start()

    def pass_on(self):
        self.way(self.R.smalls.at[pl.ds(0, 3), 0], 0, self.p.peer(1)).wait_recv()
        self.way(self.R.smalls.at[:, self.p.core], 1, self.p.peer(1)).start()

    def finish(self):
        self.way(self.R.smalls.at[:, 1 - self.p.core], 1, self.p.peer(1)).wait_recv()

    def sent(self):
        self.way(self.R.smalls.at[pl.ds(0, 3), 0], 0, self.p.peer(1)).wait_send()
        self.way(self.R.smalls.at[:, 0], 1, self.p.peer(1)).wait_send()


def pack_small(R):
    R.small[pl.ds(0, BS), :] = R.inner_in[...]
    R.small[pl.ds(BS, BS), :] = R.outer_in[...]

    def row(*refs):
        return jnp.concatenate([ref[...].astype(F32) for ref in refs], axis=1)

    none = jnp.zeros((1, BS), F32)
    rows = [
        row(R.fg_in, R.fs_in), R.ib_in[...].astype(F32), R.ob_in[...].astype(F32), row(R.gg_in, R.gs_in),
        jnp.concatenate([R.cb_in[...].astype(F32), none], axis=1),
        R.eb_in[...].astype(F32), jnp.zeros((9, 128), F32),
    ]
    R.small[pl.ds(2 * BS, 16), :] = jnp.concatenate(rows, axis=0).astype(BF16)


def unpack_small(R):
    for j in range(PAIRS):
        cols = slice(128 * j, 128 * j + 128)
        even = R.smalls[j, 0, pl.ds(2 * BS, 16), :].astype(F32)
        odd = R.smalls[j, 1, pl.ds(2 * BS, 16), :].astype(F32)
        first, second = interleave(even, odd)
        for row, (part, at) in enumerate(
            [(first, 0), (second, 0), (first, 1), (second, 1), (first, 2), (second, 2), (first, 3), (second, 3), (first, 4)]
        ):
            R.vec[row : row + 1, cols] = part[at : at + 1] * (1.0 / SHRINK if at == 2 else 1.0)
        for t in range(R.be.shape[1] // CHUNK):
            R.be[0:1, t * CHUNK + 128 * j : t * CHUNK + 128 * j + 128] = (first, second)[t % 2][5 + t // 2 : 6 + t // 2]
    complex_pairs(R.smalls.at[:, :, pl.ds(0, BS), :], R.win)
    complex_pairs(R.smalls.at[:, :, pl.ds(BS, BS), :], R.wout, R.wout_up)


def pack_sums(R):
    slots = R.tok.shape[0] // PATCHES

    def total(ref, at):
        return jnp.sum(ref[pl.ds(at, 8), :], axis=0, keepdims=True)

    feed_gain, feed_shift, contract, gain, shift = [total(R.sums, 8 * i) for i in range(5)]
    outer, inner, expand = total(R.dbias, 0), total(R.dbias, 8), total(R.dbe, 0)
    lane = lax.broadcasted_iota(jnp.int32, (1, 128), 1)
    facts = jnp.zeros((1, 128), F32)
    for i in range(5):
        facts = jnp.where(lane == i, jnp.sum(total(R.stats, 8 * i), axis=1, keepdims=True), facts)
    valid = jnp.zeros((1, 128), F32)
    for slot in range(slots):
        kind = kind_of(R, slot, 128)
        valid = valid + jnp.where(kind == 0, 4, kind).astype(F32) * float(PATCHES // 4 * WIDTH)
    facts = jnp.where(lane == 5, valid, facts)
    none = jnp.zeros((1, 128), F32)
    for j in range(PAIRS):
        cols = slice(128 * j, 128 * j + 128)
        real, imag = slice(256 * j, 256 * j + 128), slice(256 * j + 128, 256 * j + 256)
        rows = [
            interleave(gain[:, cols], shift[:, cols]),
            interleave(inner[:, real], inner[:, imag]),
            interleave(outer[:, real], outer[:, imag]),
            interleave(feed_gain[:, cols], feed_shift[:, cols]),
            interleave(contract[:, cols], none),
        ]
        for t in range(0, R.be.shape[1] // CHUNK, 2):
            low, high = [expand[:, (t + s) * CHUNK + 128 * j : (t + s) * CHUNK + 128 * j + 128] for s in range(2)]
            rows.append(interleave(low, high))
        for side in range(2):
            R.vec_own[2 * j + side] = jnp.concatenate([row[side] for row in rows] + [facts], axis=0)


class Share:
    def __init__(self, place, own, arrived, floors, sems):
        self.p, self.own, self.arrived, self.floors, self.sems = place, own, arrived, floors, sems

    def copy(self, step, src, dst, device):
        return remote(src, dst, self.sems.at[2 * step], self.sems.at[2 * step + 1], device)

    def views(self):
        return self.arrived, self.floors.at[pl.ds(0, self.p.copies - 1)]

    def wait(self, step):
        view = self.views()[step]
        self.copy(step, view, view, self.p.peer(1)).wait_recv()

    def start(self):
        for k in (6, 7, 2, 4, 3, 5, 1):
            self.copy(0, self.own.at[self.p.f ^ k], self.arrived.at[k - 1], self.p.peer(k)).start()

    def to_floors(self):
        self.wait(0)
        total = self.own[self.p.f].astype(F32)
        for k in range(1, FSDP):
            total = total + self.arrived[k - 1].astype(F32)
        self.floors[self.p.z] = total.astype(self.floors.dtype)
        mine = self.floors.at[self.p.z]
        for d in range(1, self.p.copies):
            self.copy(1, mine, mine, self.p.floor(d)).start()

    def finish(self):
        self.wait(1)
        total = self.floors[0].astype(F32)
        for z in range(1, self.p.copies):
            total = total + self.floors[z].astype(F32)
        return total

    def sent(self):
        for step, view in enumerate(self.views()):
            self.copy(step, view, view, self.p.peer(1)).wait_send()


def layer(copies, R):
    p = Place(copies)
    n = R.tok.shape[0]
    slots = n // PATCHES
    chunks = R.w.shape[0]
    blocks = n // CHUNK
    last = chunks - 1

    def loads(i):
        rows = pl.ds(multiple(i, CHUNK), CHUNK)
        return [
            pltpu.make_async_copy(src.at[rows, :], dst.at[rows, :], R.load_sems.at[i])
            for src, dst in ((R.tok_in, R.tok), (R.cot_in, R.msk))
        ]

    def loaded(i):
        both = R.tok.at[pl.ds(0, 2 * CHUNK), :]
        pltpu.make_async_copy(both, both, R.load_sems.at[i]).wait()

    stores = ((R.feed, R.out_ref), (R.fg, R.grad_ref))

    def store(which, i):
        rows = pl.ds(multiple(i, CHUNK), CHUNK)
        src, dst = stores[which]
        pltpu.make_async_copy(src.at[rows, :], dst.at[rows, :], R.store_sems.at[which]).start()

    gather = Gather(R, p)
    gather.bring()
    barrier = pltpu.get_barrier_semaphore()
    for k in range(1, FSDP):
        pl.semaphore_signal(barrier, inc=1, device_id=p.peer(k), device_id_type=MESH)
    for d in range(1, copies):
        pl.semaphore_signal(barrier, inc=1, device_id=p.floor(d), device_id_type=MESH)
    for i in range(blocks):
        for load in loads(i):
            load.start()
    R.stats[...] = jnp.zeros_like(R.stats)
    R.sums[...] = jnp.zeros_like(R.sums)
    R.dbias[...] = jnp.zeros_like(R.dbias)
    R.dbe[...] = jnp.zeros_like(R.dbe)
    pack_small(R)
    R.smalls[p.chip, p.core] = R.small[...]
    gather.lay()

    def begin(i):
        loaded(i)
        for side in range(CHUNK // PATCHES):
            mixer_start(R, i * (CHUNK // PATCHES) + side)

    pl.semaphore_wait(barrier, FSDP - 1 + copies - 1)

    small = SmallGather(R, p)
    small.start()
    gather.start(0)
    pl.loop(0, blocks)(begin)
    small.pass_on()
    small.finish()
    unpack_small(R)
    sums = Sum(p, R)

    def weights(t):
        return [R.w[t, :, :, :, pl.ds(at, CHUNK)].reshape(-1, CHUNK) for at in (0, CHUNK)]

    def weight_gradients(t):
        for at, (left, right) in ((0, (R.feed, R.hgrad)), (CHUNK, (R.hidden, R.msk))):
            piece = dot(left[...], right[...], TN).astype(BF16)
            for k in range(FSDP):
                R.sum_own[t, k // 2, k % 2, :, at : at + CHUNK] = piece[k * BS : (k + 1) * BS]
        sums.start(t)

    def chunk_cols(t):
        return slice(t * CHUNK, (t + 1) * CHUNK)

    def two(step, i):
        return step(R, 2 * i), step(R, 2 * i + 1)

    @pl.loop(0, AHEAD)
    def _(i):
        run(*two(mixer_forward, i))

        @pl.when(i == AHEAD - 1)
        def _():
            gather.start(1)
            gather.pass_on(0)

    gather.finish(0)

    @pl.loop(AHEAD, blocks)
    def _(i):
        weave(chain(*two(mixer_forward, i)), 5, mlp_chunk(R, i - AHEAD, chunk_cols(0), *weights(0), first=True))

        @pl.when(i == blocks - 2)
        def _():
            gather.start(2)

    @pl.loop(blocks - AHEAD, blocks)
    def _(i):
        run(mlp_chunk(R, i, chunk_cols(0), *weights(0), first=True))

        @pl.when(i == blocks - AHEAD)
        def _():
            gather.start(3)
            gather.pass_on(1)

    weight_gradients(0)
    gather.finish(1)

    @pl.loop(1, last)
    def _(t):
        cols = pl.ds(multiple(t, CHUNK), CHUNK)

        @pl.loop(0, blocks)
        def _(i):
            @pl.when(i == 1)
            def _():
                sums.to_chips(t - 1)

            @pl.when((t > 1) & (i == 3))
            def _():
                sums.to_floors(t - 2)

            run(mlp_chunk(R, i, cols, *weights(t)))

            @pl.when(i == 2)
            def _():
                gather.pass_on(t + 1)

        weight_gradients(t)
        gather.finish(t + 1)

    @pl.loop(0, blocks)
    def _(i):
        @pl.when(i == 1)
        def _():
            sums.to_chips(last - 1)

        @pl.when(i == 2)
        def _():
            sums.to_all(last - 3)

        @pl.when(i == 3)
        def _():
            sums.to_floors(last - 2)

        run(mlp_front(R, i, chunk_cols(last), *weights(last)))

    weight_gradients(last)

    def first_back(i, *beside):
        weave(turns(*two(mixer_backward_first, i)), 1, turns(*beside))

    run(mlp_back(R, 0, *weights(last)))
    first_back(0, mlp_back(R, 1, *weights(last)))
    sums.to_chips(last)
    sums.to_floors(last - 1)
    first_back(1, mlp_back(R, 2, *weights(last)), mixer_products(R, 0, first=True))

    sums.to_all(last - 2)

    @pl.loop(3, blocks)
    def _(i):
        first_back(i - 1, mlp_back(R, i, *weights(last)), mixer_products(R, i - 2))

    sums.to_all(last - 1)
    first_back(blocks - 1, mixer_products(R, blocks - 2))
    sums.to_floors(last)
    run(mixer_products(R, blocks - 1))

    def put(which, j, value):
        for side in range(2):
            R.mix_own[2 * j + side, pl.ds(which * BS, BS), :] = value[side * BS : (side + 1) * BS].astype(BF16)

    mixer_weight_gradients(R, put)
    mixing = Share(p, R.mix_own, R.mix_peers, R.mix_floors, R.mix_sems)
    mixing.start()

    @pl.loop(0, blocks)
    def _(i):
        run(*two(block_result, i), *two(mixer_backward_second, i))
        store(0, i)

        @pl.when(i == 2)
        def _():
            sums.to_all(last)

    pack_sums(R)
    vectors = Share(p, R.vec_own, R.vec_peers, R.vec_floors, R.vec_sems)
    vectors.start()
    mixing.to_floors()

    @pl.loop(0, blocks)
    def _(i):
        run(*two(norm_backward, i))
        store(1, i)

    vectors.to_floors()
    for t in range(chunks):
        sums.finish(t)
    done_out = pltpu.make_async_copy(R.sum_done, R.done_ref, R.store_sems.at[2])
    done_out.start()
    R.mix_ref[...] = mixing.finish()
    R.vec_ref[...] = vectors.finish()
    small.sent()
    gather.sent()
    sums.sent()
    mixing.sent()
    vectors.sent()
    for which, (src, dst) in enumerate(stores):
        pltpu.make_async_copy(src, dst, R.store_sems.at[which]).wait()
    done_out.wait()


def body_in_one(
    copies, tokens, cotangent, slot_items, filter_gain, filter_shift, inner_weight, inner_bias, outer_weight, outer_bias,
    feed_gain, feed_shift, expand_weight, expand_bias, contract_weight, contract_bias,
):
    slots = tokens.shape[0]
    n = slots * PATCHES
    deep, hidden = expand_weight.shape
    tall = contract_weight.shape[0]
    chunks = hidden // CHUNK
    floors = copies - 1
    ins = dict(
        items=slot_items, tok_in=tokens.reshape(n, WIDTH), cot_in=cotangent.reshape(n, WIDTH), table=jnp.asarray(TABLES, BF16),
        inner_in=inner_weight, outer_in=outer_weight, we_in=expand_weight, wc_in=contract_weight,
        fg_in=filter_gain[None], fs_in=filter_shift[None], ib_in=inner_bias[None], ob_in=outer_bias[None],
        gg_in=feed_gain[None], gs_in=feed_shift[None], cb_in=contract_bias[None], eb_in=expand_bias.reshape(2, 128),
    )
    places = dict.fromkeys(("tok_in", "cot_in", "we_in", "wc_in", "out_ref", "grad_ref", "done_ref"), ANY)
    places["items"] = SMEM
    outs = dict(
        out_ref=((n, WIDTH), BF16), grad_ref=((n, WIDTH), F32), done_ref=((chunks, deep, 2 * CHUNK), BF16),
        mix_ref=((2 * BS, 2 * BS), F32), vec_ref=((8, 128), F32),
    )
    wide, flat, full = ((n, 2 * WIDTH), BF16), ((n, WIDTH), BF16), ((n, WIDTH), F32)
    pairs, sums = ((2 * WIDTH, 4 * BS), BF16), ((40, WIDTH), F32)
    both = 2 * CHUNK
    memory = dict(
        tok=flat, msk=flat, spec=wide, act=wide, slope=wide, bent=wide, mid=full, feed=flat, br=full, fg=full,
        hidden=((n, CHUNK), BF16), hgrad=((n, CHUNK), BF16), w=((chunks, FSDP // 2, 2, deep, both), BF16),
        win=pairs, wout=pairs, wout_up=pairs, vec=((16, WIDTH), F32), be=((8, hidden), F32), stats=sums, sums=sums,
        dbias=((16, 2 * WIDTH), F32), dbe=((8, hidden), F32),
        dmix=((2, PAIRS, 256, 256), F32), small=((144, 128), BF16), smalls=((FSDP // 2, 2, 144, 128), BF16),
        sum_own=((chunks, 4, 2, deep, both), BF16), sum_core=((chunks, 4, deep, both), BF16),
        sum_chips=((chunks, 3, deep, both), BF16), sum_total=((chunks, deep, both), BF16),
        sum_floors=((chunks, floors, deep // copies, both), BF16), sum_done=((chunks, deep, both), BF16),
        mix_own=((FSDP, 128, 128), BF16), mix_peers=((FSDP - 1, 128, 128), BF16), mix_floors=((copies, 128, 128), BF16),
        vec_own=((FSDP, 8, 128), F32), vec_peers=((FSDP - 1, 8, 128), F32), vec_floors=((copies, 8, 128), F32),
    )
    sems = dict(
        load_sems=(n // CHUNK,), store_sems=(3,), keep_sems=(1,), small_sems=(4,), gather_send=(2,), gather_chips=(chunks,),
        gather_core=(chunks,), sum_send=(4,), sum_recv=(4, chunks), mix_sems=(4,), vec_sems=(4,),
    )
    names = list(ins) + list(outs) + list(memory) + list(sems)

    def kernel(*refs):
        R = named(names, refs)
        R.mgrad, R.out, R.ograd, R.igrad, R.cot = R.fg, R.feed, R.bent, R.slope, R.msk
        R.ngrad, R.igrad_out = R.mid, R.fg
        layer(copies, R)

    o = dict(
        zip(
            outs,
            pl.pallas_call(
                kernel,
                out_shape=[jax.ShapeDtypeStruct(*spec) for spec in outs.values()],
                in_specs=[places.get(key, VMEM) for key in ins],
                out_specs=[places.get(key, VMEM) for key in outs],
                scratch_shapes=[pltpu.VMEM(*spec) for spec in memory.values()]
                + [pltpu.SemaphoreType.DMA(shape) for shape in sems.values()],
                compiler_params=pltpu.CompilerParams(vmem_limit_bytes=ROOM, collective_id=0, has_side_effects=True),
                name="mega",
            )(*ins.values()),
        )
    )
    return finishing(tokens.shape, o, deep, hidden, tall)


PIECES = 1


def finishing(shape, o, deep, hidden, tall):
    ends = dict(
        out=(o["out_ref"].shape, BF16), grad=(o["grad_ref"].shape, F32), fg=((1, BS), F32), fs=((1, BS), F32),
        inner=((BS, 2 * BS), F32), ib=((1, 128), F32), outer=((BS, 2 * BS), F32), ob=((1, 128), F32), gg=((1, BS), F32),
        gs=((1, BS), F32), ew=((deep, hidden), F32), eb=((2, 128), F32), cw=((tall, WIDTH), F32), cb=((1, BS), F32),
        stat=((1, 5), F32),
    )
    names = list(o) + list(ends) + ["grad_held", "out_held", "done_held", "mix_held", "vec_held", "ew_held", "cw_held", "come_sems", "go_sems", "done_sems"]

    def kernel(*refs):
        R = named(names, refs)
        def way(which, i):
            src, held, dst = ((R.grad_ref, R.grad_held, R.grad), (R.out_ref, R.out_held, R.out))[which]
            size = src.shape[0] // PIECES
            rows = pl.ds(i * size, size)
            come = pltpu.make_async_copy(src.at[rows], held.at[rows], R.come_sems.at[which, i])
            return come, pltpu.make_async_copy(held.at[rows], dst.at[rows], R.go_sems.at[which])

        smalls = [
            pltpu.make_async_copy(src, held, R.done_sems.at[i])
            for i, (src, held) in enumerate(((R.done_ref, R.done_held), (R.mix_ref, R.mix_held), (R.vec_ref, R.vec_held)))
        ]
        ways = [way(which, i) for i in range(PIECES) for which in range(2)]
        for small in smalls:
            small.start()
        for come, _ in ways:
            come.start()
        for small in smalls:
            small.wait()
        chunks, deep = R.done_ref.shape[:2]
        for t in range(0, chunks, 2):
            for m in range(CHUNK // 128):
                low, high = [R.done_held[t + side, :, 128 * m : 128 * m + 128].astype(F32) for side in range(2)]
                at = 2 * m * tall + t * BS
                for side, part in enumerate(interleave(low, high)):
                    R.ew_held[:, at + side * tall : at + side * tall + 128] = part
        for t in range(chunks):
            R.cw_held[pl.ds(t * deep, deep), :] = R.done_held[t, :, CHUNK:].astype(F32)
        ends = [
            pltpu.make_async_copy(R.ew_held, R.ew, R.done_sems.at[3]),
            pltpu.make_async_copy(R.cw_held, R.cw, R.done_sems.at[4]),
        ]
        for end in ends:
            end.start()
        R.inner[...], R.outer[...] = R.mix_held[:BS], R.mix_held[BS:]
        vec = R.vec_held[...]
        R.fg[...], R.fs[...] = vec[0:1, :BS], vec[0:1, BS:]
        R.ib[...], R.ob[...] = vec[1:2], vec[2:3]
        R.gg[...], R.gs[...] = vec[3:4, :BS], vec[3:4, BS:]
        R.cb[...], R.eb[...] = vec[4:5, :BS], vec[5:7]
        lane = lax.broadcasted_iota(jnp.int32, (1, 128), 1)
        total = jnp.sum(jnp.where(lane == 5, vec[7:8], 0.0), axis=1, keepdims=True)
        R.stat[...] = jnp.sqrt(vec[7:8] / total)[:, :5]
        for come, go in ways:
            come.wait()
            go.start()
        for which, (held, dst) in enumerate(((R.grad_held, R.grad), (R.out_held, R.out))):
            pltpu.make_async_copy(held, dst, R.go_sems.at[which]).wait()
        for end in ends:
            end.wait()

    places = dict.fromkeys(("out_ref", "grad_ref", "done_ref", "mix_ref", "vec_ref", "out", "grad", "ew", "cw"), ANY)
    values = pl.pallas_call(
        kernel,
        out_shape=[jax.ShapeDtypeStruct(*spec) for spec in ends.values()],
        in_specs=[places.get(key, VMEM) for key in o],
        out_specs=[places.get(key, VMEM) for key in ends],
        scratch_shapes=[
            pltpu.VMEM(o["grad_ref"].shape, F32), pltpu.VMEM(o["out_ref"].shape, BF16), pltpu.VMEM(o["done_ref"].shape, BF16),
            pltpu.VMEM(o["mix_ref"].shape, F32), pltpu.VMEM(o["vec_ref"].shape, F32),
            pltpu.VMEM((deep, hidden), F32), pltpu.VMEM((tall, WIDTH), F32), pltpu.SemaphoreType.DMA((2, PIECES)),
            pltpu.SemaphoreType.DMA((2,)), pltpu.SemaphoreType.DMA((5,)),
        ],
        compiler_params=pltpu.CompilerParams(vmem_limit_bytes=ROOM),
        name="finishing",
    )(*o.values())
    e = dict(zip(ends, values))
    for key in ("out", "grad"):
        e[key] = e[key].reshape(shape)
    for key in ("fg", "fs", "ib", "ob", "gg", "gs", "eb", "cb", "stat"):
        e[key] = e[key].reshape(-1)
    return tuple(e.values())


def solution(mesh):
    ins, outs = specs()
    whole = body_by_collectives
    if mesh.shape["fsdp"] == FSDP and mesh.shape["rep"] in (2, 4):
        whole = functools.partial(body_in_one, mesh.shape["rep"])
    return jax.shard_map(whole, mesh=mesh, in_specs=ins, out_specs=outs, check_vma=False)
```
